32 devices in a mesh: groups: 2 (over x), ctx: 16 (over z, y, core).
Axes of the slice: x: 2, y: 2, z: 4, core: 2. Of those that a mesh axis runs over, the one named last changes fastest.
Arguments:
- tokens: bfloat16 [8192, 1024], P(('groups', 'ctx')), parts along dimension 0, may hold values from -4 to 4
- routes: int32 [8192, 2], P(('groups', 'ctx')), parts along dimension 0, may hold values from 0 to 31, all different within a row; in each aligned block of 256 rows (0 to 255, 256 to 511, ...) at most 20 rows name the same one
- gates: float32 [8192, 2], P(('groups', 'ctx')), parts along dimension 0, may hold values from 0.2 to 1
- qkv_weight: bfloat16 [1024, 3072], P('ctx'), may hold values from -2 to 2
- out_weight: bfloat16 [1024, 1024], P('ctx'), may hold values from -0.75 to 0.75
- w_in: bfloat16 [1024, 131072], P(None, 'ctx'), may hold values from -0.1875 to 0.1875
- w_out: bfloat16 [131072, 1024], P('ctx'), may hold values from -0.09375 to 0.09375
Outputs:
- layer_out: bfloat16 [8192, 1024], P(('groups', 'ctx')), parts along dimension 0
The draws below stay inside these ranges and needn't reach their ends.
There are 2 independent parts, one for each index of `groups`. The reference program is written for one: setup_inputs(seed, part) draws one part's arguments, and reference() takes and returns one part's arrays. A program takes and returns all parts, laid end to end along the dimension named above; an argument that names none is the same for every part. Nothing has to cross between parts.
Inputs may be any that keep to these rules, and one draw needn't show every extreme that they name: The 2 ids of a row differ; in each aligned block of 256 rows (the rows of one device) no expert is named by more than 20 routes, a bound that some block reaches.
All inputs are finite; a program needn't handle non-finite values.
Results may differ from the reference program's by a relative error of at most 0.004.
The reference program's roundings to bfloat16 on the way count: a program that leaves them out, or rounds other values in their place, can miss the bound.
Values may be sent and summed in bfloat16 or wider, within the bound.
No kernel may reach another device: no remote copies, remote signals or barrier semaphores. Data moves between devices by JAX's collectives and lax.ppermute only.
A program may use at most 128 MiB of HBM per device.

```python
import math
import jax
import jax.numpy as jnp
import numpy as np
from jax import lax

D = 1024
HEADS = 16
HD = 64
FF = 4096
EXPERTS = 32
TOP = 2
TOK_DEV = 256
SEQ = 1024
CAP = 20
TOKENS = 4096
N_CTX = 16


def draw_qkv_weight(key, part):
    key = jax.random.fold_in(key, 11)
    base = jnp.clip(jax.random.normal(key, (D, 3 * D), jnp.float32), -6.0, 6.0)
    sharp = 2.0
    column = jnp.arange(3 * D)
    scale = jnp.where(column < 2 * D, sharp, 1.0) * D ** (-0.5)
    return jnp.clip(base * scale[None, :], -2.0, 2.0).astype(jnp.bfloat16)


def shard_levels(key, shape, cuts, least, high):
    loudness, own = 1.0, jax.random.fold_in(key, 6)
    for axis_at, blocks in cuts:
        draws = jnp.exp(jax.random.uniform(jax.random.fold_in(own, axis_at), (blocks,), jnp.float32, least / len(cuts), high / len(cuts)))
        loudness = loudness * jnp.repeat(draws, shape[axis_at] // blocks).reshape([-1 if axis == axis_at else 1 for axis in range(len(shape))])
    return loudness


def routed_block(key, own, number, rows, count, top, limit, slope):
    order = jax.random.permutation(key, count)
    heavy_load, common = portions_of(count, rows * top, limit, slope, True), portions_of(count, rows * top, limit, slope, False)
    places = jnp.arange(count)

    def named(sizes, rotation):
        used = int((sizes > 0).sum())
        fixed = max(1, used // 4)
        shifted = fixed + (places - fixed + rotation * (used - fixed)) % max(1, count - fixed)
        return jnp.zeros((count,), jnp.int32).at[order[jnp.where(places < fixed, places, shifted)]].set(jnp.asarray(sizes, jnp.int32))

    sizes = jnp.where(number % 4 == 0, named(heavy_load, number // 4), named(common, number - number // 4 - 1))
    mixed = jax.random.permutation(jax.random.fold_in(own, 3), count)
    donor, receiver = mixed[0:count // 2 * 2:2], mixed[1:count // 2 * 2:2]
    slack = jnp.minimum(sizes[donor] - 1, limit - sizes[receiver]) // 2
    slack = jnp.where((donor == order[0]) | (receiver == order[0]) | (sizes[receiver] == 0), 0, jnp.maximum(slack, 0))
    shifted = jax.random.randint(jax.random.fold_in(own, 4), (count // 2,), 0, 1 << 20) % (slack + 1)
    sizes = sizes.at[donor].add(-shifted).at[receiver].add(shifted)
    members = jnp.searchsorted(jnp.cumsum(sizes), jnp.arange(rows * top), side="right").astype(jnp.int32)
    grid = members.reshape(top, rows).T
    grid = grid[jax.random.permutation(jax.random.fold_in(own, 1), rows)]
    rotation = jax.random.randint(jax.random.fold_in(own, 2), (rows, 1), 0, top)
    return jnp.take_along_axis(grid, (jnp.arange(top)[None, :] + rotation) % top, axis=1)


def portions_of(count, total, reach, lean, full):
    portions = [(1 << 20) // math.isqrt(standing ** lean) + 1 for standing in range(1, count + 1)]
    largest = reach if full else min(reach, max(-(-total // count), total * portions[0] // sum(portions)))
    least = 1 if total - largest >= count - 1 else 0
    counts, rest = [largest] + [least] * (count - 1), total - largest - least * (count - 1)
    while rest > 0:
        candidates = [i for i in range(1, count) if counts[i] < largest] or [i for i in range(1, count) if counts[i] < reach]
        pool, left = sum([portions[i] for i in candidates]), rest
        for i in candidates:
            addition = min(reach - counts[i], max(1, left * portions[i] // pool), rest)
            counts[i] = counts[i] + addition
            rest = rest - addition
    return np.array(counts)


def scatter_about(key, shape, deviation, most, cuts=(), kind=jnp.bfloat16):
    gain = shard_levels(key, shape, cuts, -0.22, 0.18) if cuts else 1.0
    result = jax.random.normal(key, shape, jnp.float32) * deviation * gain
    return jnp.minimum(jnp.maximum(result, -most), most).astype(kind)


def setup_inputs(seed: int = 0, part: int = 0) -> dict:
    arg_keys = jax.random.split(jax.random.key(seed), 8)
    part_keys = jax.random.split(jax.random.fold_in(arg_keys[7], part), 8)
    tokens = scatter_about(part_keys[0], (TOKENS, D), 0.5, 4.0, ((0, 16),))
    routes_keys = jax.random.split(jax.random.fold_in(part_keys[1], 1), TOKENS // TOK_DEV)
    routes_turns = jax.random.permutation(jax.random.fold_in(part_keys[1], 3), TOKENS // TOK_DEV)
    routes = jax.vmap(lambda own, number: routed_block(jax.random.fold_in(part_keys[1], 2), own, number, TOK_DEV, EXPERTS, TOP, CAP, 1))(routes_keys, routes_turns).reshape((TOKENS, TOP))
    gates = jnp.clip(0.2 + 0.8 * jax.random.uniform(part_keys[2], (TOKENS, TOP), jnp.float32) ** shard_levels(part_keys[2], (TOKENS, TOP), ((0, 16),), -0.2, 0.2), 0.2, 1.0)
    qkv_weight = draw_qkv_weight(jax.random.fold_in(arg_keys[7], 71), part)
    out_weight = scatter_about(arg_keys[4], (D, D), HD ** -0.5, 0.75, ((0, 16),))
    w_in = scatter_about(arg_keys[5], (D, EXPERTS * FF), D ** -0.5, 0.1875, ((1, 16),))
    w_out = scatter_about(arg_keys[6], (EXPERTS * FF, D), FF ** -0.5, 0.09375, ((0, 16),))
    return dict(tokens=tokens, routes=routes, gates=gates, qkv_weight=qkv_weight, out_weight=out_weight, w_in=w_in, w_out=w_out)


eps = 1e-06

def normalize(values):
    values = values.astype(jnp.float32)
    center = values - lax.optimization_barrier(jnp.mean(values, axis=-1, keepdims=True))
    spread = lax.optimization_barrier(jnp.mean(center * center, axis=-1, keepdims=True))
    return (center * lax.rsqrt(spread + eps)).astype(jnp.bfloat16)

def attend(block):
    width = block.shape[1] // 3
    length = block.shape[0]
    queries = block[:, :width].astype(jnp.float32).reshape(length, HEADS, HD)
    keys_all = block[:, width:2 * width].astype(jnp.float32).reshape(length, HEADS, HD)
    values_all = block[:, 2 * width:].astype(jnp.float32).reshape(length, HEADS, HD)
    scores = jnp.einsum('thd,shd->hts', queries, keys_all) * HD ** (-0.5)
    peak = lax.optimization_barrier(jnp.max(scores, axis=-1, keepdims=True))
    weights = jnp.exp(scores - peak)
    probs = (weights / lax.optimization_barrier(jnp.sum(weights, axis=-1, keepdims=True))).astype(jnp.bfloat16)
    mixed = jnp.einsum('hts,shd->thd', probs.astype(jnp.float32), values_all)
    return mixed.reshape(length, width).astype(jnp.bfloat16)

def reference(tokens, routes, gates, qkv_weight, out_weight, w_in, w_out):
    total, width = tokens.shape
    parts_ff = max(1, N_CTX // EXPERTS)
    hidden_units = FF // parts_ff
    normed = normalize(tokens)
    projected = jnp.dot(normed, qkv_weight, preferred_element_type=jnp.float32).astype(jnp.bfloat16)
    context = lax.map(attend, projected.reshape(total // SEQ, SEQ, 3 * width)).reshape(total, width)
    resid = tokens.astype(jnp.float32) + jnp.dot(context, out_weight, preferred_element_type=jnp.float32)
    moe_in = normalize(resid)
    flat_ids = routes.reshape(N_CTX, TOK_DEV * TOP)
    onehot = (flat_ids[:, :, None] == jnp.arange(EXPERTS, dtype=jnp.int32)[None, None, :]).astype(jnp.int32)
    before = jnp.cumsum(onehot, axis=1) - onehot
    position = lax.optimization_barrier(jnp.sum(before * onehot, axis=2))
    slot = (flat_ids * CAP + position).astype(jnp.int32)
    source = jnp.repeat(moe_in.reshape(N_CTX, TOK_DEV, width), TOP, axis=1)

    def fill(slots, rows):
        return jnp.zeros((EXPERTS * CAP, width), jnp.bfloat16).at[slots].set(rows)
    table = jax.vmap(fill)(slot, source).reshape(N_CTX, EXPERTS, CAP, width)

    def one_expert(expert):
        rows = lax.dynamic_index_in_dim(table, expert, 1, keepdims=False).reshape(N_CTX * CAP, width)
        summed = jnp.zeros((N_CTX * CAP, width), jnp.float32)
        for part in range(parts_ff):
            start = (expert * FF + part * hidden_units).astype(jnp.int32)
            first = lax.dynamic_slice_in_dim(w_in, start, hidden_units, 1)
            second = lax.dynamic_slice_in_dim(w_out, start, hidden_units, 0)
            hidden = jax.nn.gelu(jnp.dot(rows, first, preferred_element_type=jnp.float32)).astype(jnp.bfloat16)
            term = jnp.dot(hidden, second, preferred_element_type=jnp.float32).astype(jnp.bfloat16)
            term = lax.optimization_barrier(term)
            summed = summed + term.astype(jnp.float32)
        return summed.astype(jnp.bfloat16).reshape(N_CTX, CAP, width)
    expert_out = lax.map(one_expert, jnp.arange(EXPERTS, dtype=jnp.int32))
    per_source = jnp.transpose(expert_out, (1, 0, 2, 3)).reshape(N_CTX, EXPERTS * CAP, width)

    def pick(rows, slots):
        return rows[slots]
    picked = jax.vmap(pick)(per_source, slot).reshape(total, TOP, width)
    mixture = lax.optimization_barrier(jnp.sum(picked.astype(jnp.float32) * gates[:, :, None], axis=1))
    return (resid + mixture).astype(jnp.bfloat16)
```

```python
import functools

import jax
import jax.numpy as jnp
from jax import lax
from jax.experimental import pallas as pl
from jax.experimental.pallas import tpu as pltpu
from jax.sharding import PartitionSpec as P

HEADS = 16
HD = 64
EXPERTS = 32
SPAN = 4
CAP = 20
TOP = 2
MIB = 1 << 20

eps = 1e-06
bf16 = jnp.bfloat16
f32 = jnp.float32


def params(mib=40):
    return pltpu.CompilerParams(vmem_limit_bytes=mib * MIB)


def cost(flops, nbytes, trans=0):
    return pl.CostEstimate(flops=int(flops), bytes_accessed=int(nbytes), transcendentals=int(trans))


def mm(a, b, dims=(((1,), (0,)), ((), ()))):
    return lax.dot_general(a, b, dims, preferred_element_type=f32)


def normalize(values):
    center = values - jnp.mean(values, axis=-1, keepdims=True)
    spread = jnp.mean(center * center, axis=-1, keepdims=True)
    return (center * lax.rsqrt(spread + eps)).astype(bf16)


def norm_kernel(x_ref, o_ref):
    o_ref[...] = normalize(x_ref[...].astype(f32))


def norm_call(tokens):
    return pl.pallas_call(
        norm_kernel,
        out_shape=jax.ShapeDtypeStruct(tokens.shape, bf16),
        compiler_params=params(),
        cost_estimate=cost(8 * tokens.size, 4 * tokens.size),
        name="norm_tokens",
    )(tokens)


def route_kernel(routes_ref, gates_ref, d_ref, hi_ref, mid_ref, lo_ref):
    rows = routes_ref.shape[1]
    slots = d_ref.shape[0]
    expert = lax.broadcasted_iota(jnp.int32, (EXPERTS, rows), 0)
    names = [expert == routes_ref[r : r + 1, :] for r in range(TOP)]
    counts = names[0]
    for other in names[1:]:
        counts = counts | other
    counts = jnp.where(counts, 1.0, 0.0).astype(bf16)
    earlier = lax.broadcasted_iota(jnp.int32, (rows, rows), 0) < lax.broadcasted_iota(
        jnp.int32, (rows, rows), 1
    )
    before = mm(counts, jnp.where(earlier, 1.0, 0.0).astype(bf16))
    place = lax.broadcasted_iota(jnp.int32, (slots, rows), 0)
    marks = jnp.zeros((slots, rows), f32)
    weights = jnp.zeros((slots, rows), f32)
    for r in range(TOP):
        position = jnp.sum(jnp.where(names[r], before, 0.0), axis=0, keepdims=True)
        slot = routes_ref[r : r + 1, :] * CAP + position.astype(jnp.int32)
        here = place == slot
        marks = jnp.where(here, 1.0, marks)
        weights = jnp.where(here, gates_ref[r : r + 1, :], weights)
    d_ref[...] = marks.astype(bf16)
    high = weights.astype(bf16)
    rest = weights - high.astype(f32)
    middle = rest.astype(bf16)
    hi_ref[...] = high
    mid_ref[...] = middle
    lo_ref[...] = (rest - middle.astype(f32)).astype(bf16)


def route_call(routes, gates):
    rows = routes.shape[0]
    shape = jax.ShapeDtypeStruct((EXPERTS * CAP, rows), bf16)
    return pl.pallas_call(
        route_kernel,
        out_shape=[shape] * 4,
        compiler_params=params(),
        cost_estimate=cost(20 * EXPERTS * CAP * rows, 8 * EXPERTS * CAP * rows),
        name="route_slots",
    )(routes.T, gates.T)


def project_kernel(place_ref, *refs, count, blocks, share):
    xs = refs[:count]
    ws = refs[count : count + blocks * share]
    o_ref = refs[count + blocks * share]
    full = refs[count + blocks * share + 1]
    size = ws[0].shape[0]
    rows = xs[0].shape[0]
    for s in range(share):
        for m in range(blocks):
            start = pl.multiple_of((place_ref[0] ^ m) * size, size)
            full[s, pl.ds(start, size), :] = ws[s * blocks + m][...]
    for s in range(share):
        for j in range(count):
            o_ref[s, j * rows : (j + 1) * rows, :] = mm(xs[j][...], full[s]).astype(bf16)


def project_call(place, xs, ws, blocks, share):
    rows, width = xs[0].shape
    count = len(xs)
    cols = ws[0].shape[1]
    vm = pl.BlockSpec(memory_space=pltpu.VMEM)
    return pl.pallas_call(
        functools.partial(project_kernel, count=count, blocks=blocks, share=share),
        out_shape=jax.ShapeDtypeStruct((share, count * rows, cols), bf16),
        in_specs=[pl.BlockSpec(memory_space=pltpu.SMEM)] + [vm] * (count + blocks * share),
        out_specs=vm,
        scratch_shapes=[pltpu.VMEM((share, width, cols), bf16)],
        compiler_params=params(),
        cost_estimate=cost(2 * count * rows * width * cols * share, 2 * width * (count * rows + 2 * cols * share)),
        name="project",
    )(place, *xs, *ws)


def attend_kernel(p_ref, *o_refs, blocks, share):
    cols = p_ref.shape[2] // 3
    rows = o_refs[0].shape[0]
    heads = cols // HD
    lane = lax.broadcasted_iota(jnp.int32, (rows, cols), 1) // HD
    for o_ref, j in zip(o_refs, blocks):
        for s in range(share):
            queries = p_ref[s, j * rows : (j + 1) * rows, :cols] * jnp.asarray(HD ** (-0.5), bf16)
            keys = p_ref[s, :, cols : 2 * cols]
            values = p_ref[s, :, 2 * cols :]
            mixed = None
            for h in range(heads):
                mine = lane == h
                q = jnp.where(mine, queries, jnp.zeros_like(queries)) if heads > 1 else queries
                scores = mm(q, keys, (((1,), (1,)), ((), ())))
                weights = jnp.exp(scores - jnp.max(scores, axis=-1, keepdims=True))
                probs = (weights * (1.0 / jnp.sum(weights, axis=-1, keepdims=True))).astype(bf16)
                part = mm(probs, values)
                mixed = part if mixed is None else jnp.where(mine, part, mixed)
            o_ref[:, s * cols : (s + 1) * cols] = mixed.astype(bf16)


def attend_call(projected, blocks, rows):
    share, length, cols = projected.shape
    width = share * cols // 3
    return pl.pallas_call(
        functools.partial(attend_kernel, blocks=blocks, share=share),
        out_shape=[jax.ShapeDtypeStruct((rows, width), bf16)] * len(blocks),
        compiler_params=params(),
        cost_estimate=cost(
            16 * len(blocks) * rows * length * width, 4 * projected.size, len(blocks) * rows * length * width // HD
        ),
        name="attend",
    )(projected)


def output_kernel(place_ref, t_ref, d_ref, w_ref, *refs):
    ctxs = refs[:SPAN]
    r_ref, o_ref = refs[SPAN:]
    width = ctxs[0].shape[1]
    total = t_ref[...].astype(f32)
    attended = None
    for j in range(SPAN):
        start = pl.multiple_of((place_ref[0] ^ j) * width, width)
        part = mm(ctxs[j][...], w_ref[pl.ds(start, width), :])
        attended = part if attended is None else attended + part
    total = total + attended
    r_ref[...] = total
    o_ref[...] = mm(d_ref[...], normalize(total)).astype(bf16)


def output_call(place, tokens, marks, weight, ctxs):
    rows, width = tokens.shape
    vm = pl.BlockSpec(memory_space=pltpu.VMEM)
    return pl.pallas_call(
        output_kernel,
        out_shape=[
            jax.ShapeDtypeStruct((rows, width), f32),
            jax.ShapeDtypeStruct((marks.shape[0], width), bf16),
        ],
        in_specs=[pl.BlockSpec(memory_space=pltpu.SMEM)] + [vm] * (3 + SPAN),
        out_specs=[vm, vm],
        compiler_params=params(),
        cost_estimate=cost(2 * rows * width * (width + marks.shape[0]), 6 * width * width),
        name="out_projection",
    )(place, tokens, marks, weight, *ctxs)


def gelu(x):
    return jax.nn.gelu(x, approximate=True)


def expert_kernel(x_ref, win_ref, wout_ref, o_ref, rows_ref, acc_ref, term_ref, *, local, sources):
    e = pl.program_id(0)
    step = pl.program_id(1)
    last = pl.num_programs(1) - 1
    count = sources * CAP

    def pick(which):
        out_row = lax.broadcasted_iota(jnp.int32, (count, local * count), 0)
        in_row = lax.broadcasted_iota(jnp.int32, (count, local * count), 1)
        source = out_row // CAP
        wanted = source * (local * CAP) + which * CAP + (out_row - source * CAP)
        return jnp.where(in_row == wanted, 1.0, 0.0).astype(bf16)

    if local > 1:

        @pl.when(step == 0)
        def _():
            rows_ref[...] = mm(pick(e), x_ref[...]).astype(bf16)

        rows = rows_ref
    else:
        rows = x_ref

    @pl.when(step == 0)
    def _():
        acc_ref[...] = jnp.zeros_like(acc_ref)

    hidden = gelu(mm(rows[...], win_ref[...])).astype(bf16)
    acc_ref[...] += mm(hidden, wout_ref[...])

    @pl.when(step == last)
    def _():
        if local > 1:
            term_ref[e] = acc_ref[...].astype(bf16)
        else:
            o_ref[...] = acc_ref[...].astype(bf16)

    if local > 1:

        @pl.when((step == last) & (e == local - 1))
        def _():
            total = None
            for which in range(local):
                part = mm(pick(which), term_ref[which], (((0,), (0,)), ((), ())))
                total = part if total is None else total + part
            o_ref[...] = total.astype(bf16)


def expert_call(arrived, w_in, w_out, local, sources, block=512):
    count = sources * CAP
    width = arrived.shape[1]
    hidden = w_in.shape[1] // local
    steps = hidden // block
    return pl.pallas_call(
        functools.partial(expert_kernel, local=local, sources=sources),
        grid=(local, steps),
        out_shape=jax.ShapeDtypeStruct(arrived.shape, bf16),
        in_specs=[
            pl.BlockSpec(arrived.shape, lambda e, i: (0, 0)),
            pl.BlockSpec((width, block), lambda e, i: (0, e * steps + i)),
            pl.BlockSpec((block, width), lambda e, i: (e * steps + i, 0)),
        ],
        out_specs=pl.BlockSpec(arrived.shape, lambda e, i: (0, 0)),
        scratch_shapes=[
            pltpu.VMEM((count, width), bf16),
            pltpu.VMEM((count, width), f32),
            pltpu.VMEM((local, count, width), bf16),
        ],
        compiler_params=params(),
        cost_estimate=cost(4 * count * width * hidden * local, 4 * width * hidden * local, count * hidden * local),
        name="experts",
    )(arrived, w_in, w_out)


def combine_kernel(r_ref, b_ref, hi_ref, mid_ref, lo_ref, o_ref):
    dims = (((0,), (0,)), ((), ()))
    back = b_ref[...]
    mixture = mm(lo_ref[...], back, dims)
    mixture = mixture + mm(mid_ref[...], back, dims)
    mixture = mixture + mm(hi_ref[...], back, dims)
    o_ref[...] = (r_ref[...] + mixture).astype(bf16)


def combine_call(resid, back, parts):
    return pl.pallas_call(
        combine_kernel,
        out_shape=jax.ShapeDtypeStruct(resid.shape, bf16),
        compiler_params=params(),
        cost_estimate=cost(6 * back.size * resid.shape[0], 6 * resid.size + 2 * back.size),
        name="combine",
    )(resid, back, *parts)


def swap(value, axis, bits):
    size = lax.axis_size(axis)
    return lax.ppermute(value, axis, [(i, i ^ bits) for i in range(size)])


def per_device(tokens, routes, gates, qkv_weight, out_weight, w_in, w_out):
    rows, width = tokens.shape
    devices = lax.axis_size("ctx")
    groups = lax.axis_size("groups")
    upper = devices // SPAN
    me = lax.axis_index("ctx")
    member = me % SPAN
    line = me // SPAN
    group = lax.axis_index("groups")
    parts_ff = max(1, devices // EXPERTS)
    local_experts = max(1, EXPERTS // devices)

    mine = width // SPAN
    share = SHARE(groups, mine // HD)
    cols = mine // share
    offset = (group % share) * cols

    def columns(to):
        pieces = [
            lax.dynamic_slice_in_dim(qkv_weight, t * width + to * mine + offset, cols, 1)
            for t in range(3)
        ]
        return jnp.concatenate(pieces, axis=1)

    pieces = [columns(member)] + [swap(columns(member ^ j), "ctx", j) for j in range(1, SPAN)]
    block = jnp.zeros((SPAN,) + pieces[0].shape, bf16)
    for j in range(SPAN):
        block = lax.dynamic_update_slice(block, pieces[j][None], (member ^ j, 0, 0))
    block = block.reshape(-1, 3 * cols)
    lines = [block] + [swap(block, "ctx", m * SPAN) for m in range(1, upper)]
    shares = lines
    for s in range(1, share):
        shares = shares + [swap(piece, "groups", s) for piece in lines]

    normed = norm_call(tokens)
    far = swap(normed, "ctx", 2)
    near = swap(normed, "ctx", 1)
    both = swap(far, "ctx", 1)
    marks, *gate_parts = route_call(routes, gates)

    projected = project_call(line.reshape(1), [normed, near, far, both], shares, upper, share)
    sent = attend_call(projected, (3, 2), rows)
    back = {3: swap(sent[0], "ctx", 3), 2: swap(sent[1], "ctx", 2)}
    kept = attend_call(projected, (1, 0), rows)
    back[1] = swap(kept[0], "ctx", 1)
    back[0] = kept[1]
    ctxs = []
    for j in range(SPAN):
        if share > 1:
            split = back[j].reshape(rows, share, cols)
            order = [lax.dynamic_index_in_dim(split, (group % share) ^ s, 1, keepdims=False) for s in range(share)]
            ctxs.append(jnp.concatenate(order, axis=1))
        else:
            ctxs.append(back[j])
    whole_out = lax.all_gather(out_weight, "ctx", axis=0, tiled=True)
    resid, table = output_call(member.reshape(1), tokens, marks, whole_out, ctxs)

    table = table.reshape(EXPERTS, CAP, width)
    if parts_ff > 1:
        table = jnp.repeat(table, parts_ff, axis=0)
    outgoing = table.reshape(devices, local_experts * CAP, width)
    arrived = lax.all_to_all(outgoing, "ctx", split_axis=0, concat_axis=0, tiled=True)
    produced = expert_call(arrived.reshape(-1, width), w_in, w_out, local_experts, devices)
    produced = produced.reshape(devices, local_experts * CAP, width)
    returned = lax.all_to_all(produced, "ctx", split_axis=0, concat_axis=0, tiled=True)
    if parts_ff > 1:
        grouped = returned.reshape(EXPERTS, parts_ff, CAP, width)
        returned = jnp.sum(grouped.astype(f32), axis=1).astype(bf16)
    return combine_call(resid, returned.reshape(EXPERTS * CAP, width), gate_parts)


def SHARE(groups, heads):
    return 1


def solution(mesh):
    in_specs = (
        P(("groups", "ctx"), None),
        P(("groups", "ctx"), None),
        P(("groups", "ctx"), None),
        P("ctx", None),
        P("ctx", None),
        P(None, "ctx"),
        P("ctx", None),
    )
    out_specs = P(("groups", "ctx"), None)
    return jax.shard_map(
        per_device, mesh=mesh, in_specs=in_specs, out_specs=out_specs, check_vma=False
    )
```

```python
import functools

import jax
import jax.numpy as jnp
from jax import lax
from jax.experimental import pallas as pl
from jax.experimental.pallas import tpu as pltpu
from jax.sharding import PartitionSpec as P

HEADS = 16
HD = 64
EXPERTS = 32
SPAN = 4
CAP = 20
TOP = 2
MIB = 1 << 20

eps = 1e-06
bf16 = jnp.bfloat16
f32 = jnp.float32


def params(mib=40):
    return pltpu.CompilerParams(vmem_limit_bytes=mib * MIB)


def cost(flops, nbytes, trans=0):
    return pl.CostEstimate(flops=int(flops), bytes_accessed=int(nbytes), transcendentals=int(trans))


def mm(a, b, dims=(((1,), (0,)), ((), ()))):
    return lax.dot_general(a, b, dims, preferred_element_type=f32)


def normalize(values):
    center = values - jnp.mean(values, axis=-1, keepdims=True)
    spread = jnp.mean(center * center, axis=-1, keepdims=True)
    return (center * lax.rsqrt(spread + eps)).astype(bf16)


def norm_kernel(x_ref, o_ref):
    o_ref[...] = normalize(x_ref[...].astype(f32))


def norm_call(tokens):
    return pl.pallas_call(
        norm_kernel,
        out_shape=jax.ShapeDtypeStruct(tokens.shape, bf16),
        compiler_params=params(),
        cost_estimate=cost(8 * tokens.size, 4 * tokens.size),
        name="norm_tokens",
    )(tokens)


def route_kernel(routes_ref, gates_ref, d_ref, hi_ref, mid_ref, lo_ref):
    rows = routes_ref.shape[1]
    slots = d_ref.shape[0]
    expert = lax.broadcasted_iota(jnp.int32, (EXPERTS, rows), 0)
    names = [expert == routes_ref[r : r + 1, :] for r in range(TOP)]
    counts = names[0]
    for other in names[1:]:
        counts = counts | other
    counts = jnp.where(counts, 1.0, 0.0).astype(bf16)
    earlier = lax.broadcasted_iota(jnp.int32, (rows, rows), 0) < lax.broadcasted_iota(
        jnp.int32, (rows, rows), 1
    )
    before = mm(counts, jnp.where(earlier, 1.0, 0.0).astype(bf16))
    place = lax.broadcasted_iota(jnp.int32, (slots, rows), 0)
    marks = jnp.zeros((slots, rows), f32)
    weights = jnp.zeros((slots, rows), f32)
    for r in range(TOP):
        position = jnp.sum(jnp.where(names[r], before, 0.0), axis=0, keepdims=True)
        slot = routes_ref[r : r + 1, :] * CAP + position.astype(jnp.int32)
        here = place == slot
        marks = jnp.where(here, 1.0, marks)
        weights = jnp.where(here, gates_ref[r : r + 1, :], weights)
    d_ref[...] = marks.astype(bf16)
    high = weights.astype(bf16)
    rest = weights - high.astype(f32)
    middle = rest.astype(bf16)
    hi_ref[...] = high
    mid_ref[...] = middle
    lo_ref[...] = (rest - middle.astype(f32)).astype(bf16)


def route_call(routes, gates):
    rows = routes.shape[0]
    shape = jax.ShapeDtypeStruct((EXPERTS * CAP, rows), bf16)
    return pl.pallas_call(
        route_kernel,
        out_shape=[shape] * 4,
        compiler_params=params(),
        cost_estimate=cost(20 * EXPERTS * CAP * rows, 8 * EXPERTS * CAP * rows),
        name="route_slots",
    )(routes.T, gates.T)


def project_kernel(place_ref, *refs, count, lines, share):
    xs = refs[:count]
    ws = refs[count : count + lines * share]
    o_ref, part_ref, full = refs[count + lines * share :]
    size, wide = ws[0].shape
    cols = wide // 4
    rows = xs[0].shape[0]
    for s in range(share):
        for m in range(lines):
            start = pl.multiple_of((place_ref[0] ^ m) * size, size)
            full[place_ref[1] ^ s, pl.ds(start, size), :] = ws[s * lines + m][...]
    for s in range(share):
        for j in range(count):
            o_ref[s, j * rows : (j + 1) * rows, :] = mm(xs[j][...], full[s, :, : 3 * cols]).astype(bf16)
        part_ref[:, s * cols : (s + 1) * cols] = full[s, :, 3 * cols :]


def project_call(place, xs, ws, lines, share):
    rows, width = xs[0].shape
    count = len(xs)
    wide = ws[0].shape[1]
    cols = wide // 4
    vm = pl.BlockSpec(memory_space=pltpu.VMEM)
    return pl.pallas_call(
        functools.partial(project_kernel, count=count, lines=lines, share=share),
        out_shape=[
            jax.ShapeDtypeStruct((share, count * rows, 3 * cols), bf16),
            jax.ShapeDtypeStruct((width, share * cols), bf16),
        ],
        in_specs=[pl.BlockSpec(memory_space=pltpu.SMEM)] + [vm] * (count + lines * share),
        out_specs=[vm, vm],
        scratch_shapes=[pltpu.VMEM((share, width, wide), bf16)],
        compiler_params=params(),
        cost_estimate=cost(6 * count * rows * width * cols * share, 2 * width * (count * rows + 2 * wide * share)),
        name="project",
    )(place, *xs, *ws)


def attend_kernel(p_ref, *o_refs, blocks, share):
    cols = p_ref.shape[2] // 3
    rows = o_refs[0].shape[0]
    heads = cols // HD
    lane = lax.broadcasted_iota(jnp.int32, (rows, cols), 1) // HD
    for o_ref, j in zip(o_refs, blocks):
        for s in range(share):
            queries = p_ref[s, j * rows : (j + 1) * rows, :cols] * jnp.asarray(HD ** (-0.5), bf16)
            keys = p_ref[s, :, cols : 2 * cols]
            values = p_ref[s, :, 2 * cols :]
            mixed = None
            for h in range(heads):
                mine = lane == h
                q = jnp.where(mine, queries, jnp.zeros_like(queries)) if heads > 1 else queries
                scores = mm(q, keys, (((1,), (1,)), ((), ())))
                weights = jnp.exp(scores - jnp.max(scores, axis=-1, keepdims=True))
                probs = (weights * (1.0 / jnp.sum(weights, axis=-1, keepdims=True))).astype(bf16)
                part = mm(probs, values)
                mixed = part if mixed is None else jnp.where(mine, part, mixed)
            o_ref[:, s * cols : (s + 1) * cols] = mixed.astype(bf16)


def attend_call(projected, blocks, rows):
    share, length, cols = projected.shape
    width = share * cols // 3
    return pl.pallas_call(
        functools.partial(attend_kernel, blocks=blocks, share=share),
        out_shape=[jax.ShapeDtypeStruct((rows, width), bf16)] * len(blocks),
        compiler_params=params(),
        cost_estimate=cost(
            16 * len(blocks) * rows * length * width, 4 * projected.size, len(blocks) * rows * length * width // HD
        ),
        name="attend",
    )(projected)


def output_kernel(place_ref, t_ref, d_ref, *refs):
    ctxs, parts = refs[:SPAN], refs[SPAN : 2 * SPAN]
    r_ref, o_ref, c_ref, a_ref = refs[2 * SPAN :]
    wide = ctxs[0].shape[1]
    starts = [pl.multiple_of((place_ref[0] ^ j) * wide, wide) for j in range(SPAN)]
    for j in range(SPAN):
        c_ref[:, pl.ds(starts[j], wide)] = ctxs[j][...]
    for j in range(SPAN):
        a_ref[:, pl.ds(starts[j], wide)] = mm(c_ref[...], parts[j][...])
    total = t_ref[...].astype(f32) + a_ref[...]
    r_ref[...] = total
    o_ref[...] = mm(d_ref[...], normalize(total)).astype(bf16)


def output_call(place, tokens, marks, parts, ctxs):
    rows, width = tokens.shape
    vm = pl.BlockSpec(memory_space=pltpu.VMEM)
    return pl.pallas_call(
        output_kernel,
        out_shape=[
            jax.ShapeDtypeStruct((rows, width), f32),
            jax.ShapeDtypeStruct((marks.shape[0], width), bf16),
        ],
        in_specs=[pl.BlockSpec(memory_space=pltpu.SMEM)] + [vm] * (2 + 2 * SPAN),
        out_specs=[vm, vm],
        scratch_shapes=[pltpu.VMEM((rows, width), bf16), pltpu.VMEM((rows, width), f32)],
        compiler_params=params(),
        cost_estimate=cost(2 * rows * width * (width + marks.shape[0]), 6 * width * width),
        name="out_projection",
    )(place, tokens, marks, *ctxs, *parts)


def gelu(x):
    return jax.nn.gelu(x, approximate=True)


def expert_kernel(x_ref, win_ref, wout_ref, o_ref, *scratch, local, sources, step, ahead):
    rows_ref, hid_ref, pre_ref, acc_ref, term_ref, in_buf, out_buf, in_sem, out_sem = scratch
    count = sources * CAP
    width = x_ref.shape[1]
    hidden = win_ref.shape[1] // local
    steps = hidden // step
    pack = 4 * CAP

    def load_in(e, n):
        return pltpu.make_async_copy(
            win_ref.at[:, pl.ds(e * hidden + n * step, step)], in_buf.at[n], in_sem.at[n]
        )

    def load_out(e, n):
        return pltpu.make_async_copy(
            wout_ref.at[pl.ds(e * hidden + n * step, step), :],
            out_buf.at[pl.ds(n * step, step), :],
            out_sem.at[n],
        )

    chain = [load(e, n) for e in range(local) for load in (load_in, load_out) for n in range(steps)]

    def arrive(t):
        chain[t].wait()
        if t + ahead < len(chain):
            chain[t + ahead].start()

    for load in chain[:ahead]:
        load.start()

    if local > 1:
        to = lax.broadcasted_iota(jnp.int32, (local * pack, local * pack), 0)
        have = lax.broadcasted_iota(jnp.int32, (local * pack, local * pack), 1)
        expert = to // pack
        inner = to - expert * pack
        source = inner // CAP
        wanted = source * (local * CAP) + expert * CAP + (inner - source * CAP)
        order = jnp.where(have == wanted, 1.0, 0.0).astype(bf16)
        for g in range(count // pack):
            part = mm(order, x_ref[g * local * pack : (g + 1) * local * pack, :]).astype(bf16)
            for e in range(local):
                rows_ref[e, g * pack : (g + 1) * pack, :] = part[e * pack : (e + 1) * pack, :]

    for e in range(local):
        for n in range(steps):
            arrive(2 * e * steps + n)
            rows = rows_ref[e] if local > 1 else x_ref[...]
            pre_ref[n % 2] = mm(rows, in_buf[n])
            if n:
                hid_ref[:, (n - 1) * step : n * step] = gelu(pre_ref[(n - 1) % 2]).astype(bf16)
        hid_ref[:, (steps - 1) * step :] = gelu(pre_ref[(steps - 1) % 2]).astype(bf16)
        for n in range(steps):
            arrive((2 * e + 1) * steps + n)
            part = mm(hid_ref[:, n * step : (n + 1) * step], out_buf[n * step : (n + 1) * step, :])
            if n:
                part = acc_ref[...] + part
            if n + 1 < steps:
                acc_ref[...] = part
            elif local > 1:
                term_ref[e] = part.astype(bf16)
            else:
                o_ref[...] = part.astype(bf16)

    if local > 1:
        for g in range(count // pack):
            part = jnp.concatenate([term_ref[e, g * pack : (g + 1) * pack, :] for e in range(local)], axis=0)
            back = mm(order, part, (((0,), (0,)), ((), ())))
            o_ref[g * local * pack : (g + 1) * local * pack, :] = back.astype(bf16)


def expert_call(arrived, w_in, w_out, local, sources, step=2048, ahead=2):
    count = sources * CAP
    width = arrived.shape[1]
    hidden = w_in.shape[1] // local
    steps = hidden // step
    kept = (local, count, width) if local > 1 else (1, 16, 128)
    vm = pl.BlockSpec(memory_space=pltpu.VMEM)
    hbm = pl.BlockSpec(memory_space=pl.ANY)
    return pl.pallas_call(
        functools.partial(expert_kernel, local=local, sources=sources, step=step, ahead=ahead),
        out_shape=jax.ShapeDtypeStruct(arrived.shape, bf16),
        in_specs=[vm, hbm, hbm],
        out_specs=vm,
        scratch_shapes=[
            pltpu.VMEM(kept, bf16),
            pltpu.VMEM((count, hidden), bf16),
            pltpu.VMEM((2, count, step), f32),
            pltpu.VMEM((count, width), f32),
            pltpu.VMEM(kept, bf16),
            pltpu.VMEM((steps, width, step), bf16),
            pltpu.VMEM((hidden, width), bf16),
            pltpu.SemaphoreType.DMA((steps,)),
            pltpu.SemaphoreType.DMA((steps,)),
        ],
        compiler_params=params(52),
        cost_estimate=cost(4 * count * width * hidden * local, 4 * width * hidden * local, count * hidden * local),
        name="experts",
    )(arrived, w_in, w_out)


def combine_kernel(r_ref, b_ref, hi_ref, mid_ref, lo_ref, o_ref):
    dims = (((0,), (0,)), ((), ()))
    back = b_ref[...]
    mixture = mm(lo_ref[...], back, dims)
    mixture = mixture + mm(mid_ref[...], back, dims)
    mixture = mixture + mm(hi_ref[...], back, dims)
    o_ref[...] = (r_ref[...] + mixture).astype(bf16)


def combine_call(resid, back, parts):
    return pl.pallas_call(
        combine_kernel,
        out_shape=jax.ShapeDtypeStruct(resid.shape, bf16),
        compiler_params=params(),
        cost_estimate=cost(6 * back.size * resid.shape[0], 6 * resid.size + 2 * back.size),
        name="combine",
    )(resid, back, *parts)


def swap(value, axis, bits):
    size = lax.axis_size(axis)
    return lax.ppermute(value, axis, [(i, i ^ bits) for i in range(size)])


def per_device(tokens, routes, gates, qkv_weight, out_weight, w_in, w_out):
    rows, width = tokens.shape
    devices = lax.axis_size("ctx")
    groups = lax.axis_size("groups")
    lines_total = devices // SPAN
    me = lax.axis_index("ctx")
    member = me % SPAN
    line = me // SPAN
    group = lax.axis_index("groups")
    parts_ff = max(1, devices // EXPERTS)
    local_experts = max(1, EXPERTS // devices)

    mine = width // SPAN
    share = groups if (mine // HD) % groups == 0 else 1
    cols = mine // share
    offset = (group % share) * cols

    def columns(to):
        pieces = [
            lax.dynamic_slice_in_dim(qkv_weight, t * width + to * mine + offset, cols, 1)
            for t in range(3)
        ]
        pieces.append(lax.dynamic_slice_in_dim(out_weight, to * mine + offset, cols, 1))
        return jnp.concatenate(pieces, axis=1)

    pieces = [columns(member)] + [swap(columns(member ^ j), "ctx", j) for j in range(1, SPAN)]
    block = jnp.zeros((SPAN,) + pieces[0].shape, bf16)
    for j in range(SPAN):
        block = lax.dynamic_update_slice(block, pieces[j][None], (member ^ j, 0, 0))
    block = block.reshape(-1, 4 * cols)
    normed, block = lax.optimization_barrier((norm_call(tokens), block))
    lines = {0: block}
    bit = lines_total // 2
    while bit:
        for known in list(lines):
            lines[known | bit] = swap(lines[known], "ctx", bit * SPAN)
        bit //= 2
    shares = []
    for s in range(share):
        shares += [lines[m] if s == 0 else swap(lines[m], "groups", s) for m in range(lines_total)]

    far = swap(normed, "ctx", 2)
    near = swap(normed, "ctx", 1)
    both = swap(far, "ctx", 1)
    marks, *gate_parts = route_call(routes, gates)

    place = jnp.stack([line, group % share])
    projected, part = project_call(place, [normed, near, far, both], shares, lines_total, share)
    part_far = swap(part, "ctx", 2)
    part_near = swap(part, "ctx", 1)
    part_both = swap(part_far, "ctx", 1)
    sent = attend_call(projected, (3, 2), rows)
    back = {3: swap(sent[0], "ctx", 3), 2: swap(sent[1], "ctx", 2)}
    kept = attend_call(projected, (1, 0), rows)
    back[1] = swap(kept[0], "ctx", 1)
    back[0] = kept[1]
    ctxs = [back[j] for j in range(SPAN)]
    resid, table = output_call(
        member.reshape(1), tokens, marks, [part, part_near, part_far, part_both], ctxs
    )

    table = table.reshape(EXPERTS, CAP, width)
    if parts_ff > 1:
        table = jnp.repeat(table, parts_ff, axis=0)
    outgoing = table.reshape(devices, local_experts * CAP, width)
    arrived = lax.all_to_all(outgoing, "ctx", split_axis=0, concat_axis=0, tiled=True)
    produced = expert_call(arrived.reshape(-1, width), w_in, w_out, local_experts, devices)
    produced = produced.reshape(devices, local_experts * CAP, width)
    returned = lax.all_to_all(produced, "ctx", split_axis=0, concat_axis=0, tiled=True)
    if parts_ff > 1:
        grouped = returned.reshape(EXPERTS, parts_ff, CAP, width)
        returned = jnp.sum(grouped.astype(f32), axis=1).astype(bf16)
    return combine_call(resid, returned.reshape(EXPERTS * CAP, width), gate_parts)


def solution(mesh):
    in_specs = (
        P(("groups", "ctx"), None),
        P(("groups", "ctx"), None),
        P(("groups", "ctx"), None),
        P("ctx", None),
        P("ctx", None),
        P(None, "ctx"),
        P("ctx", None),
    )
    out_specs = P(("groups", "ctx"), None)
    return jax.shard_map(
        per_device, mesh=mesh, in_specs=in_specs, out_specs=out_specs, check_vma=False
    )
```

```python
import functools
import math

import jax
import jax.numpy as jnp
from jax import lax
from jax.experimental import pallas as pl
from jax.experimental.pallas import tpu as pltpu
from jax.sharding import PartitionSpec as P

HEADS = 16
HD = 64
EXPERTS = 32
SPAN = 4
CAP = 20
TOP = 2
MIB = 1 << 20

eps = 1e-06
bf16 = jnp.bfloat16
f32 = jnp.float32


def params(mib=40):
    return pltpu.CompilerParams(vmem_limit_bytes=mib * MIB)


def cost(flops, nbytes, trans=0):
    return pl.CostEstimate(flops=int(flops), bytes_accessed=int(nbytes), transcendentals=int(trans))


def mm(a, b, dims=(((1,), (0,)), ((), ()))):
    return lax.dot_general(a, b, dims, preferred_element_type=f32)


def normalize(values):
    center = values - jnp.mean(values, axis=-1, keepdims=True)
    spread = jnp.mean(center * center, axis=-1, keepdims=True)
    return (center * lax.rsqrt(spread + eps)).astype(bf16)


def norm_kernel(x_ref, o_ref):
    o_ref[...] = normalize(x_ref[...].astype(f32))


def norm_call(tokens):
    return pl.pallas_call(
        norm_kernel,
        out_shape=jax.ShapeDtypeStruct(tokens.shape, bf16),
        compiler_params=params(),
        cost_estimate=cost(8 * tokens.size, 4 * tokens.size),
        name="norm_tokens",
    )(tokens)


def route_kernel(routes_ref, gates_ref, d_ref, hi_ref, mid_ref, lo_ref):
    rows = routes_ref.shape[1]
    slots = d_ref.shape[0]
    expert = lax.broadcasted_iota(jnp.int32, (EXPERTS, rows), 0)
    names = [expert == routes_ref[r : r + 1, :] for r in range(TOP)]
    counts = names[0]
    for other in names[1:]:
        counts = counts | other
    counts = jnp.where(counts, 1.0, 0.0).astype(bf16)
    earlier = lax.broadcasted_iota(jnp.int32, (rows, rows), 0) < lax.broadcasted_iota(
        jnp.int32, (rows, rows), 1
    )
    before = mm(counts, jnp.where(earlier, 1.0, 0.0).astype(bf16))
    place = lax.broadcasted_iota(jnp.int32, (slots, rows), 0)
    marks = jnp.zeros((slots, rows), f32)
    weights = jnp.zeros((slots, rows), f32)
    for r in range(TOP):
        position = jnp.sum(jnp.where(names[r], before, 0.0), axis=0, keepdims=True)
        slot = routes_ref[r : r + 1, :] * CAP + position.astype(jnp.int32)
        here = place == slot
        marks = jnp.where(here, 1.0, marks)
        weights = jnp.where(here, gates_ref[r : r + 1, :], weights)
    d_ref[...] = marks.astype(bf16)
    high = weights.astype(bf16)
    rest = weights - high.astype(f32)
    middle = rest.astype(bf16)
    hi_ref[...] = high
    mid_ref[...] = middle
    lo_ref[...] = (rest - middle.astype(f32)).astype(bf16)


def route_call(routes, gates):
    rows = routes.shape[0]
    shape = jax.ShapeDtypeStruct((EXPERTS * CAP, rows), bf16)
    return pl.pallas_call(
        route_kernel,
        out_shape=[shape] * 4,
        compiler_params=params(),
        cost_estimate=cost(20 * EXPERTS * CAP * rows, 8 * EXPERTS * CAP * rows),
        name="route_slots",
    )(routes.T, gates.T)


def project_kernel(place_ref, *refs, count, lines, share):
    xs = refs[:count]
    ws = refs[count : count + lines * share]
    o_ref, part_ref, full = refs[count + lines * share :]
    size, wide = ws[0].shape
    cols = wide // 4
    rows = xs[0].shape[0]
    for s in range(share):
        for m in range(lines):
            start = pl.multiple_of((place_ref[0] ^ m) * size, size)
            full[place_ref[1] ^ s, pl.ds(start, size), :] = ws[s * lines + m][...]
    mine = share * cols
    for s in range(share):
        for j in range(count):
            got = mm(xs[j][...], full[s, :, : 3 * cols]).astype(bf16)
            for t in range(3):
                o_ref[j * rows : (j + 1) * rows, t * mine + s * cols : t * mine + (s + 1) * cols] = got[
                    :, t * cols : (t + 1) * cols
                ]
        part_ref[:, s * cols : (s + 1) * cols] = full[s, :, 3 * cols :]


def project_call(place, xs, ws, lines, share):
    rows, width = xs[0].shape
    count = len(xs)
    wide = ws[0].shape[1]
    cols = wide // 4
    vm = pl.BlockSpec(memory_space=pltpu.VMEM)
    return pl.pallas_call(
        functools.partial(project_kernel, count=count, lines=lines, share=share),
        out_shape=[
            jax.ShapeDtypeStruct((count * rows, 3 * share * cols), bf16),
            jax.ShapeDtypeStruct((width, share * cols), bf16),
        ],
        in_specs=[pl.BlockSpec(memory_space=pltpu.SMEM)] + [vm] * (count + lines * share),
        out_specs=[vm, vm],
        scratch_shapes=[pltpu.VMEM((share, width, wide), bf16)],
        compiler_params=params(),
        cost_estimate=cost(6 * count * rows * width * cols * share, 2 * width * (count * rows + 2 * wide * share)),
        name="project",
    )(place, *xs, *ws)


def attend_kernel(p_ref, *o_refs, blocks):
    cols = p_ref.shape[1] // 3
    rows = o_refs[0].shape[0]
    lane = lax.broadcasted_iota(jnp.int32, (rows, cols), 1) // HD
    keys = p_ref[:, cols : 2 * cols]
    values = p_ref[:, 2 * cols :]
    for o_ref, j in zip(o_refs, blocks):
        queries = p_ref[j * rows : (j + 1) * rows, :cols] * jnp.asarray(HD ** (-0.5), bf16)
        mixed = None
        for h in range(cols // HD):
            mine = lane == h
            q = jnp.where(mine, queries, jnp.zeros_like(queries))
            scores = mm(q, keys, (((1,), (1,)), ((), ())))
            weights = jnp.exp(scores - jnp.max(scores, axis=-1, keepdims=True))
            probs = (weights * (1.0 / jnp.sum(weights, axis=-1, keepdims=True))).astype(bf16)
            part = mm(probs, values)
            mixed = part if mixed is None else jnp.where(mine, part, mixed)
        o_ref[...] = mixed.astype(bf16)


def attend_call(projected, blocks, rows):
    length, width = projected.shape[0], projected.shape[1] // 3
    return pl.pallas_call(
        functools.partial(attend_kernel, blocks=blocks),
        out_shape=[jax.ShapeDtypeStruct((rows, width), bf16)] * len(blocks),
        compiler_params=params(24),
        cost_estimate=cost(
            16 * len(blocks) * rows * length * width, 2 * projected.size, len(blocks) * rows * length * width // HD
        ),
        name="attend",
    )(projected)


def output_kernel(place_ref, t_ref, d_ref, *refs):
    ctxs, parts = refs[:SPAN], refs[SPAN : 2 * SPAN]
    r_ref, o_ref, c_ref, a_ref = refs[2 * SPAN :]
    wide = ctxs[0].shape[1]
    starts = [pl.multiple_of((place_ref[0] ^ j) * wide, wide) for j in range(SPAN)]
    for j in range(SPAN):
        c_ref[:, pl.ds(starts[j], wide)] = ctxs[j][...]
    for j in range(SPAN):
        a_ref[:, pl.ds(starts[j], wide)] = mm(c_ref[...], parts[j][...])
    total = t_ref[...].astype(f32) + a_ref[...]
    r_ref[...] = total
    o_ref[...] = mm(d_ref[...], normalize(total)).astype(bf16)


def output_call(place, tokens, marks, parts, ctxs):
    rows, width = tokens.shape
    vm = pl.BlockSpec(memory_space=pltpu.VMEM)
    return pl.pallas_call(
        output_kernel,
        out_shape=[
            jax.ShapeDtypeStruct((rows, width), f32),
            jax.ShapeDtypeStruct((marks.shape[0], width), bf16),
        ],
        in_specs=[pl.BlockSpec(memory_space=pltpu.SMEM)] + [vm] * (2 + 2 * SPAN),
        out_specs=[vm, vm],
        scratch_shapes=[pltpu.VMEM((rows, width), bf16), pltpu.VMEM((rows, width), f32)],
        compiler_params=params(),
        cost_estimate=cost(2 * rows * width * (width + marks.shape[0]), 6 * width * width),
        name="out_projection",
    )(place, tokens, marks, *ctxs, *parts)


def gelu(x):
    return jax.nn.gelu(x, approximate=True)


def expert_kernel(x_ref, win_ref, wout_ref, o_ref, *scratch, local, sources, step, ahead):
    rows_ref, hid_ref, pre_ref, acc_ref, term_ref, in_buf, out_buf, in_sem, out_sem = scratch
    count = sources * CAP
    width = x_ref.shape[1]
    hidden = win_ref.shape[1] // local
    steps = hidden // step
    pack = 4 * CAP

    def load_in(e, n):
        return pltpu.make_async_copy(
            win_ref.at[:, pl.ds(e * hidden + n * step, step)], in_buf.at[n], in_sem.at[n]
        )

    def load_out(e, n):
        return pltpu.make_async_copy(
            wout_ref.at[pl.ds(e * hidden + n * step, step), :],
            out_buf.at[pl.ds(n * step, step), :],
            out_sem.at[n],
        )

    chain = [load(e, n) for e in range(local) for load in (load_in, load_out) for n in range(steps)]

    def arrive(t):
        chain[t].wait()
        if t + ahead < len(chain):
            chain[t + ahead].start()

    for load in chain[:ahead]:
        load.start()

    if local > 1:
        to = lax.broadcasted_iota(jnp.int32, (local * pack, local * pack), 0)
        have = lax.broadcasted_iota(jnp.int32, (local * pack, local * pack), 1)
        expert = to // pack
        inner = to - expert * pack
        source = inner // CAP
        wanted = source * (local * CAP) + expert * CAP + (inner - source * CAP)
        order = jnp.where(have == wanted, 1.0, 0.0).astype(bf16)
        for g in range(count // pack):
            part = mm(order, x_ref[g * local * pack : (g + 1) * local * pack, :]).astype(bf16)
            for e in range(local):
                rows_ref[e, g * pack : (g + 1) * pack, :] = part[e * pack : (e + 1) * pack, :]

    for e in range(local):
        for n in range(steps):
            arrive(2 * e * steps + n)
            rows = rows_ref[e] if local > 1 else x_ref[...]
            pre_ref[n % 2] = mm(rows, in_buf[n])
            if n:
                hid_ref[:, (n - 1) * step : n * step] = gelu(pre_ref[(n - 1) % 2]).astype(bf16)
        hid_ref[:, (steps - 1) * step :] = gelu(pre_ref[(steps - 1) % 2]).astype(bf16)
        for n in range(steps):
            arrive((2 * e + 1) * steps + n)
            part = mm(hid_ref[:, n * step : (n + 1) * step], out_buf[n * step : (n + 1) * step, :])
            if n:
                part = acc_ref[...] + part
            if n + 1 < steps:
                acc_ref[...] = part
            elif local > 1:
                term_ref[e] = part.astype(bf16)
            else:
                o_ref[...] = part.astype(bf16)

    if local > 1:
        for g in range(count // pack):
            part = jnp.concatenate([term_ref[e, g * pack : (g + 1) * pack, :] for e in range(local)], axis=0)
            back = mm(order, part, (((0,), (0,)), ((), ())))
            o_ref[g * local * pack : (g + 1) * local * pack, :] = back.astype(bf16)


def expert_call(arrived, w_in, w_out, local, sources, step=2048, ahead=2):
    count = sources * CAP
    width = arrived.shape[1]
    hidden = w_in.shape[1] // local
    steps = hidden // step
    kept = (local, count, width) if local > 1 else (1, 16, 128)
    vm = pl.BlockSpec(memory_space=pltpu.VMEM)
    hbm = pl.BlockSpec(memory_space=pl.ANY)
    return pl.pallas_call(
        functools.partial(expert_kernel, local=local, sources=sources, step=step, ahead=ahead),
        out_shape=jax.ShapeDtypeStruct(arrived.shape, bf16),
        in_specs=[vm, hbm, hbm],
        out_specs=vm,
        scratch_shapes=[
            pltpu.VMEM(kept, bf16),
            pltpu.VMEM((count, hidden), bf16),
            pltpu.VMEM((2, count, step), f32),
            pltpu.VMEM((count, width), f32),
            pltpu.VMEM(kept, bf16),
            pltpu.VMEM((steps, width, step), bf16),
            pltpu.VMEM((hidden, width), bf16),
            pltpu.SemaphoreType.DMA((steps,)),
            pltpu.SemaphoreType.DMA((steps,)),
        ],
        compiler_params=params(52),
        cost_estimate=cost(4 * count * width * hidden * local, 4 * width * hidden * local, count * hidden * local),
        name="experts",
    )(arrived, w_in, w_out)


def combine_kernel(r_ref, b_ref, hi_ref, mid_ref, lo_ref, o_ref):
    dims = (((0,), (0,)), ((), ()))
    back = b_ref[...]
    mixture = mm(lo_ref[...], back, dims)
    mixture = mixture + mm(mid_ref[...], back, dims)
    mixture = mixture + mm(hi_ref[...], back, dims)
    o_ref[...] = (r_ref[...] + mixture).astype(bf16)


def combine_call(resid, back, parts):
    return pl.pallas_call(
        combine_kernel,
        out_shape=jax.ShapeDtypeStruct(resid.shape, bf16),
        compiler_params=params(),
        cost_estimate=cost(6 * back.size * resid.shape[0], 6 * resid.size + 2 * back.size),
        name="combine",
    )(resid, back, *parts)


def swap(value, axis, bits):
    size = math.prod(lax.axis_size(name) for name in axis) if isinstance(axis, tuple) else lax.axis_size(axis)
    return lax.ppermute(value, axis, [(i, i ^ bits) for i in range(size)])


def per_device(tokens, routes, gates, qkv_weight, out_weight, w_in, w_out):
    rows, width = tokens.shape
    devices = lax.axis_size("ctx")
    groups = lax.axis_size("groups")
    lines_total = devices // SPAN
    me = lax.axis_index("ctx")
    member = me % SPAN
    line = me // SPAN
    group = lax.axis_index("groups")
    parts_ff = max(1, devices // EXPERTS)
    local_experts = max(1, EXPERTS // devices)

    mine = width // SPAN
    share = groups if (mine // HD) % groups == 0 else 1
    cols = mine // share
    offset = (group % share) * cols

    def columns(to):
        pieces = [
            lax.dynamic_slice_in_dim(qkv_weight, t * width + to * mine + offset, cols, 1)
            for t in range(3)
        ]
        pieces.append(lax.dynamic_slice_in_dim(out_weight, to * mine + offset, cols, 1))
        return jnp.concatenate(pieces, axis=1)

    pieces = [columns(member)] + [swap(columns(member ^ j), "ctx", j) for j in range(1, SPAN)]
    block = jnp.zeros((SPAN,) + pieces[0].shape, bf16)
    for j in range(SPAN):
        block = lax.dynamic_update_slice(block, pieces[j][None], (member ^ j, 0, 0))
    block = block.reshape(-1, 4 * cols)
    normed, block = lax.optimization_barrier((norm_call(tokens), block))
    lines = {0: block}
    bit = lines_total // 2
    while bit:
        for known in list(lines):
            lines[known | bit] = swap(lines[known], "ctx", bit * SPAN)
        bit //= 2
    shares = [lines[m] for m in range(lines_total)]
    for s in range(1, share):
        shares += [swap(block, ("groups", "ctx"), s * devices + m * SPAN) if m < 2 else swap(lines[m], "groups", s) for m in range(lines_total)]

    far = swap(normed, "ctx", 2)
    near = swap(normed, "ctx", 1)
    both = swap(far, "ctx", 1)
    marks, *gate_parts = route_call(routes, gates)

    place = jnp.stack([line, group % share])
    projected, part = project_call(place, [normed, near, far, both], shares, lines_total, share)
    part_far = swap(part, "ctx", 2)
    part_near = swap(part, "ctx", 1)
    sent = attend_call(projected, (3, 2), rows)
    back = {3: swap(sent[0], "ctx", 3), 2: swap(sent[1], "ctx", 2)}
    projected, *sent = lax.optimization_barrier((projected, *sent))
    kept = attend_call(projected, (1, 0), rows)
    kept, part_far = lax.optimization_barrier((kept, part_far))
    part_both = swap(part_far, "ctx", 1)
    back[1] = swap(kept[0], "ctx", 1)
    back[0] = kept[1]
    ctxs = [back[j] for j in range(SPAN)]
    resid, table = output_call(
        member.reshape(1), tokens, marks, [part, part_near, part_far, part_both], ctxs
    )

    table = table.reshape(EXPERTS, CAP, width)
    if parts_ff > 1:
        table = jnp.repeat(table, parts_ff, axis=0)
    outgoing = table.reshape(devices, local_experts * CAP, width)
    arrived = lax.all_to_all(outgoing, "ctx", split_axis=0, concat_axis=0, tiled=True)
    produced = expert_call(arrived.reshape(-1, width), w_in, w_out, local_experts, devices)
    produced = produced.reshape(devices, local_experts * CAP, width)
    returned = lax.all_to_all(produced, "ctx", split_axis=0, concat_axis=0, tiled=True)
    if parts_ff > 1:
        grouped = returned.reshape(EXPERTS, parts_ff, CAP, width)
        returned = jnp.sum(grouped.astype(f32), axis=1).astype(bf16)
    return combine_call(resid, returned.reshape(EXPERTS * CAP, width), gate_parts)


def solution(mesh):
    in_specs = (
        P(("groups", "ctx"), None),
        P(("groups", "ctx"), None),
        P(("groups", "ctx"), None),
        P("ctx", None),
        P("ctx", None),
        P(None, "ctx"),
        P("ctx", None),
    )
    out_specs = P(("groups", "ctx"), None)
    return jax.shard_map(
        per_device, mesh=mesh, in_specs=in_specs, out_specs=out_specs, check_vma=False
    )
```

```python
import functools
import math

import jax
import jax.numpy as jnp
from jax import lax
from jax.experimental import pallas as pl
from jax.experimental.pallas import tpu as pltpu
from jax.sharding import PartitionSpec as P

HEADS = 16
HD = 64
EXPERTS = 32
SPAN = 4
CAP = 20
TOP = 2
MIB = 1 << 20

eps = 1e-06
bf16 = jnp.bfloat16
f32 = jnp.float32


def params(mib=40):
    return pltpu.CompilerParams(vmem_limit_bytes=mib * MIB)


def cost(flops, nbytes, trans=0):
    return pl.CostEstimate(flops=1, bytes_accessed=1, transcendentals=0)


def mm(a, b, dims=(((1,), (0,)), ((), ()))):
    return lax.dot_general(a, b, dims, preferred_element_type=f32)


def normalize(values):
    center = values - jnp.mean(values, axis=-1, keepdims=True)
    spread = jnp.mean(center * center, axis=-1, keepdims=True)
    return (center * lax.rsqrt(spread + eps)).astype(bf16)


def norm_kernel(x_ref, o_ref):
    o_ref[...] = normalize(x_ref[...].astype(f32))


def norm_call(tokens):
    return pl.pallas_call(
        norm_kernel,
        out_shape=jax.ShapeDtypeStruct(tokens.shape, bf16),
        compiler_params=params(),
        cost_estimate=cost(8 * tokens.size, 4 * tokens.size),
        name="norm_tokens",
    )(tokens)


def route_kernel(routes_ref, gates_ref, d_ref, hi_ref, mid_ref, lo_ref):
    rows = routes_ref.shape[1]
    slots = d_ref.shape[0]
    expert = lax.broadcasted_iota(jnp.int32, (EXPERTS, rows), 0)
    names = [expert == routes_ref[r : r + 1, :] for r in range(TOP)]
    counts = names[0]
    for other in names[1:]:
        counts = counts | other
    counts = jnp.where(counts, 1.0, 0.0).astype(bf16)
    earlier = lax.broadcasted_iota(jnp.int32, (rows, rows), 0) < lax.broadcasted_iota(
        jnp.int32, (rows, rows), 1
    )
    before = mm(counts, jnp.where(earlier, 1.0, 0.0).astype(bf16))
    place = lax.broadcasted_iota(jnp.int32, (slots, rows), 0)
    marks = jnp.zeros((slots, rows), f32)
    weights = jnp.zeros((slots, rows), f32)
    for r in range(TOP):
        position = jnp.sum(jnp.where(names[r], before, 0.0), axis=0, keepdims=True)
        slot = routes_ref[r : r + 1, :] * CAP + position.astype(jnp.int32)
        here = place == slot
        marks = jnp.where(here, 1.0, marks)
        weights = jnp.where(here, gates_ref[r : r + 1, :], weights)
    d_ref[...] = marks.astype(bf16)
    high = weights.astype(bf16)
    rest = weights - high.astype(f32)
    middle = rest.astype(bf16)
    hi_ref[...] = high
    mid_ref[...] = middle
    lo_ref[...] = (rest - middle.astype(f32)).astype(bf16)


def route_call(routes, gates):
    rows = routes.shape[0]
    shape = jax.ShapeDtypeStruct((EXPERTS * CAP, rows), bf16)
    return pl.pallas_call(
        route_kernel,
        out_shape=[shape] * 4,
        compiler_params=params(24),
        cost_estimate=cost(20 * EXPERTS * CAP * rows, 8 * EXPERTS * CAP * rows),
        name="route_slots",
    )(routes.T, gates.T)


def project_kernel(line_ref, *refs, count, lines, share):
    xs = refs[:count]
    ws = refs[count : count + lines * share]
    o_ref, part_ref, full = refs[count + lines * share :]
    size, wide = ws[0].shape
    cols = wide // 4
    rows = xs[0].shape[0]
    width = share * cols
    for s in range(share):
        for m in range(lines):
            start = pl.multiple_of((line_ref[0] ^ m) * size, size)
            full[s, pl.ds(start, size), :] = ws[s * lines + m][...]
    for s in range(share):
        for j in range(count):
            got = mm(xs[j][...], full[s, :, : 3 * cols]).astype(bf16)
            for t in range(3):
                o_ref[j * rows : (j + 1) * rows, t * width + s * cols : t * width + (s + 1) * cols] = got[
                    :, t * cols : (t + 1) * cols
                ]
        part_ref[:, s * cols : (s + 1) * cols] = full[s, :, 3 * cols :]


def project_call(line, xs, ws, lines):
    rows, width = xs[0].shape
    count = len(xs)
    share = len(ws) // lines
    wide = ws[0].shape[1]
    cols = wide // 4
    vm = pl.BlockSpec(memory_space=pltpu.VMEM)
    return pl.pallas_call(
        functools.partial(project_kernel, count=count, lines=lines, share=share),
        out_shape=[
            jax.ShapeDtypeStruct((count * rows, 3 * share * cols), bf16),
            jax.ShapeDtypeStruct((width, share * cols), bf16),
        ],
        in_specs=[pl.BlockSpec(memory_space=pltpu.SMEM)] + [vm] * (count + lines * share),
        out_specs=[vm, vm],
        scratch_shapes=[pltpu.VMEM((share, width, wide), bf16)],
        compiler_params=params(24),
        cost_estimate=cost(6 * count * rows * width * cols * share, 2 * width * (count * rows + 2 * wide * share)),
        name="project",
    )(line, *xs, *ws)


def attend_kernel(p_ref, *refs, blocks):
    befores, o_refs = refs[: -len(blocks)], refs[-len(blocks) :]
    cols = p_ref.shape[1] // 3
    rows = o_refs[0].shape[0]
    lane = lax.broadcasted_iota(jnp.int32, (rows, cols), 1) // HD
    keys = p_ref[:, cols : 2 * cols]
    values = p_ref[:, 2 * cols :]
    for i, j in enumerate(blocks):
        queries = p_ref[j * rows : (j + 1) * rows, :cols] * jnp.asarray(HD ** (-0.5), bf16)
        mixed = None
        for h in range(cols // HD):
            mine = lane == h
            q = jnp.where(mine, queries, jnp.zeros_like(queries))
            scores = mm(q, keys, (((1,), (1,)), ((), ())))
            weights = jnp.exp(scores - jnp.max(scores, axis=-1, keepdims=True))
            probs = (weights * (1.0 / jnp.sum(weights, axis=-1, keepdims=True))).astype(bf16)
            part = mm(probs, values)
            mixed = part if mixed is None else jnp.where(mine, part, mixed)
        mixed = mixed.astype(bf16)
        if befores:
            first = befores[i].shape[1]
            o_refs[i][:, :first] = befores[i][...]
            o_refs[i][:, first:] = mixed
        else:
            o_refs[i][...] = mixed


def attend_call(projected, blocks, rows, befores=()):
    length, width = projected.shape[0], projected.shape[1] // 3
    first = befores[0].shape[1] if befores else 0
    return pl.pallas_call(
        functools.partial(attend_kernel, blocks=blocks),
        out_shape=[jax.ShapeDtypeStruct((rows, first + width), bf16)] * len(blocks),
        compiler_params=params(24),
        cost_estimate=cost(
            16 * len(blocks) * rows * length * width, 2 * projected.size, len(blocks) * rows * length * width // HD
        ),
        name="attend",
    )(projected, *befores)


def output_kernel(place_ref, t_ref, d_ref, *refs, share, split):
    ctxs, parts = refs[:SPAN], refs[SPAN : SPAN + 3 * split]
    r_ref, o_ref, c_ref, a_ref = refs[SPAN + 3 * split :]
    wide = ctxs[0].shape[1]
    cols = wide // share
    starts = [pl.multiple_of((place_ref[0] ^ j) * wide, wide) for j in range(SPAN)]

    def natural(value):
        pieces = []
        for p in range(share):
            piece = value[:, :cols]
            for s in range(1, share):
                piece = jnp.where((place_ref[1] ^ s) == p, value[:, s * cols : (s + 1) * cols], piece)
            pieces.append(piece)
        return jnp.concatenate(pieces, axis=1) if share > 1 else value

    def columns(j):
        pieces = []
        for own, far, near in (parts[3 * k : 3 * k + 3] for k in range(split)):
            size = own.shape[1]
            pieces.append((own, near, far, near)[j][:, size * (j == 3) : size * (j == 3) + size])
        return jnp.concatenate(pieces, axis=1) if split > 1 else pieces[0]

    for j in range(SPAN):
        c_ref[:, pl.ds(starts[j], wide)] = natural(ctxs[j][...])
    for j in range(SPAN):
        a_ref[:, pl.ds(starts[j], wide)] = natural(mm(c_ref[...], columns(j)))
    total = t_ref[...].astype(f32) + a_ref[...]
    r_ref[...] = total
    o_ref[...] = mm(d_ref[...], normalize(total)).astype(bf16)


def output_call(place, tokens, marks, parts, ctxs, share):
    rows, width = tokens.shape
    vm = pl.BlockSpec(memory_space=pltpu.VMEM)
    return pl.pallas_call(
        functools.partial(output_kernel, share=share, split=len(parts) // 3),
        out_shape=[
            jax.ShapeDtypeStruct((rows, width), f32),
            jax.ShapeDtypeStruct((marks.shape[0], width), bf16),
        ],
        in_specs=[pl.BlockSpec(memory_space=pltpu.SMEM)] + [vm] * (2 + SPAN + len(parts)),
        out_specs=[vm, vm],
        scratch_shapes=[pltpu.VMEM((rows, width), bf16), pltpu.VMEM((rows, width), f32)],
        compiler_params=params(24),
        cost_estimate=cost(2 * rows * width * (width + marks.shape[0]), 6 * width * width),
        name="out_projection",
    )(place, tokens, marks, *ctxs, *parts)


def gelu(x):
    return jax.nn.gelu(x, approximate=True)


def expert_kernel(x_ref, win_ref, wout_ref, o_ref, *scratch, local, sources, step, ahead):
    rows_ref, hid_ref, pre_ref, acc_ref, term_ref, in_buf, out_buf, in_sem, out_sem = scratch
    count = sources * CAP
    width = x_ref.shape[1]
    hidden = win_ref.shape[1] // local
    steps = hidden // step
    pack = 4 * CAP

    def load_in(e, n):
        return pltpu.make_async_copy(
            win_ref.at[:, pl.ds(e * hidden + n * step, step)], in_buf.at[n], in_sem.at[n]
        )

    def load_out(e, n):
        return pltpu.make_async_copy(
            wout_ref.at[pl.ds(e * hidden + n * step, step), :],
            out_buf.at[pl.ds(n * step, step), :],
            out_sem.at[n],
        )

    chain = [load(e, n) for e in range(local) for load in (load_in, load_out) for n in range(steps)]

    def arrive(t):
        chain[t].wait()
        if t + ahead < len(chain):
            chain[t + ahead].start()

    for load in chain[:ahead]:
        load.start()

    if local > 1:
        to = lax.broadcasted_iota(jnp.int32, (local * pack, local * pack), 0)
        have = lax.broadcasted_iota(jnp.int32, (local * pack, local * pack), 1)
        expert = to // pack
        inner = to - expert * pack
        source = inner // CAP
        wanted = source * (local * CAP) + expert * CAP + (inner - source * CAP)
        order = jnp.where(have == wanted, 1.0, 0.0).astype(bf16)
        for g in range(count // pack):
            part = mm(order, x_ref[g * local * pack : (g + 1) * local * pack, :]).astype(bf16)
            for e in range(local):
                rows_ref[e, g * pack : (g + 1) * pack, :] = part[e * pack : (e + 1) * pack, :]

    for e in range(local):
        for n in range(steps):
            arrive(2 * e * steps + n)
            rows = rows_ref[e] if local > 1 else x_ref[...]
            pre_ref[n % 2] = mm(rows, in_buf[n])
            if n:
                hid_ref[:, (n - 1) * step : n * step] = gelu(pre_ref[(n - 1) % 2]).astype(bf16)
        hid_ref[:, (steps - 1) * step :] = gelu(pre_ref[(steps - 1) % 2]).astype(bf16)
        for n in range(steps):
            arrive((2 * e + 1) * steps + n)
            part = mm(hid_ref[:, n * step : (n + 1) * step], out_buf[n * step : (n + 1) * step, :])
            if n:
                part = acc_ref[...] + part
            if n + 1 < steps:
                acc_ref[...] = part
            elif local > 1:
                term_ref[e] = part.astype(bf16)
            else:
                o_ref[...] = part.astype(bf16)

    if local > 1:
        for g in range(count // pack):
            part = jnp.concatenate([term_ref[e, g * pack : (g + 1) * pack, :] for e in range(local)], axis=0)
            back = mm(order, part, (((0,), (0,)), ((), ())))
            o_ref[g * local * pack : (g + 1) * local * pack, :] = back.astype(bf16)


def expert_call(arrived, w_in, w_out, local, sources, step=2048, ahead=2):
    count = sources * CAP
    width = arrived.shape[1]
    hidden = w_in.shape[1] // local
    steps = hidden // step
    kept = (local, count, width) if local > 1 else (1, 16, 128)
    vm = pl.BlockSpec(memory_space=pltpu.VMEM)
    hbm = pl.BlockSpec(memory_space=pl.ANY)
    return pl.pallas_call(
        functools.partial(expert_kernel, local=local, sources=sources, step=step, ahead=ahead),
        out_shape=jax.ShapeDtypeStruct(arrived.shape, bf16),
        in_specs=[vm, hbm, hbm],
        out_specs=vm,
        scratch_shapes=[
            pltpu.VMEM(kept, bf16),
            pltpu.VMEM((count, hidden), bf16),
            pltpu.VMEM((2, count, step), f32),
            pltpu.VMEM((count, width), f32),
            pltpu.VMEM(kept, bf16),
            pltpu.VMEM((steps, width, step), bf16),
            pltpu.VMEM((hidden, width), bf16),
            pltpu.SemaphoreType.DMA((steps,)),
            pltpu.SemaphoreType.DMA((steps,)),
        ],
        compiler_params=params(52),
        cost_estimate=cost(4 * count * width * hidden * local, 4 * width * hidden * local, count * hidden * local),
        name="experts",
    )(arrived, w_in, w_out)


def combine_kernel(r_ref, b_ref, hi_ref, mid_ref, lo_ref, o_ref):
    dims = (((0,), (0,)), ((), ()))
    back = b_ref[...]
    mixture = mm(lo_ref[...], back, dims)
    mixture = mixture + mm(mid_ref[...], back, dims)
    mixture = mixture + mm(hi_ref[...], back, dims)
    o_ref[...] = (r_ref[...] + mixture).astype(bf16)


def combine_call(resid, back, parts):
    return pl.pallas_call(
        combine_kernel,
        out_shape=jax.ShapeDtypeStruct(resid.shape, bf16),
        compiler_params=params(),
        cost_estimate=cost(6 * back.size * resid.shape[0], 6 * resid.size + 2 * back.size),
        name="combine",
    )(resid, back, *parts)


def swap(value, axis, bits):
    size = math.prod(lax.axis_size(name) for name in axis) if isinstance(axis, tuple) else lax.axis_size(axis)
    return lax.ppermute(value, axis, [(i, i ^ bits) for i in range(size)])


def per_device(tokens, routes, gates, qkv_weight, out_weight, w_in, w_out):
    rows, width = tokens.shape
    devices = lax.axis_size("ctx")
    groups = lax.axis_size("groups")
    lines_total = devices // SPAN
    me = lax.axis_index("ctx")
    member = me % SPAN
    line = me // SPAN
    group = lax.axis_index("groups")
    parts_ff = max(1, devices // EXPERTS)
    local_experts = max(1, EXPERTS // devices)

    mine = width // SPAN
    share = groups if (mine // HD) % groups == 0 else 1
    cols = mine // share
    offset = (group % share) * cols

    def columns(to):
        pieces = [
            lax.dynamic_slice_in_dim(qkv_weight, t * width + to * mine + offset, cols, 1)
            for t in range(3)
        ]
        pieces.append(lax.dynamic_slice_in_dim(out_weight, to * mine + offset, cols, 1))
        return jnp.concatenate(pieces, axis=1)

    pieces = [columns(member)] + [swap(columns(member ^ j), "ctx", j) for j in range(1, SPAN)]
    block = jnp.zeros((SPAN,) + pieces[0].shape, bf16)
    for j in range(SPAN):
        block = lax.dynamic_update_slice(block, pieces[j][None], (member ^ j, 0, 0))
    block = block.reshape(-1, 4 * cols)
    slots = route_call(routes, gates)
    normed, block, *slots = lax.optimization_barrier((norm_call(tokens), block, *slots))
    marks, *gate_parts = slots
    bits = [1 << i for i in reversed(range(lines_total.bit_length() - 1))]
    lines = {0: block}
    for bit in bits:
        lines[bit] = swap(block, "ctx", bit * SPAN)
    others = {}
    for s in range(1, share):
        for m in range(min(2, lines_total)):
            others[s, m] = swap(block, ("groups", "ctx"), s * devices + m * SPAN)
    far = swap(normed, "ctx", 2)
    lines, others, far = lax.optimization_barrier((lines, others, far))
    for bit in bits[1:]:
        for known in [m for m in lines if m >= 2 * bit and m & (2 * bit - 1) == 0]:
            lines[known | bit] = swap(lines[known], "ctx", bit * SPAN)
    early = [m for m in range(2, lines_total) if m & (m - 1) == 0]
    for s in range(1, share):
        for m in early:
            others[s, m] = swap(lines[m], "groups", s)
    near = swap(jnp.concatenate([normed, far], axis=0), "ctx", 1)
    lines, others, near = lax.optimization_barrier((lines, others, near))
    for s in range(1, share):
        for m in range(lines_total):
            if (s, m) not in others:
                others[s, m] = swap(lines[m], "groups", s)

    crop = [normed, near[:rows], far, near[rows:]]
    spot = line.reshape(1)

    projected, part = project_call(spot, crop, [lines[m] for m in range(lines_total)], lines_total)

    def with_core(mine_part, far_part):
        return [mine_part, far_part, swap(jnp.concatenate([mine_part, far_part], axis=1), "ctx", 1)]

    across = swap(part, "ctx", 2)
    ctxs = attend_call(projected, (0, 1, 2, 3), rows)
    parts = []
    if share > 1:
        rest = [others[s, m] for s in range(1, share) for m in range(lines_total)]
        rest, ctxs, across = lax.optimization_barrier((rest, ctxs, across))
        parts = with_core(part, across)
        projected, part = project_call(spot, crop, rest, lines_total)
        across = swap(part, "ctx", 2)
        ctxs = attend_call(projected, (0, 1, 2, 3), rows, ctxs)
    ctxs = [ctxs[0]] + [swap(ctxs[j], "ctx", j) for j in range(1, SPAN)]
    ctxs, across = lax.optimization_barrier((ctxs, across))
    parts += with_core(part, across)
    place = jnp.stack([member, group % share])
    resid, table = output_call(place, tokens, marks, parts, ctxs, share)

    table = table.reshape(EXPERTS, CAP, width)
    if parts_ff > 1:
        table = jnp.repeat(table, parts_ff, axis=0)
    outgoing = table.reshape(devices, local_experts * CAP, width)
    arrived = lax.all_to_all(outgoing, "ctx", split_axis=0, concat_axis=0, tiled=True)
    produced = expert_call(arrived.reshape(-1, width), w_in, w_out, local_experts, devices)
    produced = produced.reshape(devices, local_experts * CAP, width)
    returned = lax.all_to_all(produced, "ctx", split_axis=0, concat_axis=0, tiled=True)
    if parts_ff > 1:
        grouped = returned.reshape(EXPERTS, parts_ff, CAP, width)
        returned = jnp.sum(grouped.astype(f32), axis=1).astype(bf16)
    return combine_call(resid, returned.reshape(EXPERTS * CAP, width), gate_parts)


def solution(mesh):
    in_specs = (
        P(("groups", "ctx"), None),
        P(("groups", "ctx"), None),
        P(("groups", "ctx"), None),
        P("ctx", None),
        P("ctx", None),
        P(None, "ctx"),
        P("ctx", None),
    )
    out_specs = P(("groups", "ctx"), None)
    return jax.shard_map(
        per_device, mesh=mesh, in_specs=in_specs, out_specs=out_specs, check_vma=False
    )
```

```python
import functools
import math

import jax
import jax.numpy as jnp
from jax import lax
from jax.experimental import pallas as pl
from jax.experimental.pallas import tpu as pltpu
from jax.sharding import PartitionSpec as P

HEADS = 16
HD = 64
EXPERTS = 32
SPAN = 4
CAP = 20
TOP = 2
MIB = 1 << 20

eps = 1e-06
bf16 = jnp.bfloat16
f32 = jnp.float32


def params(mib=16):
    return pltpu.CompilerParams(vmem_limit_bytes=mib * MIB)


def cost(flops, nbytes, trans=0):
    return pl.CostEstimate(flops=int(flops), bytes_accessed=int(nbytes), transcendentals=int(trans))


def mm(a, b, dims=(((1,), (0,)), ((), ()))):
    return lax.dot_general(a, b, dims, preferred_element_type=f32)


def normalize(values):
    center = values - jnp.mean(values, axis=-1, keepdims=True)
    spread = jnp.mean(center * center, axis=-1, keepdims=True)
    return (center * lax.rsqrt(spread + eps)).astype(bf16)


def norm_kernel(x_ref, o_ref):
    o_ref[...] = normalize(x_ref[...].astype(f32))


def norm_call(tokens):
    return pl.pallas_call(
        norm_kernel,
        out_shape=jax.ShapeDtypeStruct(tokens.shape, bf16),
        compiler_params=params(),
        cost_estimate=cost(8 * tokens.size, 4 * tokens.size),
        name="norm_tokens",
    )(tokens)


def route_kernel(routes_ref, gates_ref, d_ref, hi_ref, mid_ref, lo_ref):
    rows = routes_ref.shape[1]
    slots = d_ref.shape[0]
    expert = lax.broadcasted_iota(jnp.int32, (EXPERTS, rows), 0)
    names = [expert == routes_ref[r : r + 1, :] for r in range(TOP)]
    counts = names[0]
    for other in names[1:]:
        counts = counts | other
    counts = jnp.where(counts, 1.0, 0.0).astype(bf16)
    earlier = lax.broadcasted_iota(jnp.int32, (rows, rows), 0) < lax.broadcasted_iota(
        jnp.int32, (rows, rows), 1
    )
    before = mm(counts, jnp.where(earlier, 1.0, 0.0).astype(bf16))
    place = lax.broadcasted_iota(jnp.int32, (slots, rows), 0)
    marks = jnp.zeros((slots, rows), f32)
    weights = jnp.zeros((slots, rows), f32)
    for r in range(TOP):
        position = jnp.sum(jnp.where(names[r], before, 0.0), axis=0, keepdims=True)
        slot = routes_ref[r : r + 1, :] * CAP + position.astype(jnp.int32)
        here = place == slot
        marks = jnp.where(here, 1.0, marks)
        weights = jnp.where(here, gates_ref[r : r + 1, :], weights)
    d_ref[...] = marks.astype(bf16)
    high = weights.astype(bf16)
    rest = weights - high.astype(f32)
    middle = rest.astype(bf16)
    hi_ref[...] = high
    mid_ref[...] = middle
    lo_ref[...] = (rest - middle.astype(f32)).astype(bf16)


def route_call(routes, gates):
    rows = routes.shape[0]
    shape = jax.ShapeDtypeStruct((EXPERTS * CAP, rows), bf16)
    return pl.pallas_call(
        route_kernel,
        out_shape=[shape] * 4,
        compiler_params=params(),
        cost_estimate=cost(20 * EXPERTS * CAP * rows, 8 * EXPERTS * CAP * rows),
        name="route_slots",
    )(routes.T, gates.T)


def part_kernel(place_ref, *refs, lines, share):
    ws, o_ref, full = refs[: lines * share], refs[lines * share], refs[lines * share + 1]
    size, wide = ws[0].shape
    cols = wide // 4
    for s in range(share):
        for m in range(lines):
            start = pl.multiple_of((place_ref[0] ^ m) * size, size)
            full[place_ref[1] ^ s, pl.ds(start, size), :] = ws[s * lines + m][:, 3 * cols :]
    for s in range(share):
        o_ref[:, s * cols : (s + 1) * cols] = full[s]


def part_call(place, ws, lines, share):
    size, wide = ws[0].shape
    cols = wide // 4
    vm = pl.BlockSpec(memory_space=pltpu.VMEM)
    return pl.pallas_call(
        functools.partial(part_kernel, lines=lines, share=share),
        out_shape=jax.ShapeDtypeStruct((lines * size, share * cols), bf16),
        in_specs=[pl.BlockSpec(memory_space=pltpu.SMEM)] + [vm] * (lines * share),
        out_specs=vm,
        scratch_shapes=[pltpu.VMEM((share, lines * size, cols), bf16)],
        compiler_params=params(),
        cost_estimate=cost(1, 4 * lines * size * share * cols),
        name="out_weight_part",
    )(place, *ws)


def project_kernel(place_ref, *refs, count, lines, share):
    xs = refs[:count]
    ws = refs[count : count + lines * share]
    o_ref, full = refs[count + lines * share :]
    size, wide = ws[0].shape
    cols = wide // 4
    rows = xs[0].shape[0]
    mine = share * cols
    for s in range(share):
        for m in range(lines):
            start = pl.multiple_of((place_ref[0] ^ m) * size, size)
            full[place_ref[1] ^ s, pl.ds(start, size), :] = ws[s * lines + m][:, : 3 * cols]
    for s in range(share):
        for j in range(count):
            got = mm(xs[j][...], full[s]).astype(bf16)
            for t in range(3):
                o_ref[j * rows : (j + 1) * rows, t * mine + s * cols : t * mine + (s + 1) * cols] = got[
                    :, t * cols : (t + 1) * cols
                ]


def project_call(place, xs, ws, lines, share):
    rows, width = xs[0].shape
    count = len(xs)
    cols = ws[0].shape[1] // 4
    vm = pl.BlockSpec(memory_space=pltpu.VMEM)
    return pl.pallas_call(
        functools.partial(project_kernel, count=count, lines=lines, share=share),
        out_shape=jax.ShapeDtypeStruct((count * rows, 3 * share * cols), bf16),
        in_specs=[pl.BlockSpec(memory_space=pltpu.SMEM)] + [vm] * (count + lines * share),
        out_specs=vm,
        scratch_shapes=[pltpu.VMEM((share, width, 3 * cols), bf16)],
        compiler_params=params(),
        cost_estimate=cost(6 * count * rows * width * cols * share, 2 * width * (count * rows + 8 * cols * share)),
        name="project",
    )(place, *xs, *ws)


def attend_kernel(p_ref, *o_refs, blocks):
    cols = p_ref.shape[1] // 3
    rows = o_refs[0].shape[0]
    lane = lax.broadcasted_iota(jnp.int32, (rows, cols), 1) // HD
    keys = p_ref[:, cols : 2 * cols]
    values = p_ref[:, 2 * cols :]
    for o_ref, j in zip(o_refs, blocks):
        queries = p_ref[j * rows : (j + 1) * rows, :cols] * jnp.asarray(HD ** (-0.5), bf16)
        mixed = None
        for h in range(cols // HD):
            mine = lane == h
            q = jnp.where(mine, queries, jnp.zeros_like(queries))
            scores = mm(q, keys, (((1,), (1,)), ((), ())))
            weights = jnp.exp(scores - jnp.max(scores, axis=-1, keepdims=True))
            probs = (weights * (1.0 / jnp.sum(weights, axis=-1, keepdims=True))).astype(bf16)
            part = mm(probs, values)
            mixed = part if mixed is None else jnp.where(mine, part, mixed)
        o_ref[...] = mixed.astype(bf16)


def attend_call(projected, blocks, rows):
    length, width = projected.shape[0], projected.shape[1] // 3
    return pl.pallas_call(
        functools.partial(attend_kernel, blocks=blocks),
        out_shape=[jax.ShapeDtypeStruct((rows, width), bf16)] * len(blocks),
        compiler_params=params(),
        cost_estimate=cost(
            16 * len(blocks) * rows * length * width, 2 * projected.size, len(blocks) * rows * length * width // HD
        ),
        name="attend",
    )(projected)


def output_kernel(place_ref, t_ref, d_ref, *refs):
    ctxs, parts = refs[:SPAN], refs[SPAN : 2 * SPAN]
    r_ref, o_ref, c_ref, a_ref = refs[2 * SPAN :]
    wide = ctxs[0].shape[1]
    starts = [pl.multiple_of((place_ref[0] ^ j) * wide, wide) for j in range(SPAN)]
    for j in range(SPAN):
        c_ref[:, pl.ds(starts[j], wide)] = ctxs[j][...]
    for j in range(SPAN):
        a_ref[:, pl.ds(starts[j], wide)] = mm(c_ref[...], parts[j][...])
    total = t_ref[...].astype(f32) + a_ref[...]
    r_ref[...] = total
    o_ref[...] = mm(d_ref[...], normalize(total)).astype(bf16)


def output_call(place, tokens, marks, parts, ctxs):
    rows, width = tokens.shape
    vm = pl.BlockSpec(memory_space=pltpu.VMEM)
    return pl.pallas_call(
        output_kernel,
        out_shape=[
            jax.ShapeDtypeStruct((rows, width), f32),
            jax.ShapeDtypeStruct((marks.shape[0], width), bf16),
        ],
        in_specs=[pl.BlockSpec(memory_space=pltpu.SMEM)] + [vm] * (2 + 2 * SPAN),
        out_specs=[vm, vm],
        scratch_shapes=[pltpu.VMEM((rows, width), bf16), pltpu.VMEM((rows, width), f32)],
        compiler_params=params(),
        cost_estimate=cost(2 * rows * width * (width + marks.shape[0]), 6 * width * width),
        name="out_projection",
    )(place, tokens, marks, *ctxs, *parts)


def gelu(x):
    return jax.nn.gelu(x, approximate=True)


def expert_kernel(x_ref, win_ref, wout_ref, o_ref, *scratch, local, sources, step):
    rows_ref, hid_ref, pre_ref, term_ref, out_buf, sems = scratch
    count = sources * CAP
    hidden = win_ref.shape[1] // local
    steps = hidden // step
    pack = 4 * CAP

    def load(e, n):
        span = pl.ds(e * hidden + n * step, step)
        return pltpu.make_async_copy(wout_ref.at[span, :], out_buf.at[span, :], sems.at[e, n])

    for n in range(steps):
        load(0, n).start()

    if local > 1:
        to = lax.broadcasted_iota(jnp.int32, (local * pack, local * pack), 0)
        have = lax.broadcasted_iota(jnp.int32, (local * pack, local * pack), 1)
        expert = to // pack
        inner = to - expert * pack
        source = inner // CAP
        wanted = source * (local * CAP) + expert * CAP + (inner - source * CAP)
        order = jnp.where(have == wanted, 1.0, 0.0).astype(bf16)
        for g in range(count // pack):
            part = mm(order, x_ref[g * local * pack : (g + 1) * local * pack, :]).astype(bf16)
            for e in range(local):
                rows_ref[e, g * pack : (g + 1) * pack, :] = part[e * pack : (e + 1) * pack, :]

    for e in range(local):
        for n in range(steps):
            start = e * hidden + n * step
            rows = rows_ref[e] if local > 1 else x_ref[...]
            pre_ref[n % 2] = mm(rows, win_ref[:, start : start + step])
            if n:
                hid_ref[:, (n - 1) * step : n * step] = gelu(pre_ref[(n - 1) % 2]).astype(bf16)
        hid_ref[:, (steps - 1) * step :] = gelu(pre_ref[(steps - 1) % 2]).astype(bf16)
        for n in range(steps):
            load(e, n).wait()
            if e + 1 < local:
                load(e + 1, n).start()
        term = mm(hid_ref[...], out_buf[e * hidden : (e + 1) * hidden, :]).astype(bf16)
        if local > 1:
            term_ref[e] = term
        else:
            o_ref[...] = term

    if local > 1:
        for g in range(count // pack):
            part = jnp.concatenate([term_ref[e, g * pack : (g + 1) * pack, :] for e in range(local)], axis=0)
            back = mm(order, part, (((0,), (0,)), ((), ())))
            o_ref[g * local * pack : (g + 1) * local * pack, :] = back.astype(bf16)


def expert_call(arrived, w_in, w_out, local, sources, step=1024):
    count = sources * CAP
    width = arrived.shape[1]
    hidden = w_in.shape[1] // local
    kept = (local, count, width) if local > 1 else (1, 16, 128)
    w_in = pltpu.with_memory_space_constraint(w_in, pltpu.VMEM)
    vm = pl.BlockSpec(memory_space=pltpu.VMEM)
    return pl.pallas_call(
        functools.partial(expert_kernel, local=local, sources=sources, step=step),
        out_shape=jax.ShapeDtypeStruct(arrived.shape, bf16),
        in_specs=[vm, vm, pl.BlockSpec(memory_space=pl.ANY)],
        out_specs=vm,
        scratch_shapes=[
            pltpu.VMEM(kept, bf16),
            pltpu.VMEM((count, hidden), bf16),
            pltpu.VMEM((2, count, step), f32),
            pltpu.VMEM(kept, bf16),
            pltpu.VMEM(w_out.shape, bf16),
            pltpu.SemaphoreType.DMA((local, hidden // step)),
        ],
        compiler_params=params(36),
        cost_estimate=cost(4 * count * width * hidden * local, 4 * width * hidden * local, count * hidden * local),
        name="experts",
    )(arrived, w_in, w_out)


def combine_kernel(r_ref, b_ref, hi_ref, mid_ref, lo_ref, o_ref):
    dims = (((0,), (0,)), ((), ()))
    back = b_ref[...]
    mixture = mm(lo_ref[...], back, dims)
    mixture = mixture + mm(mid_ref[...], back, dims)
    mixture = mixture + mm(hi_ref[...], back, dims)
    o_ref[...] = (r_ref[...] + mixture).astype(bf16)


def combine_call(resid, back, parts):
    return pl.pallas_call(
        combine_kernel,
        out_shape=jax.ShapeDtypeStruct(resid.shape, bf16),
        compiler_params=params(),
        cost_estimate=cost(6 * back.size * resid.shape[0], 6 * resid.size + 2 * back.size),
        name="combine",
    )(resid, back, *parts)


def swap(value, axis, bits):
    size = math.prod(lax.axis_size(name) for name in axis) if isinstance(axis, tuple) else lax.axis_size(axis)
    return lax.ppermute(value, axis, [(i, i ^ bits) for i in range(size)])


def per_device(tokens, routes, gates, qkv_weight, out_weight, w_in, w_out):
    rows, width = tokens.shape
    devices = lax.axis_size("ctx")
    groups = lax.axis_size("groups")
    lines_total = devices // SPAN
    me = lax.axis_index("ctx")
    member = me % SPAN
    line = me // SPAN
    group = lax.axis_index("groups")
    parts_ff = max(1, devices // EXPERTS)
    local_experts = max(1, EXPERTS // devices)

    mine = width // SPAN
    share = groups if (mine // HD) % groups == 0 else 1
    cols = mine // share
    offset = (group % share) * cols

    def columns(to):
        pieces = [
            lax.dynamic_slice_in_dim(qkv_weight, t * width + to * mine + offset, cols, 1)
            for t in range(3)
        ]
        pieces.append(lax.dynamic_slice_in_dim(out_weight, to * mine + offset, cols, 1))
        return jnp.concatenate(pieces, axis=1)

    pieces = [columns(member)] + [swap(columns(member ^ j), "ctx", j) for j in range(1, SPAN)]
    block = jnp.zeros((SPAN,) + pieces[0].shape, bf16)
    for j in range(SPAN):
        block = lax.dynamic_update_slice(block, pieces[j][None], (member ^ j, 0, 0))
    block = block.reshape(-1, 4 * cols)
    slots = route_call(routes, gates)
    normed, block, slots = lax.optimization_barrier((norm_call(tokens), block, slots))
    marks, *gate_parts = slots
    lines = {0: block}
    bit = lines_total // 2
    while bit:
        for known in list(lines):
            lines[known | bit] = swap(lines[known], "ctx", bit * SPAN)
        bit //= 2
    shares = [lines[m] for m in range(lines_total)]
    for s in range(1, share):
        shares += [swap(block, ("groups", "ctx"), s * devices + m * SPAN) if m < 2 else swap(lines[m], "groups", s) for m in range(lines_total)]

    far = swap(normed, "ctx", 2)
    near = swap(normed, "ctx", 1)
    both = swap(far, "ctx", 1)
    place = jnp.stack([line, group % share])
    part = part_call(place, shares, lines_total, share)
    part_far = swap(part, "ctx", 2)
    part_near = swap(part, "ctx", 1)
    projected = project_call(place, [normed, near, far, both], shares, lines_total, share)
    ctxs = attend_call(projected, (0, 1, 2, 3), rows)
    own, part_far = lax.optimization_barrier((ctxs[0], part_far))
    part_both = swap(part_far, "ctx", 1)
    back = {0: own} | {j: swap(ctxs[j], "ctx", j) for j in range(1, SPAN)}
    ctxs = [back[j] for j in range(SPAN)]
    resid, table = output_call(
        member.reshape(1), tokens, marks, [part, part_near, part_far, part_both], ctxs
    )

    table = table.reshape(EXPERTS, CAP, width)
    if parts_ff > 1:
        table = jnp.repeat(table, parts_ff, axis=0)
    outgoing = table.reshape(devices, local_experts * CAP, width)
    arrived = lax.all_to_all(outgoing, "ctx", split_axis=0, concat_axis=0, tiled=True)
    produced = expert_call(arrived.reshape(-1, width), w_in, w_out, local_experts, devices)
    produced = produced.reshape(devices, local_experts * CAP, width)
    returned = lax.all_to_all(produced, "ctx", split_axis=0, concat_axis=0, tiled=True)
    if parts_ff > 1:
        grouped = returned.reshape(EXPERTS, parts_ff, CAP, width)
        returned = jnp.sum(grouped.astype(f32), axis=1).astype(bf16)
    return combine_call(resid, returned.reshape(EXPERTS * CAP, width), gate_parts)


def solution(mesh):
    in_specs = (
        P(("groups", "ctx"), None),
        P(("groups", "ctx"), None),
        P(("groups", "ctx"), None),
        P("ctx", None),
        P("ctx", None),
        P(None, "ctx"),
        P("ctx", None),
    )
    out_specs = P(("groups", "ctx"), None)
    return jax.shard_map(
        per_device, mesh=mesh, in_specs=in_specs, out_specs=out_specs, check_vma=False
    )
```

```python
import functools
import math

import jax
import jax.numpy as jnp
from jax import lax
from jax.experimental import pallas as pl
from jax.experimental.pallas import tpu as pltpu
from jax.sharding import PartitionSpec as P

HEADS = 16
HD = 64
EXPERTS = 32
SPAN = 4
CAP = 20
TOP = 2
MIB = 1 << 20

eps = 1e-06
bf16 = jnp.bfloat16
f32 = jnp.float32


def params(mib=16):
    return pltpu.CompilerParams(vmem_limit_bytes=mib * MIB)


def cost(flops, nbytes, trans=0):
    return pl.CostEstimate(flops=int(flops), bytes_accessed=int(nbytes), transcendentals=int(trans))


def mm(a, b, dims=(((1,), (0,)), ((), ()))):
    return lax.dot_general(a, b, dims, preferred_element_type=f32)


def normalize(values):
    center = values - jnp.mean(values, axis=-1, keepdims=True)
    spread = jnp.mean(center * center, axis=-1, keepdims=True)
    return (center * lax.rsqrt(spread + eps)).astype(bf16)


def norm_kernel(x_ref, o_ref):
    o_ref[...] = normalize(x_ref[...].astype(f32))


def norm_call(tokens):
    return pl.pallas_call(
        norm_kernel,
        out_shape=jax.ShapeDtypeStruct(tokens.shape, bf16),
        compiler_params=params(),
        cost_estimate=cost(8 * tokens.size, 4 * tokens.size),
        name="norm_tokens",
    )(tokens)


def route_kernel(routes_ref, gates_ref, d_ref, hi_ref, mid_ref, lo_ref):
    rows = routes_ref.shape[1]
    slots = d_ref.shape[0]
    expert = lax.broadcasted_iota(jnp.int32, (EXPERTS, rows), 0)
    names = [expert == routes_ref[r : r + 1, :] for r in range(TOP)]
    counts = names[0]
    for other in names[1:]:
        counts = counts | other
    counts = jnp.where(counts, 1.0, 0.0).astype(bf16)
    earlier = lax.broadcasted_iota(jnp.int32, (rows, rows), 0) < lax.broadcasted_iota(
        jnp.int32, (rows, rows), 1
    )
    before = mm(counts, jnp.where(earlier, 1.0, 0.0).astype(bf16))
    place = lax.broadcasted_iota(jnp.int32, (slots, rows), 0)
    marks = jnp.zeros((slots, rows), f32)
    weights = jnp.zeros((slots, rows), f32)
    for r in range(TOP):
        position = jnp.sum(jnp.where(names[r], before, 0.0), axis=0, keepdims=True)
        slot = routes_ref[r : r + 1, :] * CAP + position.astype(jnp.int32)
        here = place == slot
        marks = jnp.where(here, 1.0, marks)
        weights = jnp.where(here, gates_ref[r : r + 1, :], weights)
    d_ref[...] = marks.astype(bf16)
    high = weights.astype(bf16)
    rest = weights - high.astype(f32)
    middle = rest.astype(bf16)
    hi_ref[...] = high
    mid_ref[...] = middle
    lo_ref[...] = (rest - middle.astype(f32)).astype(bf16)


def route_call(routes, gates):
    rows = routes.shape[0]
    shape = jax.ShapeDtypeStruct((EXPERTS * CAP, rows), bf16)
    return pl.pallas_call(
        route_kernel,
        out_shape=[shape] * 4,
        compiler_params=params(),
        cost_estimate=cost(20 * EXPERTS * CAP * rows, 8 * EXPERTS * CAP * rows),
        name="route_slots",
    )(routes.T, gates.T)


def part_kernel(place_ref, *refs, lines, share):
    ws, o_ref, full = refs[: lines * share], refs[lines * share], refs[lines * share + 1]
    size, wide = ws[0].shape
    cols = wide // 4
    for s in range(share):
        for m in range(lines):
            start = pl.multiple_of((place_ref[0] ^ m) * size, size)
            full[place_ref[1] ^ s, pl.ds(start, size), :] = ws[s * lines + m][:, 3 * cols :]
    for s in range(share):
        o_ref[:, s * cols : (s + 1) * cols] = full[s]


def part_call(place, ws, lines, share):
    size, wide = ws[0].shape
    cols = wide // 4
    vm = pl.BlockSpec(memory_space=pltpu.VMEM)
    return pl.pallas_call(
        functools.partial(part_kernel, lines=lines, share=share),
        out_shape=jax.ShapeDtypeStruct((lines * size, share * cols), bf16),
        in_specs=[pl.BlockSpec(memory_space=pltpu.SMEM)] + [vm] * (lines * share),
        out_specs=vm,
        scratch_shapes=[pltpu.VMEM((share, lines * size, cols), bf16)],
        compiler_params=params(),
        cost_estimate=cost(1, 4 * lines * size * share * cols),
        name="out_weight_part",
    )(place, *ws)


def project_kernel(place_ref, *refs, count, lines, share):
    xs = refs[:count]
    ws = refs[count : count + lines * share]
    o_ref, full = refs[count + lines * share :]
    size, wide = ws[0].shape
    cols = wide // 4
    rows = xs[0].shape[0]
    mine = share * cols
    for s in range(share):
        for m in range(lines):
            start = pl.multiple_of((place_ref[0] ^ m) * size, size)
            full[place_ref[1] ^ s, pl.ds(start, size), :] = ws[s * lines + m][:, : 3 * cols]
    for s in range(share):
        for j in range(count):
            got = mm(xs[j][...], full[s]).astype(bf16)
            for t in range(3):
                o_ref[j * rows : (j + 1) * rows, t * mine + s * cols : t * mine + (s + 1) * cols] = got[
                    :, t * cols : (t + 1) * cols
                ]


def project_call(place, xs, ws, lines, share):
    rows, width = xs[0].shape
    count = len(xs)
    cols = ws[0].shape[1] // 4
    vm = pl.BlockSpec(memory_space=pltpu.VMEM)
    return pl.pallas_call(
        functools.partial(project_kernel, count=count, lines=lines, share=share),
        out_shape=jax.ShapeDtypeStruct((count * rows, 3 * share * cols), bf16),
        in_specs=[pl.BlockSpec(memory_space=pltpu.SMEM)] + [vm] * (count + lines * share),
        out_specs=vm,
        scratch_shapes=[pltpu.VMEM((share, width, 3 * cols), bf16)],
        compiler_params=params(),
        cost_estimate=cost(6 * count * rows * width * cols * share, 2 * width * (count * rows + 8 * cols * share)),
        name="project",
    )(place, *xs, *ws)


def attend_kernel(p_ref, *o_refs, blocks):
    cols = p_ref.shape[1] // 3
    rows = o_refs[0].shape[0]
    lane = lax.broadcasted_iota(jnp.int32, (rows, cols), 1) // HD
    keys = p_ref[:, cols : 2 * cols]
    values = p_ref[:, 2 * cols :]
    for o_ref, j in zip(o_refs, blocks):
        queries = p_ref[j * rows : (j + 1) * rows, :cols] * jnp.asarray(HD ** (-0.5), bf16)
        mixed = None
        for h in range(cols // HD):
            mine = lane == h
            q = jnp.where(mine, queries, jnp.zeros_like(queries))
            scores = mm(q, keys, (((1,), (1,)), ((), ())))
            weights = jnp.exp(scores - jnp.max(scores, axis=-1, keepdims=True))
            probs = (weights * (1.0 / jnp.sum(weights, axis=-1, keepdims=True))).astype(bf16)
            part = mm(probs, values)
            mixed = part if mixed is None else jnp.where(mine, part, mixed)
        o_ref[...] = mixed.astype(bf16)


def attend_call(projected, blocks, rows):
    length, width = projected.shape[0], projected.shape[1] // 3
    return pl.pallas_call(
        functools.partial(attend_kernel, blocks=blocks),
        out_shape=[jax.ShapeDtypeStruct((rows, width), bf16)] * len(blocks),
        compiler_params=params(),
        cost_estimate=cost(
            16 * len(blocks) * rows * length * width, 2 * projected.size, len(blocks) * rows * length * width // HD
        ),
        name="attend",
    )(projected)


def output_kernel(place_ref, t_ref, d_ref, *refs):
    ctxs, parts = refs[:SPAN], refs[SPAN : 2 * SPAN]
    r_ref, o_ref, c_ref, a_ref = refs[2 * SPAN :]
    wide = ctxs[0].shape[1]
    starts = [pl.multiple_of((place_ref[0] ^ j) * wide, wide) for j in range(SPAN)]
    for j in range(SPAN):
        c_ref[:, pl.ds(starts[j], wide)] = ctxs[j][...]
    for j in range(SPAN):
        a_ref[:, pl.ds(starts[j], wide)] = mm(c_ref[...], parts[j][...])
    total = t_ref[...].astype(f32) + a_ref[...]
    r_ref[...] = total
    o_ref[...] = mm(d_ref[...], normalize(total)).astype(bf16)


def output_call(place, tokens, marks, parts, ctxs):
    rows, width = tokens.shape
    vm = pl.BlockSpec(memory_space=pltpu.VMEM)
    return pl.pallas_call(
        output_kernel,
        out_shape=[
            jax.ShapeDtypeStruct((rows, width), f32),
            jax.ShapeDtypeStruct((marks.shape[0], width), bf16),
        ],
        in_specs=[pl.BlockSpec(memory_space=pltpu.SMEM)] + [vm] * (2 + 2 * SPAN),
        out_specs=[vm, vm],
        scratch_shapes=[pltpu.VMEM((rows, width), bf16), pltpu.VMEM((rows, width), f32)],
        compiler_params=params(),
        cost_estimate=cost(2 * rows * width * (width + marks.shape[0]), 6 * width * width),
        name="out_projection",
    )(place, tokens, marks, *ctxs, *parts)


def gelu(x):
    return jax.nn.gelu(x, approximate=True)


def expert_kernel(x_ref, win_ref, wout_ref, o_ref, *scratch, local, sources, step):
    rows_ref, hid_ref, pre_ref, term_ref, out_buf, sems = scratch
    count = sources * CAP
    hidden = win_ref.shape[1] // local
    steps = hidden // step
    pack = 4 * CAP

    def load(e, n):
        span = pl.ds(e * hidden + n * step, step)
        return pltpu.make_async_copy(wout_ref.at[span, :], out_buf.at[span, :], sems.at[e, n])

    for n in range(steps):
        load(0, n).start()

    if local > 1:
        to = lax.broadcasted_iota(jnp.int32, (local * pack, local * pack), 0)
        have = lax.broadcasted_iota(jnp.int32, (local * pack, local * pack), 1)
        expert = to // pack
        inner = to - expert * pack
        source = inner // CAP
        wanted = source * (local * CAP) + expert * CAP + (inner - source * CAP)
        order = jnp.where(have == wanted, 1.0, 0.0).astype(bf16)
        for g in range(count // pack):
            part = mm(order, x_ref[g * local * pack : (g + 1) * local * pack, :]).astype(bf16)
            for e in range(local):
                rows_ref[e, g * pack : (g + 1) * pack, :] = part[e * pack : (e + 1) * pack, :]

    for e in range(local):
        for n in range(steps):
            start = e * hidden + n * step
            rows = rows_ref[e] if local > 1 else x_ref[...]
            pre_ref[n % 2] = mm(rows, win_ref[:, start : start + step])
            if n:
                hid_ref[:, (n - 1) * step : n * step] = gelu(pre_ref[(n - 1) % 2]).astype(bf16)
        hid_ref[:, (steps - 1) * step :] = gelu(pre_ref[(steps - 1) % 2]).astype(bf16)
        for n in range(steps):
            load(e, n).wait()
            if e + 1 < local:
                load(e + 1, n).start()
        term = mm(hid_ref[...], out_buf[e * hidden : (e + 1) * hidden, :]).astype(bf16)
        if local > 1:
            term_ref[e] = term
        else:
            o_ref[...] = term

    if local > 1:
        for g in range(count // pack):
            part = jnp.concatenate([term_ref[e, g * pack : (g + 1) * pack, :] for e in range(local)], axis=0)
            back = mm(order, part, (((0,), (0,)), ((), ())))
            o_ref[g * local * pack : (g + 1) * local * pack, :] = back.astype(bf16)


def expert_call(arrived, w_in, w_out, local, sources, step=1024):
    count = sources * CAP
    width = arrived.shape[1]
    hidden = w_in.shape[1] // local
    kept = (local, count, width) if local > 1 else (1, 16, 128)
    w_in = pltpu.with_memory_space_constraint(w_in, pltpu.VMEM)
    vm = pl.BlockSpec(memory_space=pltpu.VMEM)
    return pl.pallas_call(
        functools.partial(expert_kernel, local=local, sources=sources, step=step),
        out_shape=jax.ShapeDtypeStruct(arrived.shape, bf16),
        in_specs=[vm, vm, pl.BlockSpec(memory_space=pl.ANY)],
        out_specs=vm,
        scratch_shapes=[
            pltpu.VMEM(kept, bf16),
            pltpu.VMEM((count, hidden), bf16),
            pltpu.VMEM((2, count, step), f32),
            pltpu.VMEM(kept, bf16),
            pltpu.VMEM(w_out.shape, bf16),
            pltpu.SemaphoreType.DMA((local, hidden // step)),
        ],
        compiler_params=params(36),
        cost_estimate=cost(4 * count * width * hidden * local, 4 * width * hidden * local, count * hidden * local),
        name="experts",
    )(arrived, w_in, w_out)


def combine_kernel(r_ref, b_ref, hi_ref, mid_ref, lo_ref, o_ref):
    dims = (((0,), (0,)), ((), ()))
    back = b_ref[...]
    mixture = mm(lo_ref[...], back, dims)
    mixture = mixture + mm(mid_ref[...], back, dims)
    mixture = mixture + mm(hi_ref[...], back, dims)
    o_ref[...] = (r_ref[...] + mixture).astype(bf16)


def combine_call(resid, back, parts):
    return pl.pallas_call(
        combine_kernel,
        out_shape=jax.ShapeDtypeStruct(resid.shape, bf16),
        compiler_params=params(),
        cost_estimate=cost(6 * back.size * resid.shape[0], 6 * resid.size + 2 * back.size),
        name="combine",
    )(resid, back, *parts)


def swap(value, axis, bits):
    size = math.prod(lax.axis_size(name) for name in axis) if isinstance(axis, tuple) else lax.axis_size(axis)
    return lax.ppermute(value, axis, [(i, i ^ bits) for i in range(size)])


def per_device(tokens, routes, gates, qkv_weight, out_weight, w_in, w_out):
    rows, width = tokens.shape
    devices = lax.axis_size("ctx")
    groups = lax.axis_size("groups")
    lines_total = devices // SPAN
    me = lax.axis_index("ctx")
    member = me % SPAN
    line = me // SPAN
    group = lax.axis_index("groups")
    parts_ff = max(1, devices // EXPERTS)
    local_experts = max(1, EXPERTS // devices)

    mine = width // SPAN
    share = groups if (mine // HD) % groups == 0 else 1
    cols = mine // share
    offset = (group % share) * cols

    def columns(to):
        pieces = [
            lax.dynamic_slice_in_dim(qkv_weight, t * width + to * mine + offset, cols, 1)
            for t in range(3)
        ]
        pieces.append(lax.dynamic_slice_in_dim(out_weight, to * mine + offset, cols, 1))
        return jnp.concatenate(pieces, axis=1)

    pieces = [columns(member)] + [swap(columns(member ^ j), "ctx", j) for j in range(1, SPAN)]
    block = jnp.zeros((SPAN,) + pieces[0].shape, bf16)
    for j in range(SPAN):
        block = lax.dynamic_update_slice(block, pieces[j][None], (member ^ j, 0, 0))
    block = block.reshape(-1, 4 * cols)
    slots = route_call(routes, gates)
    normed, block, slots = lax.optimization_barrier((norm_call(tokens), block, slots))
    marks, *gate_parts = slots
    bits = [1 << i for i in reversed(range(lines_total.bit_length() - 1))]
    lines = {0: block}
    for bit in bits:
        lines[bit] = swap(block, "ctx", bit * SPAN)
    others = {}
    for s in range(1, share):
        for m in range(min(2, lines_total)):
            others[s, m] = swap(block, ("groups", "ctx"), s * devices + m * SPAN)
    if share > 1 and len(bits) > 1:
        lines[bits[0]], others = lax.optimization_barrier((lines[bits[0]], others))
    for bit in bits[1:]:
        for known in [m for m in lines if m >= 2 * bit and m & (2 * bit - 1) == 0]:
            lines[known | bit] = swap(lines[known], "ctx", bit * SPAN)
    for s in range(1, share):
        for m in range(2, lines_total):
            others[s, m] = swap(lines[m], "groups", s)
    shares = [lines[m] for m in range(lines_total)]
    shares += [others[s, m] for s in range(1, share) for m in range(lines_total)]

    far = swap(normed, "ctx", 2)
    near = swap(normed, "ctx", 1)
    both = swap(far, "ctx", 1)

    place = jnp.stack([line, group % share])
    part = part_call(place, shares, lines_total, share)
    part_far = swap(part, "ctx", 2)
    part_near = swap(part, "ctx", 1)
    projected = project_call(place, [normed, near, far, both], shares, lines_total, share)
    ctxs = attend_call(projected, (0, 1, 2, 3), rows)
    own, part_far = lax.optimization_barrier((ctxs[0], part_far))
    part_both = swap(part_far, "ctx", 1)
    back = {0: own} | {j: swap(ctxs[j], "ctx", j) for j in range(1, SPAN)}
    ctxs = [back[j] for j in range(SPAN)]
    resid, table = output_call(
        member.reshape(1), tokens, marks, [part, part_near, part_far, part_both], ctxs
    )

    table = table.reshape(EXPERTS, CAP, width)
    if parts_ff > 1:
        table = jnp.repeat(table, parts_ff, axis=0)
    outgoing = table.reshape(devices, local_experts * CAP, width)
    arrived = lax.all_to_all(outgoing, "ctx", split_axis=0, concat_axis=0, tiled=True)
    produced = expert_call(arrived.reshape(-1, width), w_in, w_out, local_experts, devices)
    produced = produced.reshape(devices, local_experts * CAP, width)
    returned = lax.all_to_all(produced, "ctx", split_axis=0, concat_axis=0, tiled=True)
    if parts_ff > 1:
        grouped = returned.reshape(EXPERTS, parts_ff, CAP, width)
        returned = jnp.sum(grouped.astype(f32), axis=1).astype(bf16)
    return combine_call(resid, returned.reshape(EXPERTS * CAP, width), gate_parts)


def solution(mesh):
    in_specs = (
        P(("groups", "ctx"), None),
        P(("groups", "ctx"), None),
        P(("groups", "ctx"), None),
        P("ctx", None),
        P("ctx", None),
        P(None, "ctx"),
        P("ctx", None),
    )
    out_specs = P(("groups", "ctx"), None)
    return jax.shard_map(
        per_device, mesh=mesh, in_specs=in_specs, out_specs=out_specs, check_vma=False
    )
```

```python
import functools
import math

import jax
import jax.numpy as jnp
from jax import lax
from jax.experimental import pallas as pl
from jax.experimental.pallas import tpu as pltpu
from jax.sharding import PartitionSpec as P

HEADS = 16
HD = 64
EXPERTS = 32
SPAN = 4
CAP = 20
TOP = 2
MIB = 1 << 20

eps = 1e-06
bf16 = jnp.bfloat16
f32 = jnp.float32


def params(mib=16):
    return pltpu.CompilerParams(vmem_limit_bytes=mib * MIB)


def cost(flops, nbytes, trans=0):
    return pl.CostEstimate(flops=int(flops), bytes_accessed=int(nbytes), transcendentals=int(trans))


def mm(a, b, dims=(((1,), (0,)), ((), ()))):
    return lax.dot_general(a, b, dims, preferred_element_type=f32)


def normalize(values):
    center = values - jnp.mean(values, axis=-1, keepdims=True)
    spread = jnp.mean(center * center, axis=-1, keepdims=True)
    return (center * lax.rsqrt(spread + eps)).astype(bf16)


def norm_kernel(x_ref, o_ref):
    o_ref[...] = normalize(x_ref[...].astype(f32))


def norm_call(tokens):
    return pl.pallas_call(
        norm_kernel,
        out_shape=jax.ShapeDtypeStruct(tokens.shape, bf16),
        compiler_params=params(),
        cost_estimate=cost(8 * tokens.size, 4 * tokens.size),
        name="norm_tokens",
    )(tokens)


def route_kernel(routes_ref, gates_ref, d_ref, hi_ref, mid_ref, lo_ref):
    rows = routes_ref.shape[1]
    slots = d_ref.shape[0]
    expert = lax.broadcasted_iota(jnp.int32, (EXPERTS, rows), 0)
    names = [expert == routes_ref[r : r + 1, :] for r in range(TOP)]
    counts = names[0]
    for other in names[1:]:
        counts = counts | other
    counts = jnp.where(counts, 1.0, 0.0).astype(bf16)
    earlier = lax.broadcasted_iota(jnp.int32, (rows, rows), 0) < lax.broadcasted_iota(
        jnp.int32, (rows, rows), 1
    )
    before = mm(counts, jnp.where(earlier, 1.0, 0.0).astype(bf16))
    place = lax.broadcasted_iota(jnp.int32, (slots, rows), 0)
    marks = jnp.zeros((slots, rows), f32)
    weights = jnp.zeros((slots, rows), f32)
    for r in range(TOP):
        position = jnp.sum(jnp.where(names[r], before, 0.0), axis=0, keepdims=True)
        slot = routes_ref[r : r + 1, :] * CAP + position.astype(jnp.int32)
        here = place == slot
        marks = jnp.where(here, 1.0, marks)
        weights = jnp.where(here, gates_ref[r : r + 1, :], weights)
    d_ref[...] = marks.astype(bf16)
    high = weights.astype(bf16)
    rest = weights - high.astype(f32)
    middle = rest.astype(bf16)
    hi_ref[...] = high
    mid_ref[...] = middle
    lo_ref[...] = (rest - middle.astype(f32)).astype(bf16)


def route_call(routes, gates):
    rows = routes.shape[0]
    shape = jax.ShapeDtypeStruct((EXPERTS * CAP, rows), bf16)
    return pl.pallas_call(
        route_kernel,
        out_shape=[shape] * 4,
        compiler_params=params(),
        cost_estimate=cost(20 * EXPERTS * CAP * rows, 8 * EXPERTS * CAP * rows),
        name="route_slots",
    )(routes.T, gates.T)


def part_kernel(line_ref, *refs):
    ws, o_ref = refs[:-1], refs[-1]
    size = ws[0].shape[0]
    for m, w_ref in enumerate(ws):
        o_ref[pl.ds(pl.multiple_of((line_ref[0] ^ m) * size, size), size), :] = w_ref[...]


def part_call(line, ws):
    size, cols = ws[0].shape
    vm = pl.BlockSpec(memory_space=pltpu.VMEM)
    return pl.pallas_call(
        part_kernel,
        out_shape=jax.ShapeDtypeStruct((len(ws) * size, cols), bf16),
        in_specs=[pl.BlockSpec(memory_space=pltpu.SMEM)] + [vm] * len(ws),
        out_specs=vm,
        compiler_params=params(),
        cost_estimate=cost(1, 4 * len(ws) * size * cols),
        name="out_weight_part",
    )(line, *ws)


def project_kernel(place_ref, *refs, count, lines, share):
    xs = refs[:count]
    ws = refs[count : count + lines * share]
    o_ref, full = refs[count + lines * share :]
    size, wide = ws[0].shape
    cols = wide // 3
    rows = xs[0].shape[0]
    mine = share * cols
    for s in range(share):
        for m in range(lines):
            start = pl.multiple_of((place_ref[0] ^ m) * size, size)
            full[place_ref[1] ^ s, pl.ds(start, size), :] = ws[s * lines + m][...]
    for s in range(share):
        for j in range(count):
            got = mm(xs[j][...], full[s]).astype(bf16)
            for t in range(3):
                o_ref[j * rows : (j + 1) * rows, t * mine + s * cols : t * mine + (s + 1) * cols] = got[
                    :, t * cols : (t + 1) * cols
                ]


def project_call(place, xs, ws, lines, share):
    rows, width = xs[0].shape
    count = len(xs)
    cols = ws[0].shape[1] // 3
    vm = pl.BlockSpec(memory_space=pltpu.VMEM)
    return pl.pallas_call(
        functools.partial(project_kernel, count=count, lines=lines, share=share),
        out_shape=jax.ShapeDtypeStruct((count * rows, 3 * share * cols), bf16),
        in_specs=[pl.BlockSpec(memory_space=pltpu.SMEM)] + [vm] * (count + lines * share),
        out_specs=vm,
        scratch_shapes=[pltpu.VMEM((share, width, 3 * cols), bf16)],
        compiler_params=params(),
        cost_estimate=cost(6 * count * rows * width * cols * share, 2 * width * (count * rows + 8 * cols * share)),
        name="project",
    )(place, *xs, *ws)


def attend_kernel(p_ref, *o_refs, blocks):
    cols = p_ref.shape[1] // 3
    rows = o_refs[0].shape[0]
    lane = lax.broadcasted_iota(jnp.int32, (rows, cols), 1) // HD
    keys = p_ref[:, cols : 2 * cols]
    values = p_ref[:, 2 * cols :]
    for o_ref, j in zip(o_refs, blocks):
        queries = p_ref[j * rows : (j + 1) * rows, :cols] * jnp.asarray(HD ** (-0.5), bf16)
        mixed = None
        for h in range(cols // HD):
            mine = lane == h
            q = jnp.where(mine, queries, jnp.zeros_like(queries))
            scores = mm(q, keys, (((1,), (1,)), ((), ())))
            weights = jnp.exp(scores - jnp.max(scores, axis=-1, keepdims=True))
            probs = (weights * (1.0 / jnp.sum(weights, axis=-1, keepdims=True))).astype(bf16)
            part = mm(probs, values)
            mixed = part if mixed is None else jnp.where(mine, part, mixed)
        o_ref[...] = mixed.astype(bf16)


def attend_call(projected, blocks, rows):
    length, width = projected.shape[0], projected.shape[1] // 3
    return pl.pallas_call(
        functools.partial(attend_kernel, blocks=blocks),
        out_shape=[jax.ShapeDtypeStruct((rows, width), bf16)] * len(blocks),
        compiler_params=params(),
        cost_estimate=cost(
            16 * len(blocks) * rows * length * width, 2 * projected.size, len(blocks) * rows * length * width // HD
        ),
        name="attend",
    )(projected)


def output_kernel(place_ref, t_ref, d_ref, *refs, share):
    ctxs, parts = refs[:SPAN], refs[SPAN : 2 * SPAN]
    r_ref, o_ref, c_ref, a_ref = refs[2 * SPAN :]
    wide = ctxs[0].shape[1]
    cols = wide // share
    starts = [pl.multiple_of((place_ref[0] ^ j) * wide, wide) for j in range(SPAN)]

    def natural(value):
        pieces = []
        for p in range(share):
            piece = value[:, :cols]
            for s in range(1, share):
                piece = jnp.where((place_ref[1] ^ s) == p, value[:, s * cols : (s + 1) * cols], piece)
            pieces.append(piece)
        return jnp.concatenate(pieces, axis=1) if share > 1 else value

    for j in range(SPAN):
        c_ref[:, pl.ds(starts[j], wide)] = ctxs[j][...]
    for j in range(SPAN):
        a_ref[:, pl.ds(starts[j], wide)] = natural(mm(c_ref[...], parts[j][...]))
    total = t_ref[...].astype(f32) + a_ref[...]
    r_ref[...] = total
    o_ref[...] = mm(d_ref[...], normalize(total)).astype(bf16)


def output_call(place, tokens, marks, parts, ctxs, share):
    rows, width = tokens.shape
    vm = pl.BlockSpec(memory_space=pltpu.VMEM)
    return pl.pallas_call(
        functools.partial(output_kernel, share=share),
        out_shape=[
            jax.ShapeDtypeStruct((rows, width), f32),
            jax.ShapeDtypeStruct((marks.shape[0], width), bf16),
        ],
        in_specs=[pl.BlockSpec(memory_space=pltpu.SMEM)] + [vm] * (2 + 2 * SPAN),
        out_specs=[vm, vm],
        scratch_shapes=[pltpu.VMEM((rows, width), bf16), pltpu.VMEM((rows, width), f32)],
        compiler_params=params(),
        cost_estimate=cost(2 * rows * width * (width + marks.shape[0]), 6 * width * width),
        name="out_projection",
    )(place, tokens, marks, *ctxs, *parts)


def gelu(x):
    return jax.nn.gelu(x, approximate=True)


def expert_kernel(x_ref, win_ref, wout_ref, o_ref, *scratch, local, sources, step):
    rows_ref, hid_ref, pre_ref, term_ref, out_buf, sems = scratch
    count = sources * CAP
    hidden = win_ref.shape[1] // local
    steps = hidden // step
    pack = 4 * CAP

    def load(e, n):
        span = pl.ds(e * hidden + n * step, step)
        return pltpu.make_async_copy(wout_ref.at[span, :], out_buf.at[span, :], sems.at[e, n])

    for n in range(steps):
        load(0, n).start()

    if local > 1:
        to = lax.broadcasted_iota(jnp.int32, (local * pack, local * pack), 0)
        have = lax.broadcasted_iota(jnp.int32, (local * pack, local * pack), 1)
        expert = to // pack
        inner = to - expert * pack
        source = inner // CAP
        wanted = source * (local * CAP) + expert * CAP + (inner - source * CAP)
        order = jnp.where(have == wanted, 1.0, 0.0).astype(bf16)
        for g in range(count // pack):
            part = mm(order, x_ref[g * local * pack : (g + 1) * local * pack, :]).astype(bf16)
            for e in range(local):
                rows_ref[e, g * pack : (g + 1) * pack, :] = part[e * pack : (e + 1) * pack, :]

    for e in range(local):
        for n in range(steps):
            start = e * hidden + n * step
            rows = rows_ref[e] if local > 1 else x_ref[...]
            pre_ref[n % 2] = mm(rows, win_ref[:, start : start + step])
            if n:
                hid_ref[:, (n - 1) * step : n * step] = gelu(pre_ref[(n - 1) % 2]).astype(bf16)
        hid_ref[:, (steps - 1) * step :] = gelu(pre_ref[(steps - 1) % 2]).astype(bf16)
        for n in range(steps):
            load(e, n).wait()
            if e + 1 < local:
                load(e + 1, n).start()
        term = mm(hid_ref[...], out_buf[e * hidden : (e + 1) * hidden, :]).astype(bf16)
        if local > 1:
            term_ref[e] = term
        else:
            o_ref[...] = term

    if local > 1:
        for g in range(count // pack):
            part = jnp.concatenate([term_ref[e, g * pack : (g + 1) * pack, :] for e in range(local)], axis=0)
            back = mm(order, part, (((0,), (0,)), ((), ())))
            o_ref[g * local * pack : (g + 1) * local * pack, :] = back.astype(bf16)


def expert_call(arrived, w_in, w_out, local, sources, step=1024):
    count = sources * CAP
    width = arrived.shape[1]
    hidden = w_in.shape[1] // local
    kept = (local, count, width) if local > 1 else (1, 16, 128)
    w_in = pltpu.with_memory_space_constraint(w_in, pltpu.VMEM)
    vm = pl.BlockSpec(memory_space=pltpu.VMEM)
    return pl.pallas_call(
        functools.partial(expert_kernel, local=local, sources=sources, step=step),
        out_shape=jax.ShapeDtypeStruct(arrived.shape, bf16),
        in_specs=[vm, vm, pl.BlockSpec(memory_space=pl.ANY)],
        out_specs=vm,
        scratch_shapes=[
            pltpu.VMEM(kept, bf16),
            pltpu.VMEM((count, hidden), bf16),
            pltpu.VMEM((2, count, step), f32),
            pltpu.VMEM(kept, bf16),
            pltpu.VMEM(w_out.shape, bf16),
            pltpu.SemaphoreType.DMA((local, hidden // step)),
        ],
        compiler_params=params(36),
        cost_estimate=cost(4 * count * width * hidden * local, 4 * width * hidden * local, count * hidden * local),
        name="experts",
    )(arrived, w_in, w_out)


def combine_kernel(r_ref, b_ref, hi_ref, mid_ref, lo_ref, o_ref):
    dims = (((0,), (0,)), ((), ()))
    back = b_ref[...]
    mixture = mm(lo_ref[...], back, dims)
    mixture = mixture + mm(mid_ref[...], back, dims)
    mixture = mixture + mm(hi_ref[...], back, dims)
    o_ref[...] = (r_ref[...] + mixture).astype(bf16)


def combine_call(resid, back, parts):
    return pl.pallas_call(
        combine_kernel,
        out_shape=jax.ShapeDtypeStruct(resid.shape, bf16),
        compiler_params=params(),
        cost_estimate=cost(6 * back.size * resid.shape[0], 6 * resid.size + 2 * back.size),
        name="combine",
    )(resid, back, *parts)


def swap(value, axis, bits):
    size = math.prod(lax.axis_size(name) for name in axis) if isinstance(axis, tuple) else lax.axis_size(axis)
    return lax.ppermute(value, axis, [(i, i ^ bits) for i in range(size)])


def per_device(tokens, routes, gates, qkv_weight, out_weight, w_in, w_out):
    rows, width = tokens.shape
    devices = lax.axis_size("ctx")
    groups = lax.axis_size("groups")
    lines_total = devices // SPAN
    me = lax.axis_index("ctx")
    member = me % SPAN
    line = me // SPAN
    group = lax.axis_index("groups")
    parts_ff = max(1, devices // EXPERTS)
    local_experts = max(1, EXPERTS // devices)

    mine = width // SPAN
    share = groups if (mine // HD) % groups == 0 else 1
    cols = mine // share
    offset = (group % share) * cols

    def columns(to):
        pieces = [
            lax.dynamic_slice_in_dim(qkv_weight, t * width + to * mine + offset, cols, 1)
            for t in range(3)
        ]
        pieces.append(lax.dynamic_slice_in_dim(out_weight, to * mine + offset, cols, 1))
        return jnp.concatenate(pieces, axis=1)

    pieces = [columns(member)] + [swap(columns(member ^ j), "ctx", j) for j in range(1, SPAN)]
    block = jnp.zeros((SPAN,) + pieces[0].shape, bf16)
    for j in range(SPAN):
        block = lax.dynamic_update_slice(block, pieces[j][None], (member ^ j, 0, 0))
    block = block.reshape(-1, 4 * cols)
    block, last = block[:, : 3 * cols], block[:, 3 * cols :]
    slots = route_call(routes, gates)
    normed, block, last, slots = lax.optimization_barrier((norm_call(tokens), block, last, slots))
    marks, *gate_parts = slots
    bits = [1 << i for i in reversed(range(lines_total.bit_length() - 1))]
    lines = {0: block}
    for bit in bits:
        lines[bit] = swap(block, "ctx", bit * SPAN)
    others = {}
    for s in range(1, share):
        for m in range(min(2, lines_total)):
            others[s, m] = swap(block, ("groups", "ctx"), s * devices + m * SPAN)
    if share > 1 and len(bits) > 1:
        lines[bits[0]], others = lax.optimization_barrier((lines[bits[0]], others))
    for bit in bits[1:]:
        for known in [m for m in lines if m >= 2 * bit and m & (2 * bit - 1) == 0]:
            lines[known | bit] = swap(lines[known], "ctx", bit * SPAN)
    for s in range(1, share):
        for m in bits[:-1]:
            others[s, m] = swap(lines[m], "groups", s)
    if share > 1 and len(bits) > 1:
        lines[lines_total - 1], others = lax.optimization_barrier((lines[lines_total - 1], others))
    for s in range(1, share):
        for m in range(lines_total):
            if (s, m) not in others:
                others[s, m] = swap(lines[m], "groups", s)
    shares = [lines[m] for m in range(lines_total)]
    shares += [others[s, m] for s in range(1, share) for m in range(lines_total)]

    far = swap(normed, "ctx", 2)
    near = swap(normed, "ctx", 1)
    both = swap(far, "ctx", 1)

    pieces = {0: last}
    for bit in bits:
        for known in list(pieces):
            pieces[known | bit] = swap(pieces[known], "ctx", bit * SPAN)
    part = part_call(line.reshape(1), [pieces[m] for m in range(lines_total)])
    part = jnp.concatenate([part] + [swap(part, "groups", s) for s in range(1, share)], axis=1)
    part_far = swap(part, "ctx", 2)
    part_near = swap(part, "ctx", 1)

    place = jnp.stack([line, group % share])
    projected = project_call(place, [normed, near, far, both], shares, lines_total, share)
    ctxs = attend_call(projected, (0, 1, 2, 3), rows)
    own, part_far = lax.optimization_barrier((ctxs[0], part_far))
    part_both = swap(part_far, "ctx", 1)
    back = {0: own} | {j: swap(ctxs[j], "ctx", j) for j in range(1, SPAN)}
    ctxs = [back[j] for j in range(SPAN)]
    resid, table = output_call(
        jnp.stack([member, group % share]), tokens, marks, [part, part_near, part_far, part_both], ctxs, share
    )

    table = table.reshape(EXPERTS, CAP, width)
    if parts_ff > 1:
        table = jnp.repeat(table, parts_ff, axis=0)
    outgoing = table.reshape(devices, local_experts * CAP, width)
    arrived = lax.all_to_all(outgoing, "ctx", split_axis=0, concat_axis=0, tiled=True)
    produced = expert_call(arrived.reshape(-1, width), w_in, w_out, local_experts, devices)
    produced = produced.reshape(devices, local_experts * CAP, width)
    returned = lax.all_to_all(produced, "ctx", split_axis=0, concat_axis=0, tiled=True)
    if parts_ff > 1:
        grouped = returned.reshape(EXPERTS, parts_ff, CAP, width)
        returned = jnp.sum(grouped.astype(f32), axis=1).astype(bf16)
    return combine_call(resid, returned.reshape(EXPERTS * CAP, width), gate_parts)


def solution(mesh):
    in_specs = (
        P(("groups", "ctx"), None),
        P(("groups", "ctx"), None),
        P(("groups", "ctx"), None),
        P("ctx", None),
        P("ctx", None),
        P(None, "ctx"),
        P("ctx", None),
    )
    out_specs = P(("groups", "ctx"), None)
    return jax.shard_map(
        per_device, mesh=mesh, in_specs=in_specs, out_specs=out_specs, check_vma=False
    )
```

```python
import functools
import math

import jax
import jax.numpy as jnp
from jax import lax
from jax.experimental import pallas as pl
from jax.experimental.pallas import tpu as pltpu
from jax.sharding import PartitionSpec as P

HEADS = 16
HD = 64
EXPERTS = 32
SPAN = 4
CAP = 20
TOP = 2
MIB = 1 << 20

eps = 1e-06
bf16 = jnp.bfloat16
f32 = jnp.float32


def params(mib=12):
    return pltpu.CompilerParams(vmem_limit_bytes=mib * MIB)


def cost(flops, nbytes, trans=0):
    return pl.CostEstimate(flops=int(flops), bytes_accessed=int(nbytes), transcendentals=int(trans))


def mm(a, b, dims=(((1,), (0,)), ((), ()))):
    return lax.dot_general(a, b, dims, preferred_element_type=f32)


def normalize(values):
    center = values - jnp.mean(values, axis=-1, keepdims=True)
    spread = jnp.mean(center * center, axis=-1, keepdims=True)
    return (center * lax.rsqrt(spread + eps)).astype(bf16)


def norm_kernel(x_ref, o_ref):
    o_ref[...] = normalize(x_ref[...].astype(f32))


def norm_call(tokens):
    return pl.pallas_call(
        norm_kernel,
        out_shape=jax.ShapeDtypeStruct(tokens.shape, bf16),
        compiler_params=params(),
        cost_estimate=cost(8 * tokens.size, 4 * tokens.size),
        name="norm_tokens",
    )(tokens)


def route_kernel(routes_ref, gates_ref, d_ref, hi_ref, mid_ref, lo_ref):
    rows = routes_ref.shape[1]
    slots = d_ref.shape[0]
    expert = lax.broadcasted_iota(jnp.int32, (EXPERTS, rows), 0)
    names = [expert == routes_ref[r : r + 1, :] for r in range(TOP)]
    counts = names[0]
    for other in names[1:]:
        counts = counts | other
    counts = jnp.where(counts, 1.0, 0.0).astype(bf16)
    earlier = lax.broadcasted_iota(jnp.int32, (rows, rows), 0) < lax.broadcasted_iota(
        jnp.int32, (rows, rows), 1
    )
    before = mm(counts, jnp.where(earlier, 1.0, 0.0).astype(bf16))
    place = lax.broadcasted_iota(jnp.int32, (slots, rows), 0)
    marks = jnp.zeros((slots, rows), f32)
    weights = jnp.zeros((slots, rows), f32)
    for r in range(TOP):
        position = jnp.sum(jnp.where(names[r], before, 0.0), axis=0, keepdims=True)
        slot = routes_ref[r : r + 1, :] * CAP + position.astype(jnp.int32)
        here = place == slot
        marks = jnp.where(here, 1.0, marks)
        weights = jnp.where(here, gates_ref[r : r + 1, :], weights)
    d_ref[...] = marks.astype(bf16)
    high = weights.astype(bf16)
    rest = weights - high.astype(f32)
    middle = rest.astype(bf16)
    hi_ref[...] = high
    mid_ref[...] = middle
    lo_ref[...] = (rest - middle.astype(f32)).astype(bf16)


def route_call(routes, gates):
    rows = routes.shape[0]
    shape = jax.ShapeDtypeStruct((EXPERTS * CAP, rows), bf16)
    return pl.pallas_call(
        route_kernel,
        out_shape=[shape] * 4,
        compiler_params=params(),
        cost_estimate=cost(20 * EXPERTS * CAP * rows, 8 * EXPERTS * CAP * rows),
        name="route_slots",
    )(routes.T, gates.T)


def part_kernel(line_ref, w_ref, o_ref, *, lines):
    size = w_ref.shape[0] // lines
    for m in range(lines):
        start = pl.multiple_of((line_ref[0] ^ m) * size, size)
        o_ref[pl.ds(start, size), :] = w_ref[m * size : (m + 1) * size, :]


def part_call(line, blocks, lines):
    vm = pl.BlockSpec(memory_space=pltpu.VMEM)
    return pl.pallas_call(
        functools.partial(part_kernel, lines=lines),
        out_shape=jax.ShapeDtypeStruct(blocks.shape, bf16),
        in_specs=[pl.BlockSpec(memory_space=pltpu.SMEM), vm],
        out_specs=vm,
        compiler_params=params(4),
        cost_estimate=cost(1, 4 * blocks.size),
        name="out_weight_part",
    )(line, blocks)


def project_kernel(place_ref, *refs, count, lines, share):
    xs = refs[:count]
    ws = refs[count : count + lines * share]
    o_ref, full = refs[count + lines * share :]
    size, wide = ws[0].shape
    cols = wide // 3
    rows = xs[0].shape[0]
    mine = share * cols
    for s in range(share):
        for m in range(lines):
            start = pl.multiple_of((place_ref[0] ^ m) * size, size)
            full[place_ref[1] ^ s, pl.ds(start, size), :] = ws[s * lines + m][...]
    for s in range(share):
        for j in range(count):
            got = mm(xs[j][...], full[s]).astype(bf16)
            for t in range(3):
                o_ref[j * rows : (j + 1) * rows, t * mine + s * cols : t * mine + (s + 1) * cols] = got[
                    :, t * cols : (t + 1) * cols
                ]


def project_call(place, xs, ws, lines, share):
    rows, width = xs[0].shape
    count = len(xs)
    cols = ws[0].shape[1] // 3
    vm = pl.BlockSpec(memory_space=pltpu.VMEM)
    return pl.pallas_call(
        functools.partial(project_kernel, count=count, lines=lines, share=share),
        out_shape=jax.ShapeDtypeStruct((count * rows, 3 * share * cols), bf16),
        in_specs=[pl.BlockSpec(memory_space=pltpu.SMEM)] + [vm] * (count + lines * share),
        out_specs=vm,
        scratch_shapes=[pltpu.VMEM((share, width, 3 * cols), bf16)],
        compiler_params=params(),
        cost_estimate=cost(6 * count * rows * width * cols * share, 2 * width * (count * rows + 8 * cols * share)),
        name="project",
    )(place, *xs, *ws)


def attend_kernel(p_ref, *o_refs, blocks):
    cols = p_ref.shape[1] // 3
    rows = o_refs[0].shape[0]
    lane = lax.broadcasted_iota(jnp.int32, (rows, cols), 1) // HD
    keys = p_ref[:, cols : 2 * cols]
    values = p_ref[:, 2 * cols :]
    for o_ref, j in zip(o_refs, blocks):
        queries = p_ref[j * rows : (j + 1) * rows, :cols] * jnp.asarray(HD ** (-0.5), bf16)
        mixed = None
        for h in range(cols // HD):
            mine = lane == h
            q = jnp.where(mine, queries, jnp.zeros_like(queries))
            scores = mm(q, keys, (((1,), (1,)), ((), ())))
            weights = jnp.exp(scores - jnp.max(scores, axis=-1, keepdims=True))
            probs = (weights * (1.0 / jnp.sum(weights, axis=-1, keepdims=True))).astype(bf16)
            part = mm(probs, values)
            mixed = part if mixed is None else jnp.where(mine, part, mixed)
        o_ref[...] = mixed.astype(bf16)


def attend_call(projected, blocks, rows):
    length, width = projected.shape[0], projected.shape[1] // 3
    return pl.pallas_call(
        functools.partial(attend_kernel, blocks=blocks),
        out_shape=[jax.ShapeDtypeStruct((rows, width), bf16)] * len(blocks),
        compiler_params=params(),
        cost_estimate=cost(
            16 * len(blocks) * rows * length * width, 2 * projected.size, len(blocks) * rows * length * width // HD
        ),
        name="attend",
    )(projected)


def output_kernel(place_ref, t_ref, d_ref, *refs, share):
    ctxs, parts = refs[:SPAN], refs[SPAN : 2 * SPAN]
    r_ref, o_ref, c_ref, a_ref = refs[2 * SPAN :]
    wide = ctxs[0].shape[1]
    cols = wide // share
    starts = [pl.multiple_of((place_ref[0] ^ j) * wide, wide) for j in range(SPAN)]

    def natural(value):
        pieces = []
        for p in range(share):
            piece = value[:, :cols]
            for s in range(1, share):
                piece = jnp.where((place_ref[1] ^ s) == p, value[:, s * cols : (s + 1) * cols], piece)
            pieces.append(piece)
        return jnp.concatenate(pieces, axis=1) if share > 1 else value

    for j in range(SPAN):
        c_ref[:, pl.ds(starts[j], wide)] = ctxs[j][...]
    for j in range(SPAN):
        a_ref[:, pl.ds(starts[j], wide)] = natural(mm(c_ref[...], parts[j][...]))
    total = t_ref[...].astype(f32) + a_ref[...]
    r_ref[...] = total
    o_ref[...] = mm(d_ref[...], normalize(total)).astype(bf16)


def output_call(place, tokens, marks, parts, ctxs, share):
    rows, width = tokens.shape
    vm = pl.BlockSpec(memory_space=pltpu.VMEM)
    return pl.pallas_call(
        functools.partial(output_kernel, share=share),
        out_shape=[
            jax.ShapeDtypeStruct((rows, width), f32),
            jax.ShapeDtypeStruct((marks.shape[0], width), bf16),
        ],
        in_specs=[pl.BlockSpec(memory_space=pltpu.SMEM)] + [vm] * (2 + 2 * SPAN),
        out_specs=[vm, vm],
        scratch_shapes=[pltpu.VMEM((rows, width), bf16), pltpu.VMEM((rows, width), f32)],
        compiler_params=params(),
        cost_estimate=cost(2 * rows * width * (width + marks.shape[0]), 6 * width * width),
        name="out_projection",
    )(place, tokens, marks, *ctxs, *parts)


def gelu(x):
    return jax.nn.gelu(x, approximate=True)


def expert_kernel(x_ref, win_ref, wout_ref, o_ref, *scratch, local, sources, step):
    rows_ref, hid_ref, pre_ref, term_ref, out_buf, sems = scratch
    count = sources * CAP
    hidden = win_ref.shape[1] // local
    steps = hidden // step
    pack = 4 * CAP

    def load(e, n):
        return pltpu.make_async_copy(
            wout_ref.at[pl.ds(e * hidden + n * step, step), :], out_buf.at[pl.ds(n * step, step), :], sems.at[n]
        )

    for n in range(steps):
        load(0, n).start()

    if local > 1:
        to = lax.broadcasted_iota(jnp.int32, (local * pack, local * pack), 0)
        have = lax.broadcasted_iota(jnp.int32, (local * pack, local * pack), 1)
        expert = to // pack
        inner = to - expert * pack
        source = inner // CAP
        wanted = source * (local * CAP) + expert * CAP + (inner - source * CAP)
        order = jnp.where(have == wanted, 1.0, 0.0).astype(bf16)
        for g in range(count // pack):
            part = mm(order, x_ref[g * local * pack : (g + 1) * local * pack, :]).astype(bf16)
            for e in range(local):
                rows_ref[e, g * pack : (g + 1) * pack, :] = part[e * pack : (e + 1) * pack, :]

    for e in range(local):
        for n in range(steps):
            start = e * hidden + n * step
            rows = rows_ref[e] if local > 1 else x_ref[...]
            pre_ref[n % 2] = mm(rows, win_ref[:, start : start + step])
            if n:
                hid_ref[:, (n - 1) * step : n * step] = gelu(pre_ref[(n - 1) % 2]).astype(bf16)
        hid_ref[:, (steps - 1) * step :] = gelu(pre_ref[(steps - 1) % 2]).astype(bf16)
        for n in range(steps):
            load(e, n).wait()
        term = mm(hid_ref[...], out_buf[...]).astype(bf16)
        if local > 1:
            term_ref[e] = term
        else:
            o_ref[...] = term
        if e + 1 < local:
            for n in range(steps):
                load(e + 1, n).start()

    if local > 1:
        for g in range(count // pack):
            part = jnp.concatenate([term_ref[e, g * pack : (g + 1) * pack, :] for e in range(local)], axis=0)
            back = mm(order, part, (((0,), (0,)), ((), ())))
            o_ref[g * local * pack : (g + 1) * local * pack, :] = back.astype(bf16)


def expert_call(arrived, w_in, w_out, local, sources, step=1024):
    count = sources * CAP
    width = arrived.shape[1]
    hidden = w_in.shape[1] // local
    kept = (local, count, width) if local > 1 else (1, 16, 128)
    w_in = pltpu.with_memory_space_constraint(w_in, pltpu.VMEM)
    vm = pl.BlockSpec(memory_space=pltpu.VMEM)
    return pl.pallas_call(
        functools.partial(expert_kernel, local=local, sources=sources, step=step),
        out_shape=jax.ShapeDtypeStruct(arrived.shape, bf16),
        in_specs=[vm, vm, pl.BlockSpec(memory_space=pl.ANY)],
        out_specs=vm,
        scratch_shapes=[
            pltpu.VMEM(kept, bf16),
            pltpu.VMEM((count, hidden), bf16),
            pltpu.VMEM((2, count, step), f32),
            pltpu.VMEM(kept, bf16),
            pltpu.VMEM((hidden, width), bf16),
            pltpu.SemaphoreType.DMA((hidden // step,)),
        ],
        compiler_params=params(26 if local > 1 else 40),
        cost_estimate=cost(4 * count * width * hidden * local, 4 * width * hidden * local, count * hidden * local),
        name="experts",
    )(arrived, w_in, w_out)


def combine_kernel(r_ref, b_ref, hi_ref, mid_ref, lo_ref, o_ref):
    dims = (((0,), (0,)), ((), ()))
    back = b_ref[...]
    mixture = mm(lo_ref[...], back, dims)
    mixture = mixture + mm(mid_ref[...], back, dims)
    mixture = mixture + mm(hi_ref[...], back, dims)
    o_ref[...] = (r_ref[...] + mixture).astype(bf16)


def combine_call(resid, back, parts):
    return pl.pallas_call(
        combine_kernel,
        out_shape=jax.ShapeDtypeStruct(resid.shape, bf16),
        compiler_params=params(),
        cost_estimate=cost(6 * back.size * resid.shape[0], 6 * resid.size + 2 * back.size),
        name="combine",
    )(resid, back, *parts)


def swap(value, axis, bits):
    size = math.prod(lax.axis_size(name) for name in axis) if isinstance(axis, tuple) else lax.axis_size(axis)
    return lax.ppermute(value, axis, [(i, i ^ bits) for i in range(size)])


def per_device(tokens, routes, gates, qkv_weight, out_weight, w_in, w_out):
    rows, width = tokens.shape
    devices = lax.axis_size("ctx")
    groups = lax.axis_size("groups")
    lines_total = devices // SPAN
    me = lax.axis_index("ctx")
    member = me % SPAN
    line = me // SPAN
    group = lax.axis_index("groups")
    parts_ff = max(1, devices // EXPERTS)
    local_experts = max(1, EXPERTS // devices)

    mine = width // SPAN
    share = groups if (mine // HD) % groups == 0 else 1
    cols = mine // share
    offset = (group % share) * cols

    def columns(to):
        pieces = [
            lax.dynamic_slice_in_dim(qkv_weight, t * width + to * mine + offset, cols, 1)
            for t in range(3)
        ]
        pieces.append(lax.dynamic_slice_in_dim(out_weight, to * mine + offset, cols, 1))
        return jnp.concatenate(pieces, axis=1)

    pieces = [columns(member)] + [swap(columns(member ^ j), "ctx", j) for j in range(1, SPAN)]
    block = jnp.zeros((SPAN,) + pieces[0].shape, bf16)
    for j in range(SPAN):
        block = lax.dynamic_update_slice(block, pieces[j][None], (member ^ j, 0, 0))
    block = block.reshape(-1, 4 * cols)
    block, last = block[:, : 3 * cols], block[:, 3 * cols :]
    slots = route_call(routes, gates)
    normed, block, last, slots = lax.optimization_barrier((norm_call(tokens), block, last, slots))
    marks, *gate_parts = slots
    bits = [1 << i for i in reversed(range(lines_total.bit_length() - 1))]
    lines = {0: block}
    for bit in bits:
        lines[bit] = swap(block, "ctx", bit * SPAN)
    others = {}
    for s in range(1, share):
        for m in range(min(2, lines_total)):
            others[s, m] = swap(block, ("groups", "ctx"), s * devices + m * SPAN)
    if share > 1 and len(bits) > 1:
        lines[bits[0]], others = lax.optimization_barrier((lines[bits[0]], others))
    for bit in bits[1:]:
        for known in [m for m in lines if m >= 2 * bit and m & (2 * bit - 1) == 0]:
            lines[known | bit] = swap(lines[known], "ctx", bit * SPAN)
    for s in range(1, share):
        for m in bits[:-1]:
            others[s, m] = swap(lines[m], "groups", s)
    if share > 1 and len(bits) > 1:
        lines[lines_total - 1], others = lax.optimization_barrier((lines[lines_total - 1], others))
    for s in range(1, share):
        for m in range(lines_total):
            if (s, m) not in others:
                others[s, m] = swap(lines[m], "groups", s)
    shares = [lines[m] for m in range(lines_total)]
    shares += [others[s, m] for s in range(1, share) for m in range(lines_total)]

    far = swap(normed, "ctx", 2)
    near = swap(normed, "ctx", 1)
    both = swap(far, "ctx", 1)

    for bit in reversed(bits):
        last = jnp.concatenate([last, swap(last, "ctx", bit * SPAN)], axis=0)
    part = part_call(line.reshape(1), last, lines_total)
    part = jnp.concatenate([part] + [swap(part, "groups", s) for s in range(1, share)], axis=1)
    part_far = swap(part, "ctx", 2)
    part_near = swap(part, "ctx", 1)

    place = jnp.stack([line, group % share])
    projected = project_call(place, [normed, near, far, both], shares, lines_total, share)
    ctxs = attend_call(projected, (0, 1, 2, 3), rows)
    own, part_far = lax.optimization_barrier((ctxs[0], part_far))
    part_both = swap(part_far, "ctx", 1)
    back = {0: own} | {j: swap(ctxs[j], "ctx", j) for j in range(1, SPAN)}
    ctxs = [back[j] for j in range(SPAN)]
    resid, table = output_call(
        jnp.stack([member, group % share]), tokens, marks, [part, part_near, part_far, part_both], ctxs, share
    )

    table = table.reshape(EXPERTS, CAP, width)
    if parts_ff > 1:
        table = jnp.repeat(table, parts_ff, axis=0)
    outgoing = table.reshape(devices, local_experts * CAP, width)
    arrived = lax.all_to_all(outgoing, "ctx", split_axis=0, concat_axis=0, tiled=True)
    produced = expert_call(arrived.reshape(-1, width), w_in, w_out, local_experts, devices)
    produced = produced.reshape(devices, local_experts * CAP, width)
    returned = lax.all_to_all(produced, "ctx", split_axis=0, concat_axis=0, tiled=True)
    if parts_ff > 1:
        grouped = returned.reshape(EXPERTS, parts_ff, CAP, width)
        returned = jnp.sum(grouped.astype(f32), axis=1).astype(bf16)
    return combine_call(resid, returned.reshape(EXPERTS * CAP, width), gate_parts)


def solution(mesh):
    in_specs = (
        P(("groups", "ctx"), None),
        P(("groups", "ctx"), None),
        P(("groups", "ctx"), None),
        P("ctx", None),
        P("ctx", None),
        P(None, "ctx"),
        P("ctx", None),
    )
    out_specs = P(("groups", "ctx"), None)
    return jax.shard_map(
        per_device, mesh=mesh, in_specs=in_specs, out_specs=out_specs, check_vma=False
    )
```

```python
import functools
import math

import jax
import jax.numpy as jnp
from jax import lax
from jax.experimental import pallas as pl
from jax.experimental.pallas import tpu as pltpu
from jax.sharding import PartitionSpec as P

HEADS = 16
HD = 64
EXPERTS = 32
SPAN = 4
CAP = 20
TOP = 2
MIB = 1 << 20

eps = 1e-06
bf16 = jnp.bfloat16
f32 = jnp.float32


def params(mib=12):
    return pltpu.CompilerParams(vmem_limit_bytes=mib * MIB)


def cost(flops, nbytes, trans=0):
    return pl.CostEstimate(flops=int(flops), bytes_accessed=int(nbytes), transcendentals=int(trans))


def mm(a, b, dims=(((1,), (0,)), ((), ()))):
    return lax.dot_general(a, b, dims, preferred_element_type=f32)


def normalize(values):
    center = values - jnp.mean(values, axis=-1, keepdims=True)
    spread = jnp.mean(center * center, axis=-1, keepdims=True)
    return (center * lax.rsqrt(spread + eps)).astype(bf16)


def norm_kernel(x_ref, o_ref):
    o_ref[...] = normalize(x_ref[...].astype(f32))


def norm_call(tokens):
    return pl.pallas_call(
        norm_kernel,
        out_shape=jax.ShapeDtypeStruct(tokens.shape, bf16),
        compiler_params=params(),
        cost_estimate=cost(8 * tokens.size, 4 * tokens.size),
        name="norm_tokens",
    )(tokens)


def route_kernel(routes_ref, gates_ref, d_ref, hi_ref, mid_ref, lo_ref):
    rows = routes_ref.shape[1]
    slots = d_ref.shape[0]
    expert = lax.broadcasted_iota(jnp.int32, (EXPERTS, rows), 0)
    names = [expert == routes_ref[r : r + 1, :] for r in range(TOP)]
    counts = names[0]
    for other in names[1:]:
        counts = counts | other
    counts = jnp.where(counts, 1.0, 0.0).astype(bf16)
    earlier = lax.broadcasted_iota(jnp.int32, (rows, rows), 0) < lax.broadcasted_iota(
        jnp.int32, (rows, rows), 1
    )
    before = mm(counts, jnp.where(earlier, 1.0, 0.0).astype(bf16))
    place = lax.broadcasted_iota(jnp.int32, (slots, rows), 0)
    marks = jnp.zeros((slots, rows), f32)
    weights = jnp.zeros((slots, rows), f32)
    for r in range(TOP):
        position = jnp.sum(jnp.where(names[r], before, 0.0), axis=0, keepdims=True)
        slot = routes_ref[r : r + 1, :] * CAP + position.astype(jnp.int32)
        here = place == slot
        marks = jnp.where(here, 1.0, marks)
        weights = jnp.where(here, gates_ref[r : r + 1, :], weights)
    d_ref[...] = marks.astype(bf16)
    weights = weights.T
    high = weights.astype(bf16)
    rest = weights - high.astype(f32)
    middle = rest.astype(bf16)
    hi_ref[...] = high
    mid_ref[...] = middle
    lo_ref[...] = (rest - middle.astype(f32)).astype(bf16)


def route_call(routes, gates):
    rows = routes.shape[0]
    marks = jax.ShapeDtypeStruct((EXPERTS * CAP, rows), bf16)
    gates_shape = jax.ShapeDtypeStruct((rows, EXPERTS * CAP), bf16)
    return pl.pallas_call(
        route_kernel,
        out_shape=[marks] + [gates_shape] * 3,
        compiler_params=params(),
        cost_estimate=cost(20 * EXPERTS * CAP * rows, 8 * EXPERTS * CAP * rows),
        name="route_slots",
    )(routes.T, gates.T)


def part_kernel(line_ref, w_ref, o_ref, *, lines):
    size = w_ref.shape[0] // lines
    for m in range(lines):
        start = pl.multiple_of((line_ref[0] ^ m) * size, size)
        o_ref[pl.ds(start, size), :] = w_ref[m * size : (m + 1) * size, :]


def part_call(line, blocks, lines):
    vm = pl.BlockSpec(memory_space=pltpu.VMEM)
    return pl.pallas_call(
        functools.partial(part_kernel, lines=lines),
        out_shape=jax.ShapeDtypeStruct(blocks.shape, bf16),
        in_specs=[pl.BlockSpec(memory_space=pltpu.SMEM), vm],
        out_specs=vm,
        compiler_params=params(4),
        cost_estimate=cost(1, 4 * blocks.size),
        name="out_weight_part",
    )(line, blocks)


def project_kernel(place_ref, *refs, count, lines, share):
    xs = refs[:count]
    ws = refs[count : count + lines * share]
    o_ref, x_ref, w_ref = refs[count + lines * share :]
    size, wide = ws[0].shape
    cols = wide // 3
    rows = xs[0].shape[0]
    mine = share * cols
    for s in range(share):
        for m in range(lines):
            start = pl.multiple_of((place_ref[0] ^ m) * size, size)
            w_ref[pl.ds(start, size), s * wide : (s + 1) * wide] = ws[s * lines + m][...]
    for j in range(count):
        x_ref[j * rows : (j + 1) * rows, :] = xs[j][...]
    got = mm(x_ref[...], w_ref[...]).astype(bf16)
    for t in range(3):
        for p in range(share):
            piece = got[:, t * cols : (t + 1) * cols]
            for s in range(1, share):
                other = got[:, s * wide + t * cols : s * wide + (t + 1) * cols]
                piece = jnp.where((place_ref[1] ^ s) == p, other, piece)
            o_ref[:, t * mine + p * cols : t * mine + (p + 1) * cols] = piece


def project_call(place, xs, ws, lines, share):
    rows, width = xs[0].shape
    count = len(xs)
    cols = ws[0].shape[1] // 3
    vm = pl.BlockSpec(memory_space=pltpu.VMEM)
    return pl.pallas_call(
        functools.partial(project_kernel, count=count, lines=lines, share=share),
        out_shape=jax.ShapeDtypeStruct((count * rows, 3 * share * cols), bf16),
        in_specs=[pl.BlockSpec(memory_space=pltpu.SMEM)] + [vm] * (count + lines * share),
        out_specs=vm,
        scratch_shapes=[
            pltpu.VMEM((count * rows, width), bf16),
            pltpu.VMEM((width, share * 3 * cols), bf16),
        ],
        compiler_params=params(),
        cost_estimate=cost(6 * count * rows * width * cols * share, 2 * width * (count * rows + 8 * cols * share)),
        name="project",
    )(place, *xs, *ws)


def attend_kernel(p_ref, *o_refs, tile):
    cols = p_ref.shape[1] // 3
    rows = o_refs[0].shape[0]
    lane = lax.broadcasted_iota(jnp.int32, (tile * rows, cols), 1) // HD
    keys = p_ref[:, cols : 2 * cols]
    values = p_ref[:, 2 * cols :]
    for i in range(0, len(o_refs), tile):
        queries = p_ref[i * rows : (i + tile) * rows, :cols] * jnp.asarray(HD ** (-0.5), bf16)
        mixed = None
        for h in range(cols // HD):
            mine = lane == h
            q = jnp.where(mine, queries, jnp.zeros_like(queries))
            scores = mm(q, keys, (((1,), (1,)), ((), ())))
            weights = jnp.exp(scores - jnp.max(scores, axis=-1, keepdims=True))
            probs = (weights * (1.0 / jnp.sum(weights, axis=-1, keepdims=True))).astype(bf16)
            part = mm(probs, values)
            mixed = part if mixed is None else jnp.where(mine, part, mixed)
        mixed = mixed.astype(bf16)
        for k in range(tile):
            o_refs[i + k][...] = mixed[k * rows : (k + 1) * rows]


def attend_call(projected, blocks, rows):
    length, width = projected.shape[0], projected.shape[1] // 3
    return pl.pallas_call(
        functools.partial(attend_kernel, tile=1),
        out_shape=[jax.ShapeDtypeStruct((rows, width), bf16)] * len(blocks),
        compiler_params=params(),
        cost_estimate=cost(
            16 * len(blocks) * rows * length * width, 2 * projected.size, len(blocks) * rows * length * width // HD
        ),
        name="attend",
    )(projected)


def output_kernel(place_ref, t_ref, d_ref, *refs, share):
    ctxs, parts = refs[:SPAN], refs[SPAN : 2 * SPAN]
    r_ref, o_ref, c_ref, a_ref = refs[2 * SPAN :]
    wide = ctxs[0].shape[1]
    cols = wide // share
    starts = [pl.multiple_of((place_ref[0] ^ j) * wide, wide) for j in range(SPAN)]

    def natural(value):
        pieces = []
        for p in range(share):
            piece = value[:, :cols]
            for s in range(1, share):
                piece = jnp.where((place_ref[1] ^ s) == p, value[:, s * cols : (s + 1) * cols], piece)
            pieces.append(piece)
        return jnp.concatenate(pieces, axis=1) if share > 1 else value

    for j in range(SPAN):
        c_ref[:, pl.ds(starts[j], wide)] = ctxs[j][...]
    for j in range(SPAN):
        a_ref[:, pl.ds(starts[j], wide)] = natural(mm(c_ref[...], parts[j][...]))
    total = t_ref[...].astype(f32) + a_ref[...]
    r_ref[...] = total
    o_ref[...] = mm(d_ref[...], normalize(total)).astype(bf16)


def output_call(place, tokens, marks, parts, ctxs, share):
    rows, width = tokens.shape
    vm = pl.BlockSpec(memory_space=pltpu.VMEM)
    return pl.pallas_call(
        functools.partial(output_kernel, share=share),
        out_shape=[
            jax.ShapeDtypeStruct((rows, width), f32),
            jax.ShapeDtypeStruct((marks.shape[0], width), bf16),
        ],
        in_specs=[pl.BlockSpec(memory_space=pltpu.SMEM)] + [vm] * (2 + 2 * SPAN),
        out_specs=[vm, vm],
        scratch_shapes=[pltpu.VMEM((rows, width), bf16), pltpu.VMEM((rows, width), f32)],
        compiler_params=params(),
        cost_estimate=cost(80 * rows * width * (width + marks.shape[0]), 6 * width * width),
        name="out_projection",
    )(place, tokens, marks, *ctxs, *parts)


def gelu(x):
    return jax.nn.gelu(x, approximate=True)


def expert_kernel(x_ref, win_ref, wout_ref, o_ref, *scratch, local, sources, step):
    rows_ref, hid_ref, pre_ref, term_ref, out_buf, sems = scratch
    count = sources * CAP
    hidden = win_ref.shape[1] // local
    steps = hidden // step
    pack = 4 * CAP

    def load(e, n):
        return pltpu.make_async_copy(
            wout_ref.at[pl.ds(e * hidden + n * step, step), :], out_buf.at[pl.ds(n * step, step), :], sems.at[n]
        )

    for n in range(steps):
        load(0, n).start()

    if local > 1:
        to = lax.broadcasted_iota(jnp.int32, (local * pack, local * pack), 0)
        have = lax.broadcasted_iota(jnp.int32, (local * pack, local * pack), 1)
        expert = to // pack
        inner = to - expert * pack
        source = inner // CAP
        wanted = source * (local * CAP) + expert * CAP + (inner - source * CAP)
        order = jnp.where(have == wanted, 1.0, 0.0).astype(bf16)
        for g in range(count // pack):
            part = mm(order, x_ref[g * local * pack : (g + 1) * local * pack, :]).astype(bf16)
            for e in range(local):
                rows_ref[e, g * pack : (g + 1) * pack, :] = part[e * pack : (e + 1) * pack, :]

    for e in range(local):
        for n in range(steps):
            start = e * hidden + n * step
            rows = rows_ref[e] if local > 1 else x_ref[...]
            pre_ref[n % 2] = mm(rows, win_ref[:, start : start + step])
            if n:
                hid_ref[:, (n - 1) * step : n * step] = gelu(pre_ref[(n - 1) % 2]).astype(bf16)
        hid_ref[:, (steps - 1) * step :] = gelu(pre_ref[(steps - 1) % 2]).astype(bf16)
        for n in range(steps):
            load(e, n).wait()
        term = mm(hid_ref[...], out_buf[...]).astype(bf16)
        if local > 1:
            term_ref[e] = term
        else:
            o_ref[...] = term
        if e + 1 < local:
            for n in range(steps):
                load(e + 1, n).start()

    if local > 1:
        for g in range(count // pack):
            part = jnp.concatenate([term_ref[e, g * pack : (g + 1) * pack, :] for e in range(local)], axis=0)
            back = mm(order, part, (((0,), (0,)), ((), ())))
            o_ref[g * local * pack : (g + 1) * local * pack, :] = back.astype(bf16)


def expert_call(arrived, w_in, w_out, local, sources, step=1024):
    count = sources * CAP
    width = arrived.shape[1]
    hidden = w_in.shape[1] // local
    kept = (local, count, width) if local > 1 else (1, 16, 128)
    w_in = pltpu.with_memory_space_constraint(w_in, pltpu.VMEM)
    vm = pl.BlockSpec(memory_space=pltpu.VMEM)
    return pl.pallas_call(
        functools.partial(expert_kernel, local=local, sources=sources, step=step),
        out_shape=jax.ShapeDtypeStruct(arrived.shape, bf16),
        in_specs=[vm, vm, pl.BlockSpec(memory_space=pl.ANY)],
        out_specs=vm,
        scratch_shapes=[
            pltpu.VMEM(kept, bf16),
            pltpu.VMEM((count, hidden), bf16),
            pltpu.VMEM((2, count, step), f32),
            pltpu.VMEM(kept, bf16),
            pltpu.VMEM((hidden, width), bf16),
            pltpu.SemaphoreType.DMA((hidden // step,)),
        ],
        compiler_params=params(26 if local > 1 else 40),
        cost_estimate=cost(4 * count * width * hidden * local, 4 * width * hidden * local, count * hidden * local),
        name="experts",
    )(arrived, w_in, w_out)


def combine_kernel(r_ref, b_ref, hi_ref, mid_ref, lo_ref, o_ref):
    back = b_ref[...]
    mixture = mm(lo_ref[...], back)
    mixture = mixture + mm(mid_ref[...], back)
    mixture = mixture + mm(hi_ref[...], back)
    o_ref[...] = (r_ref[...] + mixture).astype(bf16)


def combine_call(resid, back, parts):
    return pl.pallas_call(
        combine_kernel,
        out_shape=jax.ShapeDtypeStruct(resid.shape, bf16),
        compiler_params=params(),
        cost_estimate=cost(6 * back.size * resid.shape[0], 6 * resid.size + 2 * back.size),
        name="combine",
    )(resid, back, *parts)


def swap(value, axis, bits):
    size = math.prod(lax.axis_size(name) for name in axis) if isinstance(axis, tuple) else lax.axis_size(axis)
    return lax.ppermute(value, axis, [(i, i ^ bits) for i in range(size)])


def per_device(tokens, routes, gates, qkv_weight, out_weight, w_in, w_out):
    rows, width = tokens.shape
    devices = lax.axis_size("ctx")
    groups = lax.axis_size("groups")
    lines_total = devices // SPAN
    me = lax.axis_index("ctx")
    member = me % SPAN
    line = me // SPAN
    group = lax.axis_index("groups")
    parts_ff = max(1, devices // EXPERTS)
    local_experts = max(1, EXPERTS // devices)

    mine = width // SPAN
    share = groups if (mine // HD) % groups == 0 else 1
    cols = mine // share
    offset = (group % share) * cols

    def columns(to):
        pieces = [
            lax.dynamic_slice_in_dim(qkv_weight, t * width + to * mine + offset, cols, 1)
            for t in range(3)
        ]
        pieces.append(lax.dynamic_slice_in_dim(out_weight, to * mine + offset, cols, 1))
        return jnp.concatenate(pieces, axis=1)

    pieces = [columns(member)] + [swap(columns(member ^ j), "ctx", j) for j in range(1, SPAN)]
    block = jnp.zeros((SPAN,) + pieces[0].shape, bf16)
    for j in range(SPAN):
        block = lax.dynamic_update_slice(block, pieces[j][None], (member ^ j, 0, 0))
    block = block.reshape(-1, 4 * cols)
    block, last = block[:, : 3 * cols], block[:, 3 * cols :]
    slots = route_call(routes, gates)
    normed, block, last, slots = lax.optimization_barrier((norm_call(tokens), block, last, slots))
    marks, *gate_parts = slots
    bits = [1 << i for i in reversed(range(lines_total.bit_length() - 1))]
    lines = {0: block}
    for bit in bits:
        lines[bit] = swap(block, "ctx", bit * SPAN)
    others = {}
    for s in range(1, share):
        for m in range(min(2, lines_total)):
            others[s, m] = swap(block, ("groups", "ctx"), s * devices + m * SPAN)
    if share > 1 and len(bits) > 1:
        lines[bits[0]], others = lax.optimization_barrier((lines[bits[0]], others))
    for bit in bits[1:]:
        for known in [m for m in lines if m >= 2 * bit and m & (2 * bit - 1) == 0]:
            lines[known | bit] = swap(lines[known], "ctx", bit * SPAN)
    for s in range(1, share):
        for m in bits[:-1]:
            others[s, m] = swap(lines[m], "groups", s)
    if share > 1 and len(bits) > 1:
        lines[lines_total - 1], others = lax.optimization_barrier((lines[lines_total - 1], others))
    for s in range(1, share):
        for m in range(lines_total):
            if (s, m) not in others:
                others[s, m] = swap(lines[m], "groups", s)
    shares = [lines[m] for m in range(lines_total)]
    shares += [others[s, m] for s in range(1, share) for m in range(lines_total)]

    far = swap(normed, "ctx", 2)
    near = swap(normed, "ctx", 1)
    both = swap(far, "ctx", 1)

    for bit in reversed(bits):
        last = jnp.concatenate([last, swap(last, "ctx", bit * SPAN)], axis=0)
    part = part_call(line.reshape(1), last, lines_total)
    part = jnp.concatenate([part] + [swap(part, "groups", s) for s in range(1, share)], axis=1)
    part_far = swap(part, "ctx", 2)
    part_near = swap(part, "ctx", 1)

    place = jnp.stack([line, group % share])
    projected = project_call(place, [normed, near, far, both], shares, lines_total, share)
    ctxs = attend_call(projected, (0, 1, 2, 3), rows)
    own, part_far = lax.optimization_barrier((ctxs[0], part_far))
    part_both = swap(part_far, "ctx", 1)
    back = {0: own} | {j: swap(ctxs[j], "ctx", j) for j in range(1, SPAN)}
    ctxs = [back[j] for j in range(SPAN)]
    resid, table = output_call(
        jnp.stack([member, group % share]), tokens, marks, [part, part_near, part_far, part_both], ctxs, share
    )

    table = table.reshape(EXPERTS, CAP, width)
    if parts_ff > 1:
        table = jnp.repeat(table, parts_ff, axis=0)
    outgoing = table.reshape(devices, local_experts * CAP, width)
    arrived = lax.all_to_all(outgoing, "ctx", split_axis=0, concat_axis=0, tiled=True)
    produced = expert_call(arrived.reshape(-1, width), w_in, w_out, local_experts, devices)
    produced = produced.reshape(devices, local_experts * CAP, width)
    returned = lax.all_to_all(produced, "ctx", split_axis=0, concat_axis=0, tiled=True)
    if parts_ff > 1:
        grouped = returned.reshape(EXPERTS, parts_ff, CAP, width)
        returned = jnp.sum(grouped.astype(f32), axis=1).astype(bf16)
    return combine_call(resid, returned.reshape(EXPERTS * CAP, width), gate_parts)


def solution(mesh):
    in_specs = (
        P(("groups", "ctx"), None),
        P(("groups", "ctx"), None),
        P(("groups", "ctx"), None),
        P("ctx", None),
        P("ctx", None),
        P(None, "ctx"),
        P("ctx", None),
    )
    out_specs = P(("groups", "ctx"), None)
    return jax.shard_map(
        per_device, mesh=mesh, in_specs=in_specs, out_specs=out_specs, check_vma=False
    )
```

```python
import functools
import math

import jax
import jax.numpy as jnp
from jax import lax
from jax.experimental import pallas as pl
from jax.experimental.pallas import tpu as pltpu
from jax.sharding import PartitionSpec as P

HEADS = 16
HD = 64
EXPERTS = 32
SPAN = 4
CAP = 20
TOP = 2
MIB = 1 << 20

eps = 1e-06
bf16 = jnp.bfloat16
f32 = jnp.float32


def params(mib=12):
    return pltpu.CompilerParams(vmem_limit_bytes=mib * MIB)


def cost(flops, nbytes, trans=0):
    return pl.CostEstimate(flops=int(flops), bytes_accessed=int(nbytes), transcendentals=int(trans))


def mm(a, b, dims=(((1,), (0,)), ((), ()))):
    return lax.dot_general(a, b, dims, preferred_element_type=f32)


def normalize(values):
    center = values - jnp.mean(values, axis=-1, keepdims=True)
    spread = jnp.mean(center * center, axis=-1, keepdims=True)
    return (center * lax.rsqrt(spread + eps)).astype(bf16)


def norm_kernel(x_ref, o_ref):
    o_ref[...] = normalize(x_ref[...].astype(f32))


def norm_call(tokens):
    return pl.pallas_call(
        norm_kernel,
        out_shape=jax.ShapeDtypeStruct(tokens.shape, bf16),
        compiler_params=params(),
        cost_estimate=cost(8 * tokens.size, 4 * tokens.size),
        name="norm_tokens",
    )(tokens)


def route_kernel(routes_ref, gates_ref, d_ref, g_ref):
    rows = routes_ref.shape[1]
    slots = d_ref.shape[0]
    expert = lax.broadcasted_iota(jnp.int32, (EXPERTS, rows), 0)
    names = [expert == routes_ref[r : r + 1, :] for r in range(TOP)]
    counts = names[0]
    for other in names[1:]:
        counts = counts | other
    counts = jnp.where(counts, 1.0, 0.0).astype(bf16)
    earlier = lax.broadcasted_iota(jnp.int32, (rows, rows), 0) < lax.broadcasted_iota(
        jnp.int32, (rows, rows), 1
    )
    before = mm(counts, jnp.where(earlier, 1.0, 0.0).astype(bf16))
    place = lax.broadcasted_iota(jnp.int32, (slots, rows), 0)
    marks = jnp.zeros((slots, rows), f32)
    weights = jnp.zeros((slots, rows), f32)
    for r in range(TOP):
        position = jnp.sum(jnp.where(names[r], before, 0.0), axis=0, keepdims=True)
        slot = routes_ref[r : r + 1, :] * CAP + position.astype(jnp.int32)
        here = place == slot
        marks = jnp.where(here, 1.0, marks)
        weights = jnp.where(here, gates_ref[r : r + 1, :], weights)
    d_ref[...] = marks.astype(bf16)
    weights = weights.T
    high = weights.astype(bf16)
    rest = weights - high.astype(f32)
    middle = rest.astype(bf16)
    g_ref[:rows, :] = (rest - middle.astype(f32)).astype(bf16)
    g_ref[rows : 2 * rows, :] = middle
    g_ref[2 * rows :, :] = high


def route_call(routes, gates):
    rows = routes.shape[0]
    marks = jax.ShapeDtypeStruct((EXPERTS * CAP, rows), bf16)
    parts = jax.ShapeDtypeStruct((3 * rows, EXPERTS * CAP), bf16)
    return pl.pallas_call(
        route_kernel,
        out_shape=[marks, parts],
        compiler_params=params(),
        cost_estimate=cost(20 * EXPERTS * CAP * rows, 8 * EXPERTS * CAP * rows),
        name="route_slots",
    )(routes.T, gates.T)


def part_kernel(line_ref, w_ref, o_ref, *, lines):
    size = w_ref.shape[0] // lines
    for m in range(lines):
        start = pl.multiple_of((line_ref[0] ^ m) * size, size)
        o_ref[pl.ds(start, size), :] = w_ref[m * size : (m + 1) * size, :]


def part_call(line, blocks, lines):
    vm = pl.BlockSpec(memory_space=pltpu.VMEM)
    return pl.pallas_call(
        functools.partial(part_kernel, lines=lines),
        out_shape=jax.ShapeDtypeStruct(blocks.shape, bf16),
        in_specs=[pl.BlockSpec(memory_space=pltpu.SMEM), vm],
        out_specs=vm,
        compiler_params=params(4),
        cost_estimate=cost(1, 4 * blocks.size),
        name="out_weight_part",
    )(line, blocks)


def project_kernel(place_ref, *refs, count, lines, share):
    xs = refs[:count]
    ws = refs[count : count + lines * share]
    o_ref, x_ref, w_ref = refs[count + lines * share :]
    size, wide = ws[0].shape
    cols = wide // 3
    rows = xs[0].shape[0]
    mine = share * cols
    for s in range(share):
        for m in range(lines):
            start = pl.multiple_of((place_ref[0] ^ m) * size, size)
            w_ref[pl.ds(start, size), s * wide : (s + 1) * wide] = ws[s * lines + m][...]
    for j in range(count):
        x_ref[j * rows : (j + 1) * rows, :] = xs[j][...]
    got = mm(x_ref[...], w_ref[...]).astype(bf16)
    for t in range(3):
        for p in range(share):
            piece = got[:, t * cols : (t + 1) * cols]
            for s in range(1, share):
                other = got[:, s * wide + t * cols : s * wide + (t + 1) * cols]
                piece = jnp.where((place_ref[1] ^ s) == p, other, piece)
            o_ref[:, t * mine + p * cols : t * mine + (p + 1) * cols] = piece


def project_call(place, xs, ws, lines, share):
    rows, width = xs[0].shape
    count = len(xs)
    cols = ws[0].shape[1] // 3
    vm = pl.BlockSpec(memory_space=pltpu.VMEM)
    return pl.pallas_call(
        functools.partial(project_kernel, count=count, lines=lines, share=share),
        out_shape=jax.ShapeDtypeStruct((count * rows, 3 * share * cols), bf16),
        in_specs=[pl.BlockSpec(memory_space=pltpu.SMEM)] + [vm] * (count + lines * share),
        out_specs=vm,
        scratch_shapes=[
            pltpu.VMEM((count * rows, width), bf16),
            pltpu.VMEM((width, share * 3 * cols), bf16),
        ],
        compiler_params=params(),
        cost_estimate=cost(6 * count * rows * width * cols * share, 2 * width * (count * rows + 8 * cols * share)),
        name="project",
    )(place, *xs, *ws)


def attend_kernel(p_ref, *o_refs, tile):
    cols = p_ref.shape[1] // 3
    rows = o_refs[0].shape[0]
    lane = lax.broadcasted_iota(jnp.int32, (tile * rows, cols), 1) // HD
    keys = p_ref[:, cols : 2 * cols]
    values = p_ref[:, 2 * cols :]
    for i in range(0, len(o_refs), tile):
        queries = p_ref[i * rows : (i + tile) * rows, :cols] * jnp.asarray(HD ** (-0.5), bf16)
        mixed = None
        for h in range(cols // HD):
            mine = lane == h
            q = jnp.where(mine, queries, jnp.zeros_like(queries))
            scores = mm(q, keys, (((1,), (1,)), ((), ())))
            weights = jnp.exp(scores - jnp.max(scores, axis=-1, keepdims=True))
            probs = (weights * (1.0 / jnp.sum(weights, axis=-1, keepdims=True))).astype(bf16)
            part = mm(probs, values)
            mixed = part if mixed is None else jnp.where(mine, part, mixed)
        mixed = mixed.astype(bf16)
        for k in range(tile):
            o_refs[i + k][...] = mixed[k * rows : (k + 1) * rows]


def attend_call(projected, blocks, rows):
    length, width = projected.shape[0], projected.shape[1] // 3
    return pl.pallas_call(
        functools.partial(attend_kernel, tile=1),
        out_shape=[jax.ShapeDtypeStruct((rows, width), bf16)] * len(blocks),
        compiler_params=params(),
        cost_estimate=cost(
            16 * len(blocks) * rows * length * width, 2 * projected.size, len(blocks) * rows * length * width // HD
        ),
        name="attend",
    )(projected)


def output_kernel(place_ref, t_ref, d_ref, *refs, share):
    ctxs, parts = refs[:SPAN], refs[SPAN : 2 * SPAN]
    r_ref, o_ref, c_ref, a_ref = refs[2 * SPAN :]
    wide = ctxs[0].shape[1]
    cols = wide // share
    starts = [pl.multiple_of((place_ref[0] ^ j) * wide, wide) for j in range(SPAN)]

    def natural(value):
        pieces = []
        for p in range(share):
            piece = value[:, :cols]
            for s in range(1, share):
                piece = jnp.where((place_ref[1] ^ s) == p, value[:, s * cols : (s + 1) * cols], piece)
            pieces.append(piece)
        return jnp.concatenate(pieces, axis=1) if share > 1 else value

    for j in range(SPAN):
        c_ref[:, pl.ds(starts[j], wide)] = ctxs[j][...]
    for j in range(SPAN):
        a_ref[:, pl.ds(starts[j], wide)] = natural(mm(c_ref[...], parts[j][...]))
    total = t_ref[...].astype(f32) + a_ref[...]
    r_ref[...] = total
    o_ref[...] = mm(d_ref[...], normalize(total)).astype(bf16)


def output_call(place, tokens, marks, parts, ctxs, share):
    rows, width = tokens.shape
    vm = pl.BlockSpec(memory_space=pltpu.VMEM)
    return pl.pallas_call(
        functools.partial(output_kernel, share=share),
        out_shape=[
            jax.ShapeDtypeStruct((rows, width), f32),
            jax.ShapeDtypeStruct((marks.shape[0], width), bf16),
        ],
        in_specs=[pl.BlockSpec(memory_space=pltpu.SMEM)] + [vm] * (2 + 2 * SPAN),
        out_specs=[vm, vm],
        scratch_shapes=[pltpu.VMEM((rows, width), bf16), pltpu.VMEM((rows, width), f32)],
        compiler_params=params(),
        cost_estimate=cost(160 * rows * width * (width + marks.shape[0]), 6 * width * width),
        name="out_projection",
    )(place, tokens, marks, *ctxs, *parts)


def gelu(x):
    return jax.nn.gelu(x, approximate=True)


def expert_kernel(x_ref, win_ref, wout_ref, o_ref, *scratch, local, sources, step):
    rows_ref, hid_ref, pre_ref, term_ref, out_buf, sems = scratch
    count = sources * CAP
    hidden = win_ref.shape[1] // local
    steps = hidden // step
    pack = 4 * CAP

    def load(e, n):
        return pltpu.make_async_copy(
            wout_ref.at[pl.ds(e * hidden + n * step, step), :], out_buf.at[pl.ds(n * step, step), :], sems.at[n]
        )

    for n in range(steps):
        load(0, n).start()

    if local > 1:
        to = lax.broadcasted_iota(jnp.int32, (local * pack, local * pack), 0)
        have = lax.broadcasted_iota(jnp.int32, (local * pack, local * pack), 1)
        expert = to // pack
        inner = to - expert * pack
        source = inner // CAP
        wanted = source * (local * CAP) + expert * CAP + (inner - source * CAP)
        order = jnp.where(have == wanted, 1.0, 0.0).astype(bf16)
        for g in range(count // pack):
            part = mm(order, x_ref[g * local * pack : (g + 1) * local * pack, :]).astype(bf16)
            for e in range(local):
                rows_ref[e, g * pack : (g + 1) * pack, :] = part[e * pack : (e + 1) * pack, :]

    for e in range(local):
        for n in range(steps):
            start = e * hidden + n * step
            rows = rows_ref[e] if local > 1 else x_ref[...]
            pre_ref[n % 2] = mm(rows, win_ref[:, start : start + step])
            if n:
                hid_ref[:, (n - 1) * step : n * step] = gelu(pre_ref[(n - 1) % 2]).astype(bf16)
        hid_ref[:, (steps - 1) * step :] = gelu(pre_ref[(steps - 1) % 2]).astype(bf16)
        for n in range(steps):
            load(e, n).wait()
        term = mm(hid_ref[...], out_buf[...]).astype(bf16)
        if local > 1:
            term_ref[e] = term
        else:
            o_ref[...] = term
        if e + 1 < local:
            for n in range(steps):
                load(e + 1, n).start()

    if local > 1:
        for g in range(count // pack):
            part = jnp.concatenate([term_ref[e, g * pack : (g + 1) * pack, :] for e in range(local)], axis=0)
            back = mm(order, part, (((0,), (0,)), ((), ())))
            o_ref[g * local * pack : (g + 1) * local * pack, :] = back.astype(bf16)


def expert_call(arrived, w_in, w_out, local, sources, step=1024):
    count = sources * CAP
    width = arrived.shape[1]
    hidden = w_in.shape[1] // local
    kept = (local, count, width) if local > 1 else (1, 16, 128)
    w_in = pltpu.with_memory_space_constraint(w_in, pltpu.VMEM)
    vm = pl.BlockSpec(memory_space=pltpu.VMEM)
    return pl.pallas_call(
        functools.partial(expert_kernel, local=local, sources=sources, step=step),
        out_shape=jax.ShapeDtypeStruct(arrived.shape, bf16),
        in_specs=[vm, vm, pl.BlockSpec(memory_space=pl.ANY)],
        out_specs=vm,
        scratch_shapes=[
            pltpu.VMEM(kept, bf16),
            pltpu.VMEM((count, hidden), bf16),
            pltpu.VMEM((2, count, step), f32),
            pltpu.VMEM(kept, bf16),
            pltpu.VMEM((hidden, width), bf16),
            pltpu.SemaphoreType.DMA((hidden // step,)),
        ],
        compiler_params=params(26 if local > 1 else 40),
        cost_estimate=cost(4 * count * width * hidden * local, 4 * width * hidden * local, count * hidden * local),
        name="experts",
    )(arrived, w_in, w_out)


def combine_kernel(r_ref, b_ref, g_ref, o_ref):
    rows = r_ref.shape[0]
    terms = mm(g_ref[...], b_ref[...])
    mixture = terms[:rows] + terms[rows : 2 * rows] + terms[2 * rows :]
    o_ref[...] = (r_ref[...] + mixture).astype(bf16)


def combine_call(resid, back, gate_parts):
    return pl.pallas_call(
        combine_kernel,
        out_shape=jax.ShapeDtypeStruct(resid.shape, bf16),
        compiler_params=params(),
        cost_estimate=cost(6 * back.size * resid.shape[0], 6 * resid.size + 2 * back.size),
        name="combine",
    )(resid, back, gate_parts)


def swap(value, axis, bits):
    size = math.prod(lax.axis_size(name) for name in axis) if isinstance(axis, tuple) else lax.axis_size(axis)
    return lax.ppermute(value, axis, [(i, i ^ bits) for i in range(size)])


def per_device(tokens, routes, gates, qkv_weight, out_weight, w_in, w_out):
    rows, width = tokens.shape
    devices = lax.axis_size("ctx")
    groups = lax.axis_size("groups")
    lines_total = devices // SPAN
    me = lax.axis_index("ctx")
    member = me % SPAN
    line = me // SPAN
    group = lax.axis_index("groups")
    parts_ff = max(1, devices // EXPERTS)
    local_experts = max(1, EXPERTS // devices)

    mine = width // SPAN
    share = groups if (mine // HD) % groups == 0 else 1
    cols = mine // share
    offset = (group % share) * cols

    def columns(to):
        pieces = [
            lax.dynamic_slice_in_dim(qkv_weight, t * width + to * mine + offset, cols, 1)
            for t in range(3)
        ]
        pieces.append(lax.dynamic_slice_in_dim(out_weight, to * mine + offset, cols, 1))
        return jnp.concatenate(pieces, axis=1)

    pieces = [columns(member)] + [swap(columns(member ^ j), "ctx", j) for j in range(1, SPAN)]
    block = jnp.zeros((SPAN,) + pieces[0].shape, bf16)
    for j in range(SPAN):
        block = lax.dynamic_update_slice(block, pieces[j][None], (member ^ j, 0, 0))
    block = block.reshape(-1, 4 * cols)
    block, last = block[:, : 3 * cols], block[:, 3 * cols :]
    slots = route_call(routes, gates)
    normed, block, last, slots = lax.optimization_barrier((norm_call(tokens), block, last, slots))
    marks, gate_parts = slots
    bits = [1 << i for i in reversed(range(lines_total.bit_length() - 1))]
    lines = {0: block}
    for bit in bits:
        lines[bit] = swap(block, "ctx", bit * SPAN)
    others = {}
    for s in range(1, share):
        for m in range(min(2, lines_total)):
            others[s, m] = swap(block, ("groups", "ctx"), s * devices + m * SPAN)
    if share > 1 and len(bits) > 1:
        lines[bits[0]], others = lax.optimization_barrier((lines[bits[0]], others))
    for bit in bits[1:]:
        for known in [m for m in lines if m >= 2 * bit and m & (2 * bit - 1) == 0]:
            lines[known | bit] = swap(lines[known], "ctx", bit * SPAN)
    for s in range(1, share):
        for m in bits[:-1]:
            others[s, m] = swap(lines[m], "groups", s)
    if share > 1 and len(bits) > 1:
        lines[lines_total - 1], others = lax.optimization_barrier((lines[lines_total - 1], others))
    for s in range(1, share):
        for m in range(lines_total):
            if (s, m) not in others:
                others[s, m] = swap(lines[m], "groups", s)
    shares = [lines[m] for m in range(lines_total)]
    shares += [others[s, m] for s in range(1, share) for m in range(lines_total)]

    far = swap(normed, "ctx", 2)
    near = swap(normed, "ctx", 1)
    both = swap(far, "ctx", 1)

    for bit in reversed(bits):
        last = jnp.concatenate([last, swap(last, "ctx", bit * SPAN)], axis=0)
    part = part_call(line.reshape(1), last, lines_total)
    part = jnp.concatenate([part] + [swap(part, "groups", s) for s in range(1, share)], axis=1)
    part_far = swap(part, "ctx", 2)
    part_near = swap(part, "ctx", 1)

    place = jnp.stack([line, group % share])
    projected = project_call(place, [normed, near, far, both], shares, lines_total, share)
    ctxs = attend_call(projected, (0, 1, 2, 3), rows)
    own, part_far = lax.optimization_barrier((ctxs[0], part_far))
    part_both = swap(part_far, "ctx", 1)
    back = {0: own} | {j: swap(ctxs[j], "ctx", j) for j in range(1, SPAN)}
    ctxs = [back[j] for j in range(SPAN)]
    resid, table = output_call(
        jnp.stack([member, group % share]), tokens, marks, [part, part_near, part_far, part_both], ctxs, share
    )

    table = table.reshape(EXPERTS, CAP, width)
    if parts_ff > 1:
        table = jnp.repeat(table, parts_ff, axis=0)
    outgoing = table.reshape(devices, local_experts * CAP, width)
    arrived = lax.all_to_all(outgoing, "ctx", split_axis=0, concat_axis=0, tiled=True)
    produced = expert_call(arrived.reshape(-1, width), w_in, w_out, local_experts, devices)
    produced = produced.reshape(devices, local_experts * CAP, width)
    returned = lax.all_to_all(produced, "ctx", split_axis=0, concat_axis=0, tiled=True)
    if parts_ff > 1:
        grouped = returned.reshape(EXPERTS, parts_ff, CAP, width)
        returned = jnp.sum(grouped.astype(f32), axis=1).astype(bf16)
    return combine_call(resid, returned.reshape(EXPERTS * CAP, width), gate_parts)


def solution(mesh):
    in_specs = (
        P(("groups", "ctx"), None),
        P(("groups", "ctx"), None),
        P(("groups", "ctx"), None),
        P("ctx", None),
        P("ctx", None),
        P(None, "ctx"),
        P("ctx", None),
    )
    out_specs = P(("groups", "ctx"), None)
    return jax.shard_map(
        per_device, mesh=mesh, in_specs=in_specs, out_specs=out_specs, check_vma=False
    )
```

```python
import functools
import math

import jax
import jax.numpy as jnp
from jax import lax
from jax.experimental import pallas as pl
from jax.experimental.pallas import tpu as pltpu
from jax.sharding import PartitionSpec as P

HEADS = 16
HD = 64
EXPERTS = 32
SPAN = 4
CAP = 20
TOP = 2
MIB = 1 << 20

eps = 1e-06
bf16 = jnp.bfloat16
f32 = jnp.float32


def params(mib=12):
    return pltpu.CompilerParams(vmem_limit_bytes=mib * MIB)


def cost(flops, nbytes, trans=0):
    return pl.CostEstimate(flops=int(flops), bytes_accessed=int(nbytes), transcendentals=int(trans))


def mm(a, b, dims=(((1,), (0,)), ((), ()))):
    return lax.dot_general(a, b, dims, preferred_element_type=f32)


def normalize(values):
    center = values - jnp.mean(values, axis=-1, keepdims=True)
    spread = jnp.mean(center * center, axis=-1, keepdims=True)
    return (center * lax.rsqrt(spread + eps)).astype(bf16)


def norm_kernel(x_ref, o_ref):
    o_ref[...] = normalize(x_ref[...].astype(f32))


def norm_call(tokens):
    return pl.pallas_call(
        norm_kernel,
        out_shape=jax.ShapeDtypeStruct(tokens.shape, bf16),
        compiler_params=params(),
        cost_estimate=cost(8 * tokens.size, 4 * tokens.size),
        name="norm_tokens",
    )(tokens)


def route_kernel(routes_ref, gates_ref, d_ref, g_ref):
    rows = routes_ref.shape[1]
    slots = d_ref.shape[0]
    expert = lax.broadcasted_iota(jnp.int32, (EXPERTS, rows), 0)
    names = [expert == routes_ref[r : r + 1, :] for r in range(TOP)]
    counts = names[0]
    for other in names[1:]:
        counts = counts | other
    counts = jnp.where(counts, 1.0, 0.0).astype(bf16)
    earlier = lax.broadcasted_iota(jnp.int32, (rows, rows), 0) < lax.broadcasted_iota(
        jnp.int32, (rows, rows), 1
    )
    before = mm(counts, jnp.where(earlier, 1.0, 0.0).astype(bf16))
    place = lax.broadcasted_iota(jnp.int32, (slots, rows), 0)
    marks = jnp.zeros((slots, rows), f32)
    weights = jnp.zeros((slots, rows), f32)
    for r in range(TOP):
        position = jnp.sum(jnp.where(names[r], before, 0.0), axis=0, keepdims=True)
        slot = routes_ref[r : r + 1, :] * CAP + position.astype(jnp.int32)
        here = place == slot
        marks = jnp.where(here, 1.0, marks)
        weights = jnp.where(here, gates_ref[r : r + 1, :], weights)
    d_ref[...] = marks.astype(bf16)
    weights = weights.T
    high = weights.astype(bf16)
    rest = weights - high.astype(f32)
    middle = rest.astype(bf16)
    g_ref[:rows, :] = (rest - middle.astype(f32)).astype(bf16)
    g_ref[rows : 2 * rows, :] = middle
    g_ref[2 * rows :, :] = high


def route_call(routes, gates):
    rows = routes.shape[0]
    marks = jax.ShapeDtypeStruct((EXPERTS * CAP, rows), bf16)
    parts = jax.ShapeDtypeStruct((3 * rows, EXPERTS * CAP), bf16)
    return pl.pallas_call(
        route_kernel,
        out_shape=[marks, parts],
        compiler_params=params(),
        cost_estimate=cost(20 * EXPERTS * CAP * rows, 8 * EXPERTS * CAP * rows),
        name="route_slots",
    )(routes.T, gates.T)


def part_kernel(line_ref, w_ref, o_ref, *, lines):
    size = w_ref.shape[0] // lines
    for m in range(lines):
        start = pl.multiple_of((line_ref[0] ^ m) * size, size)
        o_ref[pl.ds(start, size), :] = w_ref[m * size : (m + 1) * size, :]


def part_call(line, blocks, lines):
    vm = pl.BlockSpec(memory_space=pltpu.VMEM)
    return pl.pallas_call(
        functools.partial(part_kernel, lines=lines),
        out_shape=jax.ShapeDtypeStruct(blocks.shape, bf16),
        in_specs=[pl.BlockSpec(memory_space=pltpu.SMEM), vm],
        out_specs=vm,
        compiler_params=params(4),
        cost_estimate=cost(1, 4 * blocks.size),
        name="out_weight_part",
    )(line, blocks)


def project_kernel(place_ref, *refs, count, lines, share):
    xs = refs[:count]
    ws = refs[count : count + lines * share]
    o_ref, x_ref, w_ref = refs[count + lines * share :]
    size, wide = ws[0].shape
    cols = wide // 3
    rows = xs[0].shape[0]
    mine = share * cols
    for s in range(share):
        for m in range(lines):
            start = pl.multiple_of((place_ref[0] ^ m) * size, size)
            w_ref[pl.ds(start, size), s * wide : (s + 1) * wide] = ws[s * lines + m][...]
    for j in range(count):
        x_ref[j * rows : (j + 1) * rows, :] = xs[j][...]
    got = mm(x_ref[...], w_ref[...]).astype(bf16)
    for t in range(3):
        for s in range(share):
            piece = got[:, s * wide + t * cols : s * wide + (t + 1) * cols]
            if cols % 128 == 0:
                start = pl.multiple_of(t * mine + (place_ref[1] ^ s) * cols, 128)
                o_ref[:, pl.ds(start, cols)] = piece
            else:
                for p in range(share):
                    at = slice(t * mine + p * cols, t * mine + (p + 1) * cols)
                    o_ref[:, at] = jnp.where((place_ref[1] ^ s) == p, piece, o_ref[:, at])


def project_call(place, xs, ws, lines, share):
    rows, width = xs[0].shape
    count = len(xs)
    cols = ws[0].shape[1] // 3
    vm = pl.BlockSpec(memory_space=pltpu.VMEM)
    return pl.pallas_call(
        functools.partial(project_kernel, count=count, lines=lines, share=share),
        out_shape=jax.ShapeDtypeStruct((count * rows, 3 * share * cols), bf16),
        in_specs=[pl.BlockSpec(memory_space=pltpu.SMEM)] + [vm] * (count + lines * share),
        out_specs=vm,
        scratch_shapes=[
            pltpu.VMEM((count * rows, width), bf16),
            pltpu.VMEM((width, share * 3 * cols), bf16),
        ],
        compiler_params=params(),
        cost_estimate=cost(6 * count * rows * width * cols * share, 2 * width * (count * rows + 8 * cols * share)),
        name="project",
    )(place, *xs, *ws)


def attend_kernel(p_ref, *o_refs, tile):
    cols = p_ref.shape[1] // 3
    rows = o_refs[0].shape[0]
    lane = lax.broadcasted_iota(jnp.int32, (tile * rows, cols), 1) // HD
    keys = p_ref[:, cols : 2 * cols]
    values = p_ref[:, 2 * cols :]
    for i in range(0, len(o_refs), tile):
        queries = p_ref[i * rows : (i + tile) * rows, :cols] * jnp.asarray(HD ** (-0.5), bf16)
        mixed = None
        for h in range(cols // HD):
            mine = lane == h
            q = jnp.where(mine, queries, jnp.zeros_like(queries))
            scores = mm(q, keys, (((1,), (1,)), ((), ())))
            weights = jnp.exp(scores - jnp.max(scores, axis=-1, keepdims=True))
            probs = (weights * (1.0 / jnp.sum(weights, axis=-1, keepdims=True))).astype(bf16)
            part = mm(probs, values)
            mixed = part if mixed is None else jnp.where(mine, part, mixed)
        mixed = mixed.astype(bf16)
        for k in range(tile):
            o_refs[i + k][...] = mixed[k * rows : (k + 1) * rows]


def attend_call(projected, blocks, rows):
    length, width = projected.shape[0], projected.shape[1] // 3
    return pl.pallas_call(
        functools.partial(attend_kernel, tile=1),
        out_shape=[jax.ShapeDtypeStruct((rows, width), bf16)] * len(blocks),
        compiler_params=params(),
        cost_estimate=cost(
            16 * len(blocks) * rows * length * width, 2 * projected.size, len(blocks) * rows * length * width // HD
        ),
        name="attend",
    )(projected)


def output_kernel(place_ref, t_ref, d_ref, *refs, share):
    ctxs, parts = refs[:SPAN], refs[SPAN : 2 * SPAN]
    r_ref, o_ref, c_ref, a_ref = refs[2 * SPAN :]
    wide = ctxs[0].shape[1]
    cols = wide // share
    starts = [pl.multiple_of((place_ref[0] ^ j) * wide, wide) for j in range(SPAN)]

    def natural(value):
        pieces = []
        for p in range(share):
            piece = value[:, :cols]
            for s in range(1, share):
                piece = jnp.where((place_ref[1] ^ s) == p, value[:, s * cols : (s + 1) * cols], piece)
            pieces.append(piece)
        return jnp.concatenate(pieces, axis=1) if share > 1 else value

    for j in range(SPAN):
        c_ref[:, pl.ds(starts[j], wide)] = ctxs[j][...]
    for j in range(SPAN):
        got = mm(c_ref[...], parts[j][...])
        if cols % 128:
            a_ref[:, pl.ds(starts[j], wide)] = natural(got)
            continue
        for s in range(share):
            start = pl.multiple_of(starts[j] + (place_ref[1] ^ s) * cols, 128)
            a_ref[:, pl.ds(start, cols)] = got[:, s * cols : (s + 1) * cols]
    total = t_ref[...].astype(f32) + a_ref[...]
    r_ref[...] = total
    o_ref[...] = mm(d_ref[...], normalize(total)).astype(bf16)


def output_call(place, tokens, marks, parts, ctxs, share):
    rows, width = tokens.shape
    vm = pl.BlockSpec(memory_space=pltpu.VMEM)
    return pl.pallas_call(
        functools.partial(output_kernel, share=share),
        out_shape=[
            jax.ShapeDtypeStruct((rows, width), f32),
            jax.ShapeDtypeStruct((marks.shape[0], width), bf16),
        ],
        in_specs=[pl.BlockSpec(memory_space=pltpu.SMEM)] + [vm] * (2 + 2 * SPAN),
        out_specs=[vm, vm],
        scratch_shapes=[pltpu.VMEM((rows, width), bf16), pltpu.VMEM((rows, width), f32)],
        compiler_params=params(),
        cost_estimate=cost(160 * rows * width * (width + marks.shape[0]), 6 * width * width),
        name="out_projection",
    )(place, tokens, marks, *ctxs, *parts)


def gelu(x):
    return jax.nn.gelu(x, approximate=True)


def expert_kernel(x_ref, win_ref, wout_ref, o_ref, *scratch, local, sources, step):
    rows_ref, hid_ref, pre_ref, term_ref, out_buf, sems = scratch
    count = sources * CAP
    hidden = win_ref.shape[1] // local
    steps = hidden // step
    pack = 4 * CAP

    def load(e, n):
        return pltpu.make_async_copy(
            wout_ref.at[pl.ds(e * hidden + n * step, step), :], out_buf.at[pl.ds(n * step, step), :], sems.at[n]
        )

    for n in range(steps):
        load(0, n).start()

    if local > 1:
        to = lax.broadcasted_iota(jnp.int32, (local * pack, local * pack), 0)
        have = lax.broadcasted_iota(jnp.int32, (local * pack, local * pack), 1)
        expert = to // pack
        inner = to - expert * pack
        source = inner // CAP
        wanted = source * (local * CAP) + expert * CAP + (inner - source * CAP)
        order = jnp.where(have == wanted, 1.0, 0.0).astype(bf16)
        for g in range(count // pack):
            part = mm(order, x_ref[g * local * pack : (g + 1) * local * pack, :]).astype(bf16)
            for e in range(local):
                rows_ref[e, g * pack : (g + 1) * pack, :] = part[e * pack : (e + 1) * pack, :]

    for e in range(local):
        for n in range(steps):
            start = e * hidden + n * step
            rows = rows_ref[e] if local > 1 else x_ref[...]
            pre_ref[n % 2] = mm(rows, win_ref[:, start : start + step])
            if n:
                hid_ref[:, (n - 1) * step : n * step] = gelu(pre_ref[(n - 1) % 2]).astype(bf16)
        hid_ref[:, (steps - 1) * step :] = gelu(pre_ref[(steps - 1) % 2]).astype(bf16)
        for n in range(steps):
            load(e, n).wait()
        term = mm(hid_ref[...], out_buf[...]).astype(bf16)
        if local > 1:
            term_ref[e] = term
        else:
            o_ref[...] = term
        if e + 1 < local:
            for n in range(steps):
                load(e + 1, n).start()

    if local > 1:
        for g in range(count // pack):
            part = jnp.concatenate([term_ref[e, g * pack : (g + 1) * pack, :] for e in range(local)], axis=0)
            back = mm(order, part, (((0,), (0,)), ((), ())))
            o_ref[g * local * pack : (g + 1) * local * pack, :] = back.astype(bf16)


def expert_call(arrived, w_in, w_out, local, sources, step=1024):
    count = sources * CAP
    width = arrived.shape[1]
    hidden = w_in.shape[1] // local
    kept = (local, count, width) if local > 1 else (1, 16, 128)
    w_in = pltpu.with_memory_space_constraint(w_in, pltpu.VMEM)
    vm = pl.BlockSpec(memory_space=pltpu.VMEM)
    return pl.pallas_call(
        functools.partial(expert_kernel, local=local, sources=sources, step=step),
        out_shape=jax.ShapeDtypeStruct(arrived.shape, bf16),
        in_specs=[vm, vm, pl.BlockSpec(memory_space=pl.ANY)],
        out_specs=vm,
        scratch_shapes=[
            pltpu.VMEM(kept, bf16),
            pltpu.VMEM((count, hidden), bf16),
            pltpu.VMEM((2, count, step), f32),
            pltpu.VMEM(kept, bf16),
            pltpu.VMEM((hidden, width), bf16),
            pltpu.SemaphoreType.DMA((hidden // step,)),
        ],
        compiler_params=params(26 if local > 1 else 40),
        cost_estimate=cost(4 * count * width * hidden * local, 4 * width * hidden * local, count * hidden * local),
        name="experts",
    )(arrived, w_in, w_out)


def combine_kernel(r_ref, b_ref, g_ref, o_ref):
    rows = r_ref.shape[0]
    terms = mm(g_ref[...], b_ref[...])
    mixture = terms[:rows] + terms[rows : 2 * rows] + terms[2 * rows :]
    o_ref[...] = (r_ref[...] + mixture).astype(bf16)


def combine_call(resid, back, gate_parts):
    return pl.pallas_call(
        combine_kernel,
        out_shape=jax.ShapeDtypeStruct(resid.shape, bf16),
        compiler_params=params(),
        cost_estimate=cost(6 * back.size * resid.shape[0], 6 * resid.size + 2 * back.size),
        name="combine",
    )(resid, back, gate_parts)


def swap(value, axis, bits):
    size = math.prod(lax.axis_size(name) for name in axis) if isinstance(axis, tuple) else lax.axis_size(axis)
    return lax.ppermute(value, axis, [(i, i ^ bits) for i in range(size)])


def per_device(tokens, routes, gates, qkv_weight, out_weight, w_in, w_out):
    rows, width = tokens.shape
    devices = lax.axis_size("ctx")
    groups = lax.axis_size("groups")
    lines_total = devices // SPAN
    me = lax.axis_index("ctx")
    member = me % SPAN
    line = me // SPAN
    group = lax.axis_index("groups")
    parts_ff = max(1, devices // EXPERTS)
    local_experts = max(1, EXPERTS // devices)

    mine = width // SPAN
    share = groups if (mine // HD) % groups == 0 else 1
    cols = mine // share
    offset = (group % share) * cols

    def columns(to):
        pieces = [
            lax.dynamic_slice_in_dim(qkv_weight, t * width + to * mine + offset, cols, 1)
            for t in range(3)
        ]
        pieces.append(lax.dynamic_slice_in_dim(out_weight, to * mine + offset, cols, 1))
        return jnp.concatenate(pieces, axis=1)

    pieces = [columns(member)] + [swap(columns(member ^ j), "ctx", j) for j in range(1, SPAN)]
    block = jnp.zeros((SPAN,) + pieces[0].shape, bf16)
    for j in range(SPAN):
        block = lax.dynamic_update_slice(block, pieces[j][None], (member ^ j, 0, 0))
    block = block.reshape(-1, 4 * cols)
    block, last = block[:, : 3 * cols], block[:, 3 * cols :]
    slots = route_call(routes, gates)
    normed, block, last, slots = lax.optimization_barrier((norm_call(tokens), block, last, slots))
    marks, gate_parts = slots
    bits = [1 << i for i in reversed(range(lines_total.bit_length() - 1))]
    lines = {0: block}
    for bit in bits:
        lines[bit] = swap(block, "ctx", bit * SPAN)
    others = {}
    for s in range(1, share):
        for m in range(min(2, lines_total)):
            others[s, m] = swap(block, ("groups", "ctx"), s * devices + m * SPAN)
    if share > 1 and len(bits) > 1:
        lines[bits[0]], others = lax.optimization_barrier((lines[bits[0]], others))
    for bit in bits[1:]:
        for known in [m for m in lines if m >= 2 * bit and m & (2 * bit - 1) == 0]:
            lines[known | bit] = swap(lines[known], "ctx", bit * SPAN)
    for s in range(1, share):
        for m in bits[:-1]:
            others[s, m] = swap(lines[m], "groups", s)
    if share > 1 and len(bits) > 1:
        lines[lines_total - 1], others = lax.optimization_barrier((lines[lines_total - 1], others))
    for s in range(1, share):
        for m in range(lines_total):
            if (s, m) not in others:
                others[s, m] = swap(lines[m], "groups", s)
    shares = [lines[m] for m in range(lines_total)]
    shares += [others[s, m] for s in range(1, share) for m in range(lines_total)]

    far = swap(normed, "ctx", 2)
    near = swap(normed, "ctx", 1)
    both = swap(far, "ctx", 1)

    for bit in reversed(bits):
        last = jnp.concatenate([last, swap(last, "ctx", bit * SPAN)], axis=0)
    part = part_call(line.reshape(1), last, lines_total)
    part = jnp.concatenate([part] + [swap(part, "groups", s) for s in range(1, share)], axis=1)
    part_far = swap(part, "ctx", 2)
    part_near = swap(part, "ctx", 1)

    place = jnp.stack([line, group % share])
    projected = project_call(place, [normed, near, far, both], shares, lines_total, share)
    ctxs = attend_call(projected, (0, 1, 2, 3), rows)
    own, part_far = lax.optimization_barrier((ctxs[0], part_far))
    part_both = swap(part_far, "ctx", 1)
    back = {0: own} | {j: swap(ctxs[j], "ctx", j) for j in range(1, SPAN)}
    ctxs = [back[j] for j in range(SPAN)]
    resid, table = output_call(
        jnp.stack([member, group % share]), tokens, marks, [part, part_near, part_far, part_both], ctxs, share
    )

    table = table.reshape(EXPERTS, CAP, width)
    if parts_ff > 1:
        table = jnp.repeat(table, parts_ff, axis=0)
    outgoing = table.reshape(devices, local_experts * CAP, width)
    arrived = lax.all_to_all(outgoing, "ctx", split_axis=0, concat_axis=0, tiled=True)
    produced = expert_call(arrived.reshape(-1, width), w_in, w_out, local_experts, devices)
    produced = produced.reshape(devices, local_experts * CAP, width)
    returned = lax.all_to_all(produced, "ctx", split_axis=0, concat_axis=0, tiled=True)
    if parts_ff > 1:
        grouped = returned.reshape(EXPERTS, parts_ff, CAP, width)
        returned = jnp.sum(grouped.astype(f32), axis=1).astype(bf16)
    return combine_call(resid, returned.reshape(EXPERTS * CAP, width), gate_parts)


def solution(mesh):
    in_specs = (
        P(("groups", "ctx"), None),
        P(("groups", "ctx"), None),
        P(("groups", "ctx"), None),
        P("ctx", None),
        P("ctx", None),
        P(None, "ctx"),
        P("ctx", None),
    )
    out_specs = P(("groups", "ctx"), None)
    return jax.shard_map(
        per_device, mesh=mesh, in_specs=in_specs, out_specs=out_specs, check_vma=False
    )
```
